512 devices in a mesh: grp: 8 (over z), dev: 64 (over y, x, core).
Axes of the slice: x: 4, y: 8, z: 8, core: 2. Of those that a mesh axis runs over, the one named last changes fastest.
Arguments:
- right_side: float32 [128, 2048, 128], P('grp', 'dev'), may hold values from -6 to 6
- coefficient: float32 [128, 2048, 128], P('grp', 'dev'), may hold values from 0.1 to 1
- solute: float32 [128, 2048, 128], P('grp', 'dev'), may hold values from 0.2 to 1.5
- diffusivity: float32 [128, 2048, 128], P('grp', 'dev'), may hold values from 0.05 to 0.5
- interface_flags: int32 [16, 256, 16], P('grp', 'dev'), may hold values 0 or 1
- coarse_inverse: float32 [512, 512], P(('grp', 'dev')), as said below
Outputs:
- pressure: float32 [128, 2048, 128], P('grp', 'dev')
- residual: float32 [128, 2048, 128], P('grp', 'dev')
- solute_image: float32 [128, 2048, 128], P('grp', 'dev')
The draws below stay inside these ranges and needn't reach their ends.
Inputs may be any that keep to these rules, and one draw needn't show every extreme that they name: `coarse_inverse`: symmetric and positive definite; entries off the diagonal are nonnegative.
All inputs are finite; a program needn't handle non-finite values. No bound on the sum of `interface_flags` on one device may be relied on, other than what follows from the above.
Results may differ from the reference program's by a relative error of at most 0.003.
Values sent between devices are 32-bit elements; how exact they have to be, the bound alone decides.
A program may use at most 64 MiB of HBM per device.

```python
import math
import jax
import jax.numpy as jnp
import numpy as np
from jax import lax

EX = 2
EY = 4
EZ = 16
ITERS = 2
NX = 128
NY = 2048
NZ = 128
NEX = 16
NEY = 256
NCOARSE = 512
N_GRP = 8
N_DEV = 64


def draw_coarse_inverse(key, part):
    key = jax.random.fold_in(key, 11)
    off_key, diag_key, back_key = jax.random.split(key, 3)
    uniform_raw = jax.random.uniform(off_key, (NCOARSE, NCOARSE), jnp.float32)
    symmetric = 0.5 * (uniform_raw + uniform_raw.T)
    back_raw = jax.random.uniform(back_key, (NCOARSE, NCOARSE), jnp.float32)
    back_sym = 0.5 * (back_raw + back_raw.T)
    level = 0.8 / math.sqrt(NCOARSE)
    index = jnp.arange(NCOARSE, dtype=jnp.int32)
    first_pos = index // N_DEV
    second_pos = index % N_DEV
    distance = jnp.abs(first_pos[:, None] - first_pos[None, :]) + jnp.abs(second_pos[:, None] - second_pos[None, :])
    identity = jnp.eye(NCOARSE, dtype=jnp.float32)
    partner_hit = index[:, None] == (index[None, :] + NCOARSE // 2) % NCOARSE
    partner = jnp.where(partner_hit, 1.0, 0.0).astype(jnp.float32) * (1.0 - identity)
    adjacent = jnp.where(distance == 1, 1.0, 0.0).astype(jnp.float32) * (1.0 - partner)
    edges = 0.15 + 0.1 * symmetric
    far_edges = 0.5 + 0.1 * symmetric
    background = level * 2.0 * back_sym
    diagonal = jax.random.uniform(diag_key, (NCOARSE,), jnp.float32, 3.6, 4.0)
    return edges * adjacent + far_edges * partner + background * (1.0 - identity) + identity * diagonal[None, :]


def plant(values, own_key, low, high):
    place = [jax.random.randint(jax.random.fold_in(own_key, axis), (), 0, length) for axis, length in enumerate(values.shape)]
    widest = values.shape.index(max(values.shape))
    neighbour = place[:widest] + [(place[widest] + 1) % values.shape[widest]] + place[widest + 1:]
    return values.at[tuple(place)].set(low).at[tuple(neighbour)].set(high)


def shard_levels(rng, shape, pieces, low, high):
    gain = 1.0
    for position, blocks in pieces:
        heights = jax.random.uniform(jax.random.fold_in(jax.random.fold_in(rng, 6), position), (blocks,), jnp.float32, low / len(pieces), high / len(pieces))
        gain = gain * jnp.repeat(jnp.exp(heights), shape[position] // blocks).reshape((-1,) + (1,) * (len(shape) - 1 - position))
    return gain


def bell_draw(key, dims, scale, bound, cuts=(), held_as=jnp.bfloat16):
    gain = shard_levels(key, dims, cuts, -0.22, 0.18) if cuts else 1.0
    values = jax.random.normal(key, dims, jnp.float32) * scale * gain
    return jnp.minimum(jnp.maximum(values, -bound), bound).astype(held_as)


def setup_inputs(seed: int = 0) -> dict:
    key_list = jax.random.split(jax.random.key(seed), 7)
    right_side = bell_draw(key_list[0], (NX, NY, NZ), 1.0, 6.0, ((0, 8), (1, 64)), jnp.float32)
    coefficient = jnp.clip(jnp.exp(math.log(1.0) - 2.3025851 * jax.random.uniform(key_list[1], (NX, NY, NZ), jnp.float32) ** shard_levels(key_list[1], (NX, NY, NZ), ((0, 8), (1, 64)), -0.2, 0.2)), 0.1, 1.0)
    solute = jnp.clip(0.2 + 1.3 * jax.random.uniform(key_list[2], (NX, NY, NZ), jnp.float32) ** shard_levels(key_list[2], (NX, NY, NZ), ((0, 8), (1, 64)), -0.2, 0.2), 0.2, 1.5)
    diffusivity = jnp.clip(jnp.exp(math.log(0.5) - 2.3025851 * jax.random.uniform(key_list[3], (NX, NY, NZ), jnp.float32) ** shard_levels(key_list[3], (NX, NY, NZ), ((0, 8), (1, 64)), -0.2, 0.2)), 0.05, 0.5)
    interface_flags = plant((jax.random.randint(key_list[4], (NEX, NEY, EZ), 0, 4) < 1).astype(jnp.int32), jax.random.fold_in(key_list[4], 1), 0, 1)
    coarse_inverse = draw_coarse_inverse(jax.random.fold_in(key_list[6], 71), 0)
    return {"right_side": right_side, "coefficient": coefficient, "solute": solute, "diffusivity": diffusivity, "interface_flags": interface_flags, "coarse_inverse": coarse_inverse}


HIGHEST = lax.Precision.HIGHEST
GLL_POINTS = [-1.0, -0.8717401485096066, -0.5917001814331423, -0.2092992179024789, 0.2092992179024789, 0.5917001814331423, 0.8717401485096066, 1.0]
GLL_WEIGHTS = [0.0357142857142857, 0.2107042271435061, 0.3411226924835044, 0.4124587946587038, 0.4124587946587038, 0.3411226924835044, 0.2107042271435061, 0.0357142857142857]
SHIFT_MASS = 0.5
MASS_RATE = 2.0
GROWTH = 40.0
SEGREGATION = 0.7

def derivative_table():
    products = []
    for row_at in range(8):
        value = 1.0
        for other in range(8):
            if other != row_at:
                value = value * (GLL_POINTS[row_at] - GLL_POINTS[other])
        products.append(value)
    table = [[0.0] * 8 for row_at in range(8)]
    for row_at in range(8):
        total = 0.0
        for other in range(8):
            if other != row_at:
                entry = products[row_at] / products[other] / (GLL_POINTS[row_at] - GLL_POINTS[other])
                table[row_at][other] = entry
                total = total + entry
        table[row_at][row_at] = -total
    return np.array(table)

def margin_matrices():
    deriv_np = derivative_table()
    spacing = GLL_POINTS[1] - GLL_POINTS[0]
    stiffness = [[0.0] * 10 for row_at in range(10)]
    masses = [0.0] * 10
    for row_at in range(8):
        masses[row_at + 1] = GLL_WEIGHTS[row_at]
        for other in range(8):
            total = 0.0
            for point in range(8):
                total = total + deriv_np[point, row_at] * GLL_WEIGHTS[point] * deriv_np[point, other]
            stiffness[row_at + 1][other + 1] = total
    for outer_end, inner_end in ((0, 1), (9, 8)):
        stiffness[outer_end][outer_end] += 1.0 / spacing
        stiffness[inner_end][inner_end] += 1.0 / spacing
        stiffness[outer_end][inner_end] -= 1.0 / spacing
        stiffness[inner_end][outer_end] -= 1.0 / spacing
        masses[outer_end] += 0.5 * spacing
        masses[inner_end] += 0.5 * spacing
    return (stiffness, masses)

def jacobi_eigen(matrix_rows):
    count_in = len(matrix_rows)
    work = [list(row_now) for row_now in matrix_rows]
    vectors = [[1.0 if other == row_at else 0.0 for other in range(count_in)] for row_at in range(count_in)]
    for sweep in range(15):
        for first in range(count_in):
            for second in range(first + 1, count_in):
                entry = work[first][second]
                if entry != 0.0:
                    theta = (work[second][second] - work[first][first]) / (2.0 * entry)
                    sign_now = 1.0 if theta >= 0.0 else -1.0
                    tangent = sign_now / (abs(theta) + math.sqrt(theta * theta + 1.0))
                    cosine = 1.0 / math.sqrt(tangent * tangent + 1.0)
                    sine = tangent * cosine
                    for index in range(count_in):
                        left_val = work[index][first]
                        right_val = work[index][second]
                        work[index][first] = cosine * left_val - sine * right_val
                        work[index][second] = sine * left_val + cosine * right_val
                    for index in range(count_in):
                        left_val = work[first][index]
                        right_val = work[second][index]
                        work[first][index] = cosine * left_val - sine * right_val
                        work[second][index] = sine * left_val + cosine * right_val
                    for index in range(count_in):
                        left_val = vectors[index][first]
                        right_val = vectors[index][second]
                        vectors[index][first] = cosine * left_val - sine * right_val
                        vectors[index][second] = sine * left_val + cosine * right_val
    return ([work[index][index] for index in range(10 if count_in == 10 else count_in)], vectors)

def fdm_tables():
    stiffness, masses = margin_matrices()
    scaled = [[stiffness[row_at][other] / math.sqrt(masses[row_at] * masses[other]) for other in range(10)] for row_at in range(10)]
    values, vectors = jacobi_eigen(scaled)
    basis = np.array([[vectors[row_at][other] / math.sqrt(masses[row_at]) for other in range(10)] for row_at in range(10)])
    return (basis, np.array(values))

def z_forward_table(elements):
    basis, values = fdm_tables()
    extend_np = np.zeros((8 * elements, 10 * elements))
    for element in range(elements):
        for slot_in in range(10):
            source = 8 * element + slot_in - 1
            if slot_in == 0:
                source = 8 * element - 2
            if slot_in == 9:
                source = 8 * element + 9
            if 0 <= source < 8 * elements:
                extend_np[source, 10 * element + slot_in] = 1.0
    return extend_np @ np.kron(np.eye(elements), basis)

def z_backward_table(elements):
    basis, values = fdm_tables()
    return np.kron(np.eye(elements), basis[1:9].T)

def eigen_sums(count_x, count_y, count_z):
    basis, values = fdm_tables()
    first_vec = jnp.asarray(np.tile(values, count_x), jnp.float32)
    second_vec = jnp.asarray(np.tile(values, count_y), jnp.float32)
    third_vec = jnp.asarray(np.tile(values, count_z), jnp.float32)
    return first_vec[:, None, None] + second_vec[None, :, None] + third_vec[None, None, :] + SHIFT_MASS

def z_derivative(elements):
    return np.kron(np.eye(elements), derivative_table().T)

def z_pairs(elements):
    pairs_np = np.eye(8 * elements)
    for element in range(elements - 1):
        pairs_np[8 * element + 7, 8 * element + 8] = 1.0
        pairs_np[8 * element + 8, 8 * element + 7] = 1.0
    return pairs_np

def axis_factors(start_at, count_in, total_len):
    positions = start_at + jnp.arange(count_in, dtype=jnp.int32)
    inside = (positions > 0) & (positions < total_len - 1)
    remainder = positions % 8
    shared = ((remainder == 0) | (remainder == 7)) & inside
    keep_part = jnp.where(inside, 1.0, 0.0).astype(jnp.float32)
    share_part = jnp.where(shared, 0.5, 1.0).astype(jnp.float32)
    return (keep_part, share_part)

def outer_three(first_vec, second_vec, third_vec):
    return first_vec[:, None, None] * second_vec[None, :, None] * third_vec[None, None, :]

def tiled_weights(count_in):
    return jnp.asarray(np.tile(np.array(GLL_WEIGHTS), count_in // 8), jnp.float32)

def pair_sum(inner_part, low_plane, high_plane, along_dim):
    length_along = inner_part.shape[along_dim]
    number = length_along // 8
    firsts = lax.slice_in_dim(inner_part, 0, length_along, 8, along_dim)
    last_planes = lax.slice_in_dim(inner_part, 7, length_along, 8, along_dim)
    next_first = jnp.concatenate([lax.slice_in_dim(firsts, 1, number, 1, along_dim), high_plane], along_dim)
    prev_last = jnp.concatenate([low_plane, lax.slice_in_dim(last_planes, 0, number - 1, 1, along_dim)], along_dim)
    split_shape = inner_part.shape[:along_dim] + (number, 8) + inner_part.shape[along_dim + 1:]
    single_shape = inner_part.shape[:along_dim] + (number, 1) + inner_part.shape[along_dim + 1:]
    middle = lax.slice_in_dim(inner_part.reshape(split_shape), 1, 7, 1, along_dim + 1)
    joined = jnp.concatenate([(firsts + prev_last).reshape(single_shape), middle, (last_planes + next_first).reshape(single_shape)], along_dim + 1)
    return joined.reshape(inner_part.shape)

def stiffness_apply(values_in, coeff_in, derivative, z_forward, z_backward, weight_cube):
    size_x, size_y, size_z = values_in.shape
    block_shape = (size_x // 8, 8, size_y // 8, 8, size_z)
    blocks = values_in.reshape(block_shape)
    grad_x = jnp.einsum('pi,aibjz->apbjz', derivative, blocks, precision=HIGHEST).reshape(values_in.shape)
    grad_y = jnp.einsum('qj,aibjz->aibqz', derivative, blocks, precision=HIGHEST).reshape(values_in.shape)
    grad_z = jnp.dot(values_in, z_forward, precision=HIGHEST)
    scaled = coeff_in * weight_cube
    back_x = jnp.einsum('pi,apbjz->aibjz', derivative, (scaled * grad_x).reshape(block_shape), precision=HIGHEST)
    back_y = jnp.einsum('qj,aibqz->aibjz', derivative, (scaled * grad_y).reshape(block_shape), precision=HIGHEST)
    back_z = jnp.dot(scaled * grad_z, z_backward, precision=HIGHEST)
    return back_x.reshape(values_in.shape) + back_y.reshape(values_in.shape) + back_z

def element_apply(values_in, along_dim, table_rows):
    width = table_rows.shape[1]
    number = values_in.shape[along_dim] // width
    split_shape = values_in.shape[:along_dim] + (number, width) + values_in.shape[along_dim + 1:]
    blocks = values_in.reshape(split_shape)
    if along_dim == 0:
        solved = jnp.einsum('pi,aiyz->apyz', table_rows, blocks, precision=HIGHEST)
    else:
        solved = jnp.einsum('pi,xaiz->xapz', table_rows, blocks, precision=HIGHEST)
    final_shape = values_in.shape[:along_dim] + (table_rows.shape[0] * number,) + values_in.shape[along_dim + 1:]
    return solved.reshape(final_shape)

def extend_solve(padded, along_dim, table_rows):
    length_pad = padded.shape[along_dim]
    number = (length_pad - 4) // 8
    split_shape = padded.shape[:along_dim] + (number, 8) + padded.shape[along_dim + 1:]
    single_shape = padded.shape[:along_dim] + (number, 1) + padded.shape[along_dim + 1:]
    inner_part = lax.slice_in_dim(padded, 2, length_pad - 2, 1, along_dim).reshape(split_shape)
    low_plane = lax.slice_in_dim(padded, 0, 8 * number, 8, along_dim).reshape(single_shape)
    high_plane = lax.slice_in_dim(padded, 11, length_pad, 8, along_dim).reshape(single_shape)
    extended = jnp.concatenate([low_plane, inner_part, high_plane], along_dim + 1)
    final_shape = padded.shape[:along_dim] + (10 * number,) + padded.shape[along_dim + 1:]
    return element_apply(extended.reshape(final_shape), along_dim, table_rows)

def schwarz_apply(padded, z_fore, z_back, forward_rows, back_rows):
    along_z = jnp.dot(padded, z_fore, precision=HIGHEST)
    into_x = extend_solve(along_z, 0, forward_rows)
    into_y = extend_solve(into_x, 1, forward_rows)
    denom = eigen_sums(into_y.shape[0] // 10, into_y.shape[1] // 10, into_y.shape[2] // 10)
    divided = into_y / denom
    back_x = element_apply(divided, 0, back_rows)
    back_y = element_apply(back_x, 1, back_rows)
    return jnp.dot(back_y, z_back, precision=HIGHEST)

def assemble(values_in, z_sum):
    plane_x = jnp.zeros_like(values_in[0:1])
    along_x = pair_sum(values_in, plane_x, plane_x, 0)
    plane_y = jnp.zeros_like(along_x[:, 0:1])
    along_y = pair_sum(along_x, plane_y, plane_y, 1)
    return jnp.dot(along_y, z_sum, precision=HIGHEST)

def reference(right_side, coefficient, solute, diffusivity, interface_flags, coarse_inverse):
    size_x, size_y, size_z = right_side.shape
    elements_z = size_z // 8
    derivative = jnp.asarray(derivative_table(), jnp.float32)
    z_forward = jnp.asarray(z_derivative(elements_z), jnp.float32)
    z_backward = jnp.asarray(z_derivative(elements_z).T, jnp.float32)
    z_sum = jnp.asarray(z_pairs(elements_z), jnp.float32)
    z_fore = jnp.asarray(z_forward_table(elements_z), jnp.float32)
    z_back = jnp.asarray(z_backward_table(elements_z), jnp.float32)
    basis, values = fdm_tables()
    forward_rows = jnp.asarray(basis.T, jnp.float32)
    back_rows = jnp.asarray(basis[1:9], jnp.float32)
    weight_x = tiled_weights(size_x)
    weight_y = tiled_weights(size_y)
    weight_z = tiled_weights(size_z)
    weight_cube = outer_three(weight_x, weight_y, weight_z)
    keep_x, share_x = axis_factors(0, size_x, size_x)
    keep_y, share_y = axis_factors(0, size_y, size_y)
    keep_z, share_z = axis_factors(0, size_z, size_z)
    dirichlet_mask = outer_three(keep_x, keep_y, keep_z)
    inv_mult = outer_three(share_x, share_y, share_z)
    block_x = 8 * EX
    block_y = 8 * EY
    q_scale = 1.0 / math.sqrt(512 * EX * EY * EZ)

    def coarse_field(residual_now):
        sums = (residual_now * inv_mult).reshape(N_GRP, block_x, N_DEV, block_y, size_z).sum(axis=(1, 3, 4)) * q_scale
        coarse_now = jnp.dot(coarse_inverse, sums.reshape(-1), precision=HIGHEST).reshape(N_GRP, N_DEV)
        spread = jnp.repeat(jnp.repeat(coarse_now, block_x, axis=0), block_y, axis=1)
        return spread[:, :, None]

    def precondition(residual_now):
        padded = jnp.pad(residual_now, ((2, 2), (2, 2), (0, 0)))
        solved = schwarz_apply(padded, z_fore, z_back, forward_rows, back_rows)
        return assemble(solved + coarse_field(residual_now), z_sum) * inv_mult * dirichlet_mask

    def inner_product(first_field, second_field):
        return jnp.sum(first_field * second_field * inv_mult)
    start_vec = assemble(right_side, z_sum) * dirichlet_mask
    pressure = jnp.zeros_like(right_side)
    residual = start_vec
    precond_now = precondition(residual)
    energy_now = inner_product(residual, precond_now)
    direction = precond_now
    for step_index in range(ITERS):
        applied = assemble(stiffness_apply(direction, coefficient, derivative, z_forward, z_backward, weight_cube), z_sum) * dirichlet_mask
        step_length = energy_now / inner_product(direction, applied)
        pressure = pressure + step_length * direction
        residual = residual - step_length * applied
        if step_index + 1 < ITERS:
            precond_now = precondition(residual)
            energy_next = inner_product(residual, precond_now)
            direction = precond_now + energy_next / energy_now * direction
            energy_now = energy_next
    flag_points = jnp.repeat(jnp.repeat(jnp.repeat(interface_flags, 8, axis=0), 8, axis=1), 8, axis=2).astype(jnp.float32)
    bottom = jnp.where(jnp.arange(size_z, dtype=jnp.int32) % 8 == 0, 1.0, 0.0).astype(jnp.float32)
    face_weight = outer_three(weight_x, weight_y, bottom)
    flux = GROWTH * SEGREGATION * flag_points * face_weight * solute
    local_image = stiffness_apply(solute, diffusivity, derivative, z_forward, z_backward, weight_cube) + MASS_RATE * weight_cube * solute + flux
    solute_image = assemble(local_image, z_sum)
    return (pressure, residual, solute_image)
```

```python
import functools
import math

import jax
import jax.numpy as jnp
import ml_dtypes
import numpy as np
from jax import lax
from jax.experimental import pallas as pl
from jax.experimental.pallas import tpu as pltpu
from jax.sharding import PartitionSpec as P

GLL_POINTS = [
    -1.0,
    -0.8717401485096066,
    -0.5917001814331423,
    -0.2092992179024789,
    0.2092992179024789,
    0.5917001814331423,
    0.8717401485096066,
    1.0,
]
GLL_WEIGHTS = [
    0.0357142857142857,
    0.2107042271435061,
    0.3411226924835044,
    0.4124587946587038,
    0.4124587946587038,
    0.3411226924835044,
    0.2107042271435061,
    0.0357142857142857,
]
SHIFT_MASS = 0.5
MASS_RATE = 2.0
GROWTH = 40.0
SEGREGATION = 0.7


def derivative_table():
    products = []
    for row_at in range(8):
        value = 1.0
        for other in range(8):
            if other != row_at:
                value = value * (GLL_POINTS[row_at] - GLL_POINTS[other])
        products.append(value)
    table = [[0.0] * 8 for row_at in range(8)]
    for row_at in range(8):
        total = 0.0
        for other in range(8):
            if other != row_at:
                entry = (
                    products[row_at] / products[other] / (GLL_POINTS[row_at] - GLL_POINTS[other])
                )
                table[row_at][other] = entry
                total = total + entry
        table[row_at][row_at] = -total
    return np.array(table)


def margin_matrices():
    deriv_np = derivative_table()
    spacing = GLL_POINTS[1] - GLL_POINTS[0]
    stiffness = [[0.0] * 10 for row_at in range(10)]
    masses = [0.0] * 10
    for row_at in range(8):
        masses[row_at + 1] = GLL_WEIGHTS[row_at]
        for other in range(8):
            total = 0.0
            for point in range(8):
                total = (
                    total + deriv_np[point, row_at] * GLL_WEIGHTS[point] * deriv_np[point, other]
                )
            stiffness[row_at + 1][other + 1] = total
    for outer_end, inner_end in ((0, 1), (9, 8)):
        stiffness[outer_end][outer_end] += 1.0 / spacing
        stiffness[inner_end][inner_end] += 1.0 / spacing
        stiffness[outer_end][inner_end] -= 1.0 / spacing
        stiffness[inner_end][outer_end] -= 1.0 / spacing
        masses[outer_end] += 0.5 * spacing
        masses[inner_end] += 0.5 * spacing
    return (stiffness, masses)


def jacobi_eigen(matrix_rows):
    count_in = len(matrix_rows)
    work = [list(row_now) for row_now in matrix_rows]
    vectors = [
        [1.0 if other == row_at else 0.0 for other in range(count_in)] for row_at in range(count_in)
    ]
    for sweep in range(15):
        for first in range(count_in):
            for second in range(first + 1, count_in):
                entry = work[first][second]
                if entry != 0.0:
                    theta = (work[second][second] - work[first][first]) / (2.0 * entry)
                    sign_now = 1.0 if theta >= 0.0 else -1.0
                    tangent = sign_now / (abs(theta) + math.sqrt(theta * theta + 1.0))
                    cosine = 1.0 / math.sqrt(tangent * tangent + 1.0)
                    sine = tangent * cosine
                    for index in range(count_in):
                        left_val = work[index][first]
                        right_val = work[index][second]
                        work[index][first] = cosine * left_val - sine * right_val
                        work[index][second] = sine * left_val + cosine * right_val
                    for index in range(count_in):
                        left_val = work[first][index]
                        right_val = work[second][index]
                        work[first][index] = cosine * left_val - sine * right_val
                        work[second][index] = sine * left_val + cosine * right_val
                    for index in range(count_in):
                        left_val = vectors[index][first]
                        right_val = vectors[index][second]
                        vectors[index][first] = cosine * left_val - sine * right_val
                        vectors[index][second] = sine * left_val + cosine * right_val
    return ([work[index][index] for index in range(10 if count_in == 10 else count_in)], vectors)


def fdm_tables():
    stiffness, masses = margin_matrices()
    scaled = [
        [
            stiffness[row_at][other] / math.sqrt(masses[row_at] * masses[other])
            for other in range(10)
        ]
        for row_at in range(10)
    ]
    values, vectors = jacobi_eigen(scaled)
    basis = np.array(
        [
            [vectors[row_at][other] / math.sqrt(masses[row_at]) for other in range(10)]
            for row_at in range(10)
        ]
    )
    return (basis, np.array(values))


def z_forward_table(elements):
    basis, values = fdm_tables()
    extend_np = np.zeros((8 * elements, 10 * elements))
    for element in range(elements):
        for slot_in in range(10):
            source = 8 * element + slot_in - 1
            if slot_in == 0:
                source = 8 * element - 2
            if slot_in == 9:
                source = 8 * element + 9
            if 0 <= source < 8 * elements:
                extend_np[source, 10 * element + slot_in] = 1.0
    return extend_np @ np.kron(np.eye(elements), basis)


def z_backward_table(elements):
    basis, values = fdm_tables()
    return np.kron(np.eye(elements), basis[1:9].T)


def z_derivative(elements):
    return np.kron(np.eye(elements), derivative_table().T)


def z_pairs(elements):
    pairs_np = np.eye(8 * elements)
    for element in range(elements - 1):
        pairs_np[8 * element + 7, 8 * element + 8] = 1.0
        pairs_np[8 * element + 8, 8 * element + 7] = 1.0
    return pairs_np


LOCAL_X, LOCAL_Y, LOCAL_Z = (16, 32, 128)
ROWS = LOCAL_X * LOCAL_Y
DIRS = ((-1, 0), (1, 0), (0, -1), (0, 1), (-1, -1), (-1, 1), (1, -1), (1, 1))
F32 = jnp.float32
BF16 = jnp.bfloat16
MESH_ID = pl.DeviceIdType.MESH


def split_np(table):
    high = np.asarray(table, np.float32).astype(ml_dtypes.bfloat16)
    low = (np.asarray(table, np.float64) - high.astype(np.float64)).astype(ml_dtypes.bfloat16)
    return (high, low)


def left_table(matrix, rows):
    high, low = split_np(matrix)
    joined = np.concatenate([high, high, low], axis=1)
    out = np.zeros((rows, 128), ml_dtypes.bfloat16)
    out[: joined.shape[0], : joined.shape[1]] = joined
    return out


def y_pairs():
    pairs = np.eye(LOCAL_Y)
    for element in range(LOCAL_Y // 8 - 1):
        pairs[8 * element + 7, 8 * element + 8] = 1.0
        pairs[8 * element + 8, 8 * element + 7] = 1.0
    return pairs


def inner_share(count_in):
    share = np.ones(count_in)
    for position in range(count_in):
        if position % 8 in (0, 7) and position not in (0, count_in - 1):
            share[position] = 0.5
    return share


def padded_to(matrix, rows, columns):
    out = np.zeros((rows, columns))
    out[: matrix.shape[0], : matrix.shape[1]] = matrix
    return out


def make_tables():
    basis, values = fdm_tables()
    deriv = derivative_table()
    ends = np.ones(LOCAL_Z)
    ends[0] = 0.0
    ends[-1] = 0.0
    pairs_z = z_pairs(LOCAL_Z // 8)
    fore = pairs_z @ np.diag(ends) @ z_forward_table(LOCAL_Z // 8)
    back = z_backward_table(LOCAL_Z // 8) @ pairs_z @ np.diag(ends * inner_share(LOCAL_Z))
    fore_hi, fore_lo = split_np(padded_to(fore, 128, 256))
    back_hi, back_lo = split_np(padded_to(back, 256, 128))
    zf1 = np.concatenate([fore_hi, fore_hi], axis=0)
    zb1 = np.concatenate([back_hi, back_lo], axis=1)

    def square(matrix):
        high, low = split_np(matrix)
        return np.concatenate([np.concatenate([high, low], axis=1)] * 2, axis=0)

    deriv_z = np.kron(np.eye(LOCAL_Z // 8), deriv.T)
    deriv_y = np.kron(np.eye(LOCAL_Y // 8), deriv)
    count_y = LOCAL_Y // 8
    extend = np.zeros((10 * count_y, 40))
    for element in range(count_y):
        for slot in range(10):
            source = 8 * element + slot - 1
            if slot == 0:
                source = 8 * element - 2 if element else 32
            if slot == 9:
                source = 8 * element + 9 if element + 1 < count_y else 33
            extend[10 * element + slot, source] = 1.0
    y_fore = np.kron(np.eye(count_y), basis.T) @ extend
    y_back = np.diag(inner_share(LOCAL_Y)) @ y_pairs() @ np.kron(np.eye(count_y), basis[1:9])
    sums = (
        values[:, None, None]
        + np.tile(values, count_y)[None, :, None]
        + np.tile(values, LOCAL_Z // 8)[None, None, :]
        + SHIFT_MASS
    )
    recip = np.zeros((10 * 40, 256), np.float32)
    recip[:, :160] = (1.0 / sums).reshape(400, 160)
    weights = np.array(GLL_WEIGHTS)
    wyz = np.tile(weights, count_y)[:, None] * np.tile(weights, LOCAL_Z // 8)[None, :]
    spread = np.zeros((LOCAL_Z // 8, LOCAL_Z), ml_dtypes.bfloat16)
    for element in range(LOCAL_Z // 8):
        spread[element, 8 * element] = 1.0
    return dict(
        yf=left_table(y_fore, 48),
        yb=left_table(y_back, 32),
        yd=left_table(deriv_y, 32),
        ydt=left_table(deriv_y.T, 32),
        zf1=zf1,
        zf2=fore_lo,
        zb1=zb1,
        zd=square(deriv_z),
        zdt=square(deriv_z.T),
        wyz=wyz.astype(np.float32),
        spread=spread,
        recip=recip,
    )


TABLE_NAMES = ("yf", "yb", "yd", "ydt", "zf1", "zf2", "zb1", "zd", "zdt", "wyz", "spread", "recip")


def parity_signs(basis):
    signs = []
    for mode in range(10):
        even = np.abs(basis[:, mode] - basis[::-1, mode]).max()
        odd = np.abs(basis[:, mode] + basis[::-1, mode]).max()
        signs.append(1 if even < odd else -1)
    return signs


def weighted(coefficients, terms):
    total = None
    for coefficient, term in zip(coefficients, terms):
        piece = term * float(coefficient)
        total = piece if total is None else total + piece
    return total


def x_derive(values, matrix):
    sums = [values[i] + values[7 - i] for i in range(4)]
    gaps = [values[i] - values[7 - i] for i in range(4)]
    out = [None] * 8
    for p in range(4):
        first = weighted([(matrix[p, i] + matrix[p, 7 - i]) / 2 for i in range(4)], sums)
        second = weighted([(matrix[p, i] - matrix[p, 7 - i]) / 2 for i in range(4)], gaps)
        out[p] = second + first
        out[7 - p] = second - first
    return out


def x_modes(values, basis, signs):
    sums = [values[i] + values[9 - i] for i in range(5)]
    gaps = [values[i] - values[9 - i] for i in range(5)]
    return [
        weighted([basis[i, mode] for i in range(5)], sums if signs[mode] > 0 else gaps)
        for mode in range(10)
    ]


def x_unmodes(values, basis, signs):
    evens = [mode for mode in range(10) if signs[mode] > 0]
    odds = [mode for mode in range(10) if signs[mode] < 0]
    out = [None] * 8
    for i in range(1, 5):
        first = weighted([basis[i, mode] for mode in evens], [values[mode] for mode in evens])
        second = weighted([basis[i, mode] for mode in odds], [values[mode] for mode in odds])
        out[i - 1] = first + second
        out[8 - i] = first - second
    return out


def dot(first, second):
    return jnp.dot(first, second, preferred_element_type=F32)


def halves(values):
    high = values.astype(BF16)
    return (high, (values - high.astype(F32)).astype(BF16))


def left_mul(table, first, second):
    values = jnp.concatenate([first, second], axis=1)
    high = values.astype(BF16).astype(F32)
    rows = values.shape[0]
    parts = [high, values - high, high]
    if 3 * rows < 128:
        parts.append(jnp.zeros((128 - 3 * rows, values.shape[1]), F32))
    return dot(table, jnp.concatenate(parts, axis=0).astype(BF16))


def right_mul(values, table):
    high, low = halves(values)
    out = dot(jnp.concatenate([high, low], axis=1), table)
    return out[:, :128] + out[:, 128:]


def fold_rows(values):
    return jnp.sum(values.reshape(values.shape[0] // 8, 8, 128), axis=0)


def all_sum(values):
    lanes = jnp.sum(jnp.sum(values, axis=0, keepdims=True), axis=1, keepdims=True)
    return jnp.broadcast_to(lanes, (8, 128))


def times_tile(values, tile):
    return (values.reshape(values.shape[0] // 8, 8, 128) * tile[None]).reshape(values.shape)


def message_rows(direction, layers, extra):
    sx, sy = direction
    rows = 8 * layers if sx and sy else 32 * layers if sx else 16 * layers
    return rows + (8 if extra else 0)


def message_offsets(layers, extra):
    offsets = [0]
    for direction in DIRS:
        offsets.append(offsets[-1] + message_rows(direction, layers, extra))
    return offsets


ROUNDS = (("rhs", 2, True), ("sol", 1, False), ("sch0", 1, False), ("sti0", 2, False), ("sch1", 1, False), ("sti1", 1, False))


def body(sizes, *refs):
    n_grp, n_low, n_high = sizes
    n_dev = n_low * n_high
    (rhs_h, coef_h, sol_h, dif_h, flags_h, crow_h) = refs[:6]
    refs = refs[6:]
    tab_h = refs[: len(TABLE_NAMES)]
    refs = refs[len(TABLE_NAMES) :]
    out_p, out_r, out_s = refs[:3]
    refs = refs[3:]
    names = ("rhs", "kc", "kd", "sol", "solraw", "pin", "y1", "u", "v", "x2")
    names += ("s", "z0", "b", "p0", "w", "z1", "r1", "a1", "ct")
    buf = dict(zip(names, refs))
    refs = refs[len(names) :]
    send_bufs = dict(zip([r[0] for r in ROUNDS], refs[:6]))
    recv_bufs = dict(zip([r[0] for r in ROUNDS], refs[6:12]))
    g_send, g_recv, halo_send_sem, halo_recv_sem, g_send_sem, g_recv_sem, load_sem = refs[12:19]
    flags_ref, crow_ref = refs[19:21]
    tab = dict(zip(TABLE_NAMES, refs[21:]))

    grp = lax.axis_index("grp")
    dev = lax.axis_index("dev")
    low = lax.rem(dev, n_low)
    high = lax.div(dev, n_low)
    x_lo = jnp.where(grp > 0, 1.0, 0.0).astype(F32)
    x_hi = jnp.where(grp < n_grp - 1, 1.0, 0.0).astype(F32)
    y_lo = jnp.where(dev > 0, 1.0, 0.0).astype(F32)
    y_hi = jnp.where(dev < n_dev - 1, 1.0, 0.0).astype(F32)

    def neighbour(direction):
        return (
            lax.rem(grp + direction[0] + n_grp, n_grp),
            lax.rem(dev + direction[1] + n_dev, n_dev),
        )

    def stage_partner(stage, step):
        if stage == 0:
            return (grp, high * n_low + lax.rem(low + step, n_low))
        if stage == 1:
            return (grp, lax.rem(high + step, n_high) * n_low + low)
        return (lax.rem(grp + step, n_grp), dev)

    stage_sizes = (n_low, n_high, n_grp)

    loads = {}
    wanted = [("sol", sol_h, buf["sol"]), ("kd", dif_h, buf["kd"]), ("flags", flags_h, flags_ref)]
    wanted += [(name, source, tab[name]) for name, source in zip(TABLE_NAMES, tab_h)]
    wanted += [("rhs", rhs_h, buf["rhs"]), ("crow", crow_h, crow_ref), ("kc", coef_h, buf["kc"])]
    for at, (name, source, target) in enumerate(wanted):
        loads[name] = pltpu.make_async_copy(source, target, load_sem.at[3 + at])
        loads[name].start()

    barrier = pltpu.get_barrier_semaphore()
    greetings = 0
    for direction in DIRS:
        pl.semaphore_signal(barrier, inc=1, device_id=neighbour(direction), device_id_type=MESH_ID)
        greetings += 1
    for stage in range(3):
        for step in range(1, stage_sizes[stage]):
            pl.semaphore_signal(
                barrier, inc=1, device_id=stage_partner(stage, step), device_id_type=MESH_ID
            )
            greetings += 1

    row32 = lax.broadcasted_iota(jnp.int32, (32, 128), 0)
    lane32 = lax.broadcasted_iota(jnp.int32, (32, 128), 1)
    keep_z = jnp.where((lane32 > 0) & (lane32 < 127), 1.0, 0.0).astype(F32)
    share_z = jnp.where(((lane32 % 8 == 0) | (lane32 % 8 == 7)) & (lane32 > 0) & (lane32 < 127), 0.5, 1.0).astype(F32)
    lane_up = jnp.where((lane32 % 8 == 7) & (lane32 < 127), 1.0, 0.0).astype(F32)
    lane_down = jnp.where((lane32 % 8 == 0) & (lane32 > 0), 1.0, 0.0).astype(F32)
    row_up = jnp.where((row32 % 8 == 7) & (row32 < 31), 1.0, 0.0).astype(F32)
    row_down = jnp.where((row32 % 8 == 0) & (row32 > 0), 1.0, 0.0).astype(F32)
    edge_y = jnp.where(row32 == 0, y_lo, jnp.where(row32 == 31, y_hi, 1.0)).astype(F32)
    inner_y = jnp.where((row32 % 8 == 0) | (row32 % 8 == 7), 0.5, 1.0).astype(F32)
    face_y = jnp.where((row32 == 0) | (row32 == 31), 0.5, 1.0).astype(F32) * edge_y
    share_y = inner_y * edge_y
    tile_row = lax.broadcasted_iota(jnp.int32, (8, 128), 0)
    tile_lane = lax.broadcasted_iota(jnp.int32, (8, 128), 1)
    tile_index = tile_row * 128 + tile_lane

    def share_x(plane):
        if plane == 0:
            return 0.5 * x_lo
        if plane == 15:
            return 0.5 * x_hi
        return 0.5 if plane in (7, 8) else 1.0

    def x_times(values, factor):
        return values if isinstance(factor, float) and factor == 1.0 else values * factor

    def z_assembled(values):
        return (
            values
            + lane_up * pltpu.roll(values, 127, 1)
            + lane_down * pltpu.roll(values, 1, 1)
        )

    def y_assembled(values):
        return (
            values + row_up * pltpu.roll(values, 31, 0) + row_down * pltpu.roll(values, 1, 0)
        )

    halo_copies = {}

    def exchange(name, src, tile=None):
        at_round = [r[0] for r in ROUNDS].index(name)
        layers, extra = ROUNDS[at_round][1:]
        offsets = message_offsets(layers, extra)
        send, recv = send_bufs[name], recv_bufs[name]
        copies = []
        for at, direction in enumerate(DIRS):
            sx, sy = direction
            base = offsets[at]
            rows = message_rows(direction, layers, False)
            if sx and sy:
                for layer in range(layers):
                    plane = layer if sx < 0 else 16 - layers + layer
                    start = 32 * plane + (0 if sy < 0 else 24)
                    send[base + 8 * layer : base + 8 * layer + 8, :] = src[start : start + 8, :]
            elif sx:
                start = 0 if sx < 0 else 32 * (16 - layers)
                send[base : base + rows, :] = src[start : start + rows, :]
            else:
                for layer in range(layers):
                    row = layer if sy < 0 else 32 - layers + layer
                    send[base + 16 * layer : base + 16 * layer + 16, :] = src[
                        pl.ds(row, 16, stride=32), :
                    ]
            if extra:
                send[base + rows : base + rows + 8, :] = tile
            total = message_rows(direction, layers, extra)
            copy = pltpu.make_async_remote_copy(
                src_ref=send.at[pl.ds(base, total)],
                dst_ref=recv.at[pl.ds(base, total)],
                send_sem=halo_send_sem.at[8 * at_round + at],
                recv_sem=halo_recv_sem.at[8 * at_round + at],
                device_id=neighbour(direction),
                device_id_type=MESH_ID,
            )
            copy.start()
            copies.append(copy)
        halo_copies[name] = copies

    def arrived(name):
        for copy in halo_copies[name]:
            copy.wait_recv()

    def part(name, direction, layer=0):
        at_round = [r[0] for r in ROUNDS].index(name)
        layers, extra = ROUNDS[at_round][1:]
        offsets = message_offsets(layers, extra)
        at = DIRS.index((-direction[0], -direction[1]))
        unit = 8 if direction[0] and direction[1] else 32 if direction[0] else 16
        start = offsets[at] + unit * layer
        return recv_bufs[name][start : start + unit, :]

    def part_row(name, direction, layer, last):
        at_round = [r[0] for r in ROUNDS].index(name)
        layers, extra = ROUNDS[at_round][1:]
        at = DIRS.index((-direction[0], -direction[1]))
        start = message_offsets(layers, extra)[at] + 8 * layer + last
        return recv_bufs[name][start : start + 1, :]

    def add_faces(name, ref, masked):
        def scale(values, first, second):
            if not masked:
                return values
            return values * (first * second if first is not None and second is not None else second if first is None else first)

        ref[0:32, :] += scale(part(name, (-1, 0)), x_lo, None)
        ref[480:512, :] += scale(part(name, (1, 0)), x_hi, None)
        ref[pl.ds(0, 16, stride=32), :] += scale(part(name, (0, -1)), y_lo, None)
        ref[pl.ds(31, 16, stride=32), :] += scale(part(name, (0, 1)), y_hi, None)
        ref[0:1, :] += scale(part_row(name, (-1, -1), 0, 7), x_lo, y_lo)
        ref[31:32, :] += scale(part_row(name, (-1, 1), 0, 0), x_lo, y_hi)
        ref[480:481, :] += scale(part_row(name, (1, -1), 0, 7), x_hi, y_lo)
        ref[511:512, :] += scale(part_row(name, (1, 1), 0, 0), x_hi, y_hi)

    g_copies = []
    g_pending = {}

    def g_start(which, stage, tile):
        slot = 3 * which + stage
        g_send[8 * slot : 8 * slot + 8, :] = tile
        copies = []
        for step in range(1, stage_sizes[stage]):
            at = 7 * slot + step - 1
            copy = pltpu.make_async_remote_copy(
                src_ref=g_send.at[pl.ds(8 * slot, 8)],
                dst_ref=g_recv.at[pl.ds(8 * at, 8)],
                send_sem=g_send_sem.at[at],
                recv_sem=g_recv_sem.at[at],
                device_id=stage_partner(stage, step),
                device_id_type=MESH_ID,
            )
            copy.start()
            copies.append(copy)
        g_copies.extend(copies)
        g_pending[slot] = (tile, copies)

    def g_finish(which, stage):
        slot = 3 * which + stage
        tile, copies = g_pending[slot]
        for copy in copies:
            copy.wait_recv()
        for step in range(1, stage_sizes[stage]):
            at = 7 * slot + step - 1
            tile = tile + g_recv[8 * at : 8 * at + 8, :]
        return tile

    def g_forward(which, stage):
        g_start(which, stage + 1, g_finish(which, stage))

    def scalar_spot(at):
        return jnp.where(tile_index == 4 * 128 + at, 1.0, 0.0).astype(F32)

    def read_scalar(tile, at):
        return all_sum(tile * scalar_spot(at))

    def coarse_tile(ref):
        middle = None
        for plane in range(16):
            piece = x_times(ref[32 * plane : 32 * plane + 32, :], share_x(plane))
            middle = piece if middle is None else middle + piece
        tile = jnp.zeros((8, 128), F32)
        rows = {
            -1: ref[0:32, :] * (0.5 * x_lo),
            0: middle,
            1: ref[480:512, :] * (0.5 * x_hi),
        }
        for dx in (-1, 0, 1):
            field = rows[dx] * keep_z
            own = fold_rows(field * share_y)
            before = field[0:8] * jnp.where(tile_row == 0, 0.5 * y_lo, 0.0)
            after = field[24:32] * jnp.where(tile_row == 7, 0.5 * y_hi, 0.0)
            for dy, values in ((-1, before), (0, own), (1, after)):
                spot = lax.rem(grp + dx + n_grp, n_grp) * n_dev + lax.rem(dev + dy + n_dev, n_dev)
                tile = tile + jnp.where(tile_index == spot, all_sum(values), 0.0)
        return tile

    q_scale = 1.0 / math.sqrt(LOCAL_X * LOCAL_Y * LOCAL_Z)

    def coarse_patterns(tile):
        values = {}
        for dx in (-1, 0, 1):
            for dy in (-1, 0, 1):
                if dx == 0 and dy == 0:
                    row = buf["ct"][...]
                else:
                    direction = (dx, dy)
                    layers, extra = ROUNDS[0][1:]
                    at = DIRS.index((-dx, -dy))
                    start = message_offsets(layers, extra)[at] + message_rows((dx, dy), layers, False)
                    row = recv_bufs["rhs"][start : start + 8, :]
                values[dx, dy] = all_sum(row * tile) * q_scale
        lines = {}
        for dx in (-1, 0, 1):
            centre = jnp.concatenate([values[dx, 0]] * 4, axis=0)
            first = jnp.concatenate([values[dx, -1]] * 4, axis=0)
            last = jnp.concatenate([values[dx, 1]] * 4, axis=0)
            line = jnp.where(row32 == 0, (centre + first) * (0.5 * y_lo), centre)
            line = jnp.where(row32 == 31, (centre + last) * (0.5 * y_hi), line)
            lines[dx] = line * keep_z
        return (
            (lines[0] + lines[-1]) * (0.5 * x_lo),
            lines[0],
            (lines[0] + lines[1]) * (0.5 * x_hi),
        )

    def build_pin(name, src):
        pin = buf["pin"]
        zero8 = jnp.zeros((8, 128), F32)
        for plane in range(18):
            pin[40 * plane + 32 : 40 * plane + 40, :] = zero8
        for plane in range(16):
            pin[40 * (plane + 1) : 40 * (plane + 1) + 32, :] = src[32 * plane : 32 * plane + 32, :]
        pin[40:72, :] += part(name, (-1, 0), 1)
        pin[640:672, :] += part(name, (1, 0), 0)
        pin[pl.ds(40, 16, stride=40), :] += part(name, (0, -1), 1)
        pin[pl.ds(71, 16, stride=40), :] += part(name, (0, 1), 0)
        pin[pl.ds(72, 16, stride=40), :] = part(name, (0, -1), 0)
        pin[pl.ds(73, 16, stride=40), :] = part(name, (0, 1), 1)
        for at_plane, dx, layer in ((1, -1, 1), (16, 1, 0), (0, -1, 0), (17, 1, 1)):
            base = 40 * at_plane
            if at_plane in (0, 17):
                pin[base : base + 32, :] = part(name, (dx, 0), layer)
            pin[base : base + 1, :] += part_row(name, (dx, -1), layer, 7)
            pin[base + 31 : base + 32, :] += part_row(name, (dx, 1), layer, 0)
            pin[base + 32 : base + 33, :] += part_row(name, (dx, -1), layer, 6)
            pin[base + 33 : base + 34, :] += part_row(name, (dx, 1), layer, 1)

    row40 = lax.broadcasted_iota(jnp.int32, (40, 128), 0)
    edge40 = jnp.where(
        (row40 == 0) | (row40 == 32), y_lo, jnp.where((row40 == 31) | (row40 == 33), y_hi, 1.0)
    ).astype(F32)

    def pin_plane(plane):
        values = buf["pin"][40 * plane : 40 * plane + 40, :] * edge40
        if plane < 2:
            values = values * x_lo
        if plane > 15:
            values = values * x_hi
        return values

    def assembled_own(plane):
        return z_assembled(pin_plane(plane + 1)[0:32]) * keep_z

    basis, _ = fdm_tables()
    signs = parity_signs(basis)
    deriv = derivative_table()
    sources = ([0, 1, 2, 3, 4, 5, 6, 7, 8, 10], [7, 9, 10, 11, 12, 13, 14, 15, 16, 17])

    def schwarz(dst, hooks):
        y1, u, v, x2 = buf["y1"], buf["u"], buf["v"], buf["x2"]
        yf, yb = tab["yf"][...], tab["yb"][...]
        for pair in range(9):
            out = left_mul(yf, pin_plane(2 * pair), pin_plane(2 * pair + 1))
            y1[80 * pair : 80 * pair + 40, :] = out[0:40, :128]
            y1[80 * pair + 40 : 80 * pair + 80, :] = out[0:40, 128:]
        hooks[0]()
        for element in range(2):
            for tile in range(5):
                values = [y1[40 * p + 8 * tile : 40 * p + 8 * tile + 8, :] for p in sources[element]]
                for mode, piece in enumerate(x_modes(values, basis, signs)):
                    start = 40 * (10 * element + mode) + 8 * tile
                    u[start : start + 8, :] = piece
        for element in range(2):
            block = u[400 * element : 400 * element + 400, :]
            first, second = halves(block)
            modes = dot(jnp.concatenate([first, second], axis=1), tab["zf1"][...])
            modes = (modes + dot(first, tab["zf2"][...])) * tab["recip"][...]
            first, second = halves(modes)
            back = dot(first, tab["zb1"][...])
            v[400 * element : 400 * element + 400, :] = (
                back[:, :128] + back[:, 128:] + dot(second, tab["zb1"][:, 0:128])
            )
            hooks[1 + element]()
        for tile in range(5):
            outs = []
            for element in range(2):
                starts = [40 * (10 * element + mode) + 8 * tile for mode in range(10)]
                outs += x_unmodes([v[s : s + 8, :] for s in starts], basis, signs)
            shared = (outs[7] + outs[8]) * 0.5
            outs[7] = shared
            outs[8] = shared
            outs[0] = outs[0] * (0.5 * x_lo)
            outs[15] = outs[15] * (0.5 * x_hi)
            for plane in range(16):
                x2[40 * plane + 8 * tile : 40 * plane + 8 * tile + 8, :] = outs[plane]
        for pair in range(8):
            out = left_mul(yb, x2[80 * pair : 80 * pair + 40, :], x2[80 * pair + 40 : 80 * pair + 80, :])
            dst[64 * pair : 64 * pair + 32, :] = out[:, :128] * face_y
            dst[64 * pair + 32 : 64 * pair + 64, :] = out[:, 128:] * face_y

    def stiff(src, coef, dst, extra=None):
        energy = jnp.zeros((8, 128), F32)
        for chunk in range(2):
            at = slice(256 * chunk, 256 * chunk + 256)
            grad = right_mul(src[at, :], tab["zd"][...])
            flow = grad * coef[at, :]
            energy = energy + fold_rows(grad * flow)
            dst[at, :] = right_mul(flow, tab["zdt"][...])
        for pair in range(8):
            one = slice(64 * pair, 64 * pair + 32)
            two = slice(64 * pair + 32, 64 * pair + 64)
            grad = left_mul(tab["yd"][...], src[one, :], src[two, :])
            flow_one = grad[:, :128] * coef[one, :]
            flow_two = grad[:, 128:] * coef[two, :]
            energy = energy + fold_rows(grad[:, :128] * flow_one) + fold_rows(grad[:, 128:] * flow_two)
            back = left_mul(tab["ydt"][...], flow_one, flow_two)
            dst[one, :] += back[:, :128]
            dst[two, :] += back[:, 128:]
        for tile in range(4):
            sums = []
            for element in range(2):
                starts = [32 * (8 * element + i) + 8 * tile for i in range(8)]
                grads = x_derive([src[s : s + 8, :] for s in starts], deriv)
                flows = [grad * coef[s : s + 8, :] for grad, s in zip(grads, starts)]
                for grad, flow in zip(grads, flows):
                    energy = energy + grad * flow
                backs = x_derive(flows, deriv.T)
                for s, back in zip(starts, backs):
                    value = dst[s : s + 8, :] + back
                    if extra is not None:
                        value = value + extra[s : s + 8, :]
                    sums.append(value)
            shared = sums[7] + sums[8]
            sums[7] = shared
            sums[8] = shared
            for plane in range(16):
                dst[32 * plane + 8 * tile : 32 * plane + 8 * tile + 8, :] = sums[plane]
        for plane in range(16):
            at = slice(32 * plane, 32 * plane + 32)
            dst[at, :] = y_assembled(dst[at, :])
        return energy

    weights = GLL_WEIGHTS + GLL_WEIGHTS

    for name in ("sol", "kd", "flags", "wyz", "spread", "zd", "zdt", "yd", "ydt"):
        loads[name].wait()
    wyz = tab["wyz"][...]
    flags = jnp.concatenate([flags_ref[0], flags_ref[1]], axis=0).astype(F32).astype(BF16)
    flag_rows = dot(flags, tab["spread"][...])
    weight_column = GLL_WEIGHTS
    row8 = tile_row
    w_rows = jnp.zeros((8, 128), F32)
    for at, weight in enumerate(weight_column):
        w_rows = jnp.where(row8 == at, weight, w_rows)
    for plane in range(16):
        at = slice(32 * plane, 32 * plane + 32)
        buf["kd"][at, :] = buf["kd"][at, :] * (wyz * weights[plane])
        flux = jnp.concatenate(
            [
                flag_rows[4 * (plane // 8) + ey : 4 * (plane // 8) + ey + 1, :] * w_rows
                for ey in range(4)
            ],
            axis=0,
        )
        factor = wyz * (MASS_RATE * weights[plane]) + flux * (GROWTH * SEGREGATION * weights[plane])
        buf["x2"][at, :] = buf["sol"][at, :] * factor
    stiff(buf["sol"], buf["kd"], buf["solraw"], extra=buf["x2"])

    loads["rhs"].wait()
    loads["crow"].wait()
    for plane in range(16):
        at = slice(32 * plane, 32 * plane + 32)
        values = buf["rhs"][at, :]
        if plane == 7:
            values = values + buf["rhs"][256:288, :]
        if plane == 8:
            values = values + buf["rhs"][224:256, :]
        buf["s"][at, :] = y_assembled(values)
    ct = buf["ct"]
    ct[...] = jnp.zeros((8, 128), F32)
    count = n_grp * n_dev
    for chunk in range((count + 127) // 128):
        width = min(128, count - 128 * chunk)
        ct[chunk : chunk + 1, 0:width] = crow_ref[:, 128 * chunk : 128 * chunk + width]
    first_tile = coarse_tile(buf["s"])

    pl.semaphore_wait(barrier, greetings)
    exchange("rhs", buf["s"], ct[...])
    g_start(0, 0, first_tile)
    exchange("sol", buf["solraw"])
    for name in ("kc", "yf", "yb", "zf1", "zf2", "zb1", "recip"):
        loads[name].wait()
    for plane in range(16):
        at = slice(32 * plane, 32 * plane + 32)
        buf["kc"][at, :] = buf["kc"][at, :] * (wyz * weights[plane])

    def nothing():
        pass

    arrived("rhs")
    build_pin("rhs", buf["s"])
    g_forward(0, 0)
    schwarz(buf["z0"], (nothing, lambda: g_forward(0, 1), nothing))
    exchange("sch0", buf["z0"])
    for plane in range(16):
        buf["b"][32 * plane : 32 * plane + 32, :] = assembled_own(plane)
    total = g_finish(0, 2)
    patterns = coarse_patterns(total)

    def finish_precond(name, ref, patterns):
        arrived(name)
        add_faces(name, ref, False)
        for plane in range(16):
            at = slice(32 * plane, 32 * plane + 32)
            ref[at, :] += patterns[0 if plane == 0 else 2 if plane == 15 else 1]

    finish_precond("sch0", buf["z0"], patterns)
    share_yz = share_y * share_z

    def energy_of(first, second):
        tile = jnp.zeros((8, 128), F32)
        for plane in range(16):
            at = slice(32 * plane, 32 * plane + 32)
            piece = x_times(first[at, :] * second[at, :] * share_yz, share_x(plane))
            tile = tile + fold_rows(piece)
        return all_sum(tile)

    curve = all_sum(stiff(buf["z0"], buf["kc"], buf["a1"]))
    exchange("sti0", buf["a1"])
    rz = energy_of(buf["b"], buf["z0"])
    tile = coarse_tile(buf["a1"])
    tile = tile + scalar_spot(0) * rz + scalar_spot(1) * curve
    g_start(1, 0, tile)

    arrived("sol")
    add_faces("sol", buf["solraw"], True)
    for plane in range(16):
        at = slice(32 * plane, 32 * plane + 32)
        buf["solraw"][at, :] = z_assembled(buf["solraw"][at, :])
    store_s = pltpu.make_async_copy(buf["solraw"], out_s, load_sem.at[0])
    store_s.start()

    arrived("sti0")
    build_pin("sti0", buf["a1"])
    g_forward(1, 0)
    schwarz(buf["w"], (nothing, lambda: g_forward(1, 1), nothing))
    exchange("sch1", buf["w"])
    for plane in range(16):
        buf["p0"][32 * plane : 32 * plane + 32, :] = assembled_own(plane)
    total = g_finish(1, 2)
    patterns = coarse_patterns(total)
    rz0 = read_scalar(total, 0)
    curve0 = read_scalar(total, 1)
    alpha0 = rz0 / curve0
    for plane in range(16):
        at = slice(32 * plane, 32 * plane + 32)
        buf["r1"][at, :] = buf["b"][at, :] - times_tile(buf["p0"][at, :], alpha0)
    finish_precond("sch1", buf["w"], patterns)
    for plane in range(16):
        at = slice(32 * plane, 32 * plane + 32)
        buf["z1"][at, :] = buf["z0"][at, :] - times_tile(buf["w"][at, :], alpha0)
    curve = all_sum(stiff(buf["z1"], buf["kc"], buf["rhs"]))
    exchange("sti1", buf["rhs"])
    rz = energy_of(buf["r1"], buf["z1"])
    cross = energy_of(buf["p0"], buf["z1"])
    g_start(2, 0, scalar_spot(0) * rz + scalar_spot(1) * curve + scalar_spot(2) * cross)
    g_forward(2, 0)
    g_forward(2, 1)
    arrived("sti1")
    add_faces("sti1", buf["rhs"], False)
    for plane in range(16):
        at = slice(32 * plane, 32 * plane + 32)
        values = z_assembled(buf["rhs"][at, :]) * keep_z * edge_y
        if plane == 0:
            values = values * x_lo
        if plane == 15:
            values = values * x_hi
        buf["rhs"][at, :] = values
    total = g_finish(2, 2)
    rz1 = read_scalar(total, 0)
    curve1 = read_scalar(total, 1)
    cross1 = read_scalar(total, 2)
    beta = rz1 / rz0
    full = curve1 + 2.0 * beta * cross1 + beta * beta * curve0
    alpha1 = rz1 / full
    alpha_old = alpha0 + alpha1 * beta
    step_old = alpha1 * beta
    for plane in range(16):
        at = slice(32 * plane, 32 * plane + 32)
        buf["w"][at, :] = times_tile(buf["z0"][at, :], alpha_old) + times_tile(buf["z1"][at, :], alpha1)
        buf["r1"][at, :] = (
            buf["r1"][at, :]
            - times_tile(buf["rhs"][at, :], alpha1)
            - times_tile(buf["p0"][at, :], step_old)
        )
    store_p = pltpu.make_async_copy(buf["w"], out_p, load_sem.at[1])
    store_p.start()
    store_r = pltpu.make_async_copy(buf["r1"], out_r, load_sem.at[2])
    store_r.start()
    for name in halo_copies:
        for copy in halo_copies[name]:
            copy.wait_send()
    for copy in g_copies:
        copy.wait_send()
    store_s.wait()
    store_p.wait()
    store_r.wait()


def run_kernel(sizes, fields, flags, coarse_row, tables):
    constants = [jnp.asarray(tables[name]) for name in TABLE_NAMES]
    far = pl.BlockSpec(memory_space=pltpu.HBM)
    field = pltpu.VMEM((ROWS, LOCAL_Z), F32)

    def rows(count):
        return pltpu.VMEM((count, LOCAL_Z), F32)

    halo = [rows(message_offsets(layers, extra)[-1]) for _, layers, extra in ROUNDS]
    scratch = (
        [field] * 5
        + [rows(720), rows(720), rows(800), rows(800), rows(640)]
        + [field] * 8
        + [rows(8)]
        + halo
        + halo
        + [rows(72), rows(8 * 63)]
        + [pltpu.SemaphoreType.DMA((count,)) for count in (48, 48, 63, 63, 9 + len(constants))]
        + [pltpu.VMEM(flags.shape, jnp.int32), pltpu.VMEM(coarse_row.shape, F32)]
        + [pltpu.VMEM(table.shape, table.dtype) for table in constants]
    )
    return pl.pallas_call(
        functools.partial(body, sizes),
        out_shape=[jax.ShapeDtypeStruct((ROWS, LOCAL_Z), F32)] * 3,
        in_specs=[far] * (6 + len(constants)),
        out_specs=[far] * 3,
        scratch_shapes=scratch,
        compiler_params=pltpu.CompilerParams(
            collective_id=0, has_side_effects=True, vmem_limit_bytes=63 * 1024 * 1024
        ),
    )(*fields, flags, coarse_row, *constants)


def solution(mesh):
    n_grp, n_dev = (mesh.shape["grp"], mesh.shape["dev"])
    n_low = 8 if n_dev % 8 == 0 else 2
    sizes = (n_grp, n_low, n_dev // n_low)
    tables = make_tables()

    def shards(right_side, coefficient, solute, diffusivity, interface_flags, coarse_inverse):
        fields = [v.reshape(ROWS, LOCAL_Z) for v in (right_side, coefficient, solute, diffusivity)]
        outs = run_kernel(sizes, fields, interface_flags, coarse_inverse, tables)
        return tuple(v.reshape(LOCAL_X, LOCAL_Y, LOCAL_Z) for v in outs)

    placed = (
        P("grp", "dev", None),
        P("grp", "dev", None),
        P("grp", "dev", None),
        P("grp", "dev", None),
        P("grp", "dev", None),
        P(("grp", "dev"), None),
    )
    return jax.shard_map(
        shards,
        mesh=mesh,
        in_specs=placed,
        out_specs=(P("grp", "dev", None), P("grp", "dev", None), P("grp", "dev", None)),
        check_vma=False,
    )
```

```python
import functools
import math

import jax
import jax.numpy as jnp
import ml_dtypes
import numpy as np
from jax import lax
from jax.experimental import pallas as pl
from jax.experimental.pallas import tpu as pltpu
from jax.sharding import PartitionSpec as P

GLL_POINTS = [
    -1.0,
    -0.8717401485096066,
    -0.5917001814331423,
    -0.2092992179024789,
    0.2092992179024789,
    0.5917001814331423,
    0.8717401485096066,
    1.0,
]
GLL_WEIGHTS = [
    0.0357142857142857,
    0.2107042271435061,
    0.3411226924835044,
    0.4124587946587038,
    0.4124587946587038,
    0.3411226924835044,
    0.2107042271435061,
    0.0357142857142857,
]
SHIFT_MASS = 0.5
MASS_RATE = 2.0
GROWTH = 40.0
SEGREGATION = 0.7


def derivative_table():
    products = []
    for row_at in range(8):
        value = 1.0
        for other in range(8):
            if other != row_at:
                value = value * (GLL_POINTS[row_at] - GLL_POINTS[other])
        products.append(value)
    table = [[0.0] * 8 for row_at in range(8)]
    for row_at in range(8):
        total = 0.0
        for other in range(8):
            if other != row_at:
                entry = (
                    products[row_at] / products[other] / (GLL_POINTS[row_at] - GLL_POINTS[other])
                )
                table[row_at][other] = entry
                total = total + entry
        table[row_at][row_at] = -total
    return np.array(table)


def margin_matrices():
    deriv_np = derivative_table()
    spacing = GLL_POINTS[1] - GLL_POINTS[0]
    stiffness = [[0.0] * 10 for row_at in range(10)]
    masses = [0.0] * 10
    for row_at in range(8):
        masses[row_at + 1] = GLL_WEIGHTS[row_at]
        for other in range(8):
            total = 0.0
            for point in range(8):
                total = (
                    total + deriv_np[point, row_at] * GLL_WEIGHTS[point] * deriv_np[point, other]
                )
            stiffness[row_at + 1][other + 1] = total
    for outer_end, inner_end in ((0, 1), (9, 8)):
        stiffness[outer_end][outer_end] += 1.0 / spacing
        stiffness[inner_end][inner_end] += 1.0 / spacing
        stiffness[outer_end][inner_end] -= 1.0 / spacing
        stiffness[inner_end][outer_end] -= 1.0 / spacing
        masses[outer_end] += 0.5 * spacing
        masses[inner_end] += 0.5 * spacing
    return (stiffness, masses)


def jacobi_eigen(matrix_rows):
    count_in = len(matrix_rows)
    work = [list(row_now) for row_now in matrix_rows]
    vectors = [
        [1.0 if other == row_at else 0.0 for other in range(count_in)] for row_at in range(count_in)
    ]
    for sweep in range(15):
        for first in range(count_in):
            for second in range(first + 1, count_in):
                entry = work[first][second]
                if entry != 0.0:
                    theta = (work[second][second] - work[first][first]) / (2.0 * entry)
                    sign_now = 1.0 if theta >= 0.0 else -1.0
                    tangent = sign_now / (abs(theta) + math.sqrt(theta * theta + 1.0))
                    cosine = 1.0 / math.sqrt(tangent * tangent + 1.0)
                    sine = tangent * cosine
                    for index in range(count_in):
                        left_val = work[index][first]
                        right_val = work[index][second]
                        work[index][first] = cosine * left_val - sine * right_val
                        work[index][second] = sine * left_val + cosine * right_val
                    for index in range(count_in):
                        left_val = work[first][index]
                        right_val = work[second][index]
                        work[first][index] = cosine * left_val - sine * right_val
                        work[second][index] = sine * left_val + cosine * right_val
                    for index in range(count_in):
                        left_val = vectors[index][first]
                        right_val = vectors[index][second]
                        vectors[index][first] = cosine * left_val - sine * right_val
                        vectors[index][second] = sine * left_val + cosine * right_val
    return ([work[index][index] for index in range(10 if count_in == 10 else count_in)], vectors)


def fdm_tables():
    stiffness, masses = margin_matrices()
    scaled = [
        [
            stiffness[row_at][other] / math.sqrt(masses[row_at] * masses[other])
            for other in range(10)
        ]
        for row_at in range(10)
    ]
    values, vectors = jacobi_eigen(scaled)
    basis = np.array(
        [
            [vectors[row_at][other] / math.sqrt(masses[row_at]) for other in range(10)]
            for row_at in range(10)
        ]
    )
    return (basis, np.array(values))


def z_forward_table(elements):
    basis, values = fdm_tables()
    extend_np = np.zeros((8 * elements, 10 * elements))
    for element in range(elements):
        for slot_in in range(10):
            source = 8 * element + slot_in - 1
            if slot_in == 0:
                source = 8 * element - 2
            if slot_in == 9:
                source = 8 * element + 9
            if 0 <= source < 8 * elements:
                extend_np[source, 10 * element + slot_in] = 1.0
    return extend_np @ np.kron(np.eye(elements), basis)


def z_backward_table(elements):
    basis, values = fdm_tables()
    return np.kron(np.eye(elements), basis[1:9].T)


def z_derivative(elements):
    return np.kron(np.eye(elements), derivative_table().T)


def z_pairs(elements):
    pairs_np = np.eye(8 * elements)
    for element in range(elements - 1):
        pairs_np[8 * element + 7, 8 * element + 8] = 1.0
        pairs_np[8 * element + 8, 8 * element + 7] = 1.0
    return pairs_np


LOCAL_X, LOCAL_Y, LOCAL_Z = (16, 32, 128)
ROWS = LOCAL_X * LOCAL_Y
DIRS = ((-1, -1), (-1, 1), (1, -1), (1, 1), (0, -1), (0, 1), (-1, 0), (1, 0))
F32 = jnp.float32
BF16 = jnp.bfloat16
MESH_ID = pl.DeviceIdType.MESH


def split_np(table):
    high = np.asarray(table, np.float32).astype(ml_dtypes.bfloat16)
    low = (np.asarray(table, np.float64) - high.astype(np.float64)).astype(ml_dtypes.bfloat16)
    return (high, low)


def left_table(matrix, rows):
    high, low = split_np(matrix)
    joined = np.concatenate([high, high, low], axis=1)
    out = np.zeros((rows, 128), ml_dtypes.bfloat16)
    out[: joined.shape[0], : joined.shape[1]] = joined
    return out


def y_pairs():
    pairs = np.eye(LOCAL_Y)
    for element in range(LOCAL_Y // 8 - 1):
        pairs[8 * element + 7, 8 * element + 8] = 1.0
        pairs[8 * element + 8, 8 * element + 7] = 1.0
    return pairs


def inner_share(count_in):
    share = np.ones(count_in)
    for position in range(count_in):
        if position % 8 in (0, 7) and position not in (0, count_in - 1):
            share[position] = 0.5
    return share


def padded_to(matrix, rows, columns):
    out = np.zeros((rows, columns))
    out[: matrix.shape[0], : matrix.shape[1]] = matrix
    return out


def make_tables():
    basis, values = fdm_tables()
    deriv = derivative_table()
    ends = np.ones(LOCAL_Z)
    ends[0] = 0.0
    ends[-1] = 0.0
    pairs_z = z_pairs(LOCAL_Z // 8)
    fore = pairs_z @ np.diag(ends) @ z_forward_table(LOCAL_Z // 8)
    back = z_backward_table(LOCAL_Z // 8) @ pairs_z @ np.diag(ends * inner_share(LOCAL_Z))
    fore_hi, fore_lo = split_np(padded_to(fore, 128, 256))
    back_hi, back_lo = split_np(padded_to(back, 256, 128))
    zf1 = np.concatenate([fore_hi, fore_hi], axis=0)
    zb1 = np.concatenate([back_hi, back_lo], axis=1)

    def square(matrix):
        high, low = split_np(matrix)
        return np.concatenate([np.concatenate([high, low], axis=1)] * 2, axis=0)

    deriv_z = np.kron(np.eye(LOCAL_Z // 8), deriv.T)
    deriv_y = np.kron(np.eye(LOCAL_Y // 8), deriv)
    count_y = LOCAL_Y // 8
    extend = np.zeros((10 * count_y, 40))
    for element in range(count_y):
        for slot in range(10):
            source = 8 * element + slot - 1
            if slot == 0:
                source = 8 * element - 2 if element else 32
            if slot == 9:
                source = 8 * element + 9 if element + 1 < count_y else 33
            extend[10 * element + slot, source] = 1.0
    y_fore = np.kron(np.eye(count_y), basis.T) @ extend
    y_back = np.diag(inner_share(LOCAL_Y)) @ y_pairs() @ np.kron(np.eye(count_y), basis[1:9])
    sums = (
        values[:, None, None]
        + np.tile(values, count_y)[None, :, None]
        + np.tile(values, LOCAL_Z // 8)[None, None, :]
        + SHIFT_MASS
    )
    recip = np.zeros((10 * 40, 256), np.float32)
    recip[:, :160] = (1.0 / sums).reshape(400, 160)
    weights = np.array(GLL_WEIGHTS)
    wyz = np.tile(weights, count_y)[:, None] * np.tile(weights, LOCAL_Z // 8)[None, :]
    spread = np.zeros((LOCAL_Z // 8, LOCAL_Z), ml_dtypes.bfloat16)
    for element in range(LOCAL_Z // 8):
        spread[element, 8 * element] = 1.0
    return dict(
        yf=left_table(y_fore, 48),
        yb=left_table(y_back, 32),
        yd=left_table(deriv_y, 32),
        ydt=left_table(deriv_y.T, 32),
        zf1=zf1,
        zf2=fore_lo,
        zb1=zb1,
        zd=square(deriv_z),
        zdt=square(deriv_z.T),
        wyz=wyz.astype(np.float32),
        spread=spread,
        recip=recip,
    )


TABLE_NAMES = ("yf", "yb", "yd", "ydt", "zf1", "zf2", "zb1", "zd", "zdt", "wyz", "spread", "recip")


def parity_signs(basis):
    signs = []
    for mode in range(10):
        even = np.abs(basis[:, mode] - basis[::-1, mode]).max()
        odd = np.abs(basis[:, mode] + basis[::-1, mode]).max()
        signs.append(1 if even < odd else -1)
    return signs


def weighted(coefficients, terms):
    total = None
    for coefficient, term in zip(coefficients, terms):
        piece = term * float(coefficient)
        total = piece if total is None else total + piece
    return total


def x_derive(values, matrix):
    sums = [values[i] + values[7 - i] for i in range(4)]
    gaps = [values[i] - values[7 - i] for i in range(4)]
    out = [None] * 8
    for p in range(4):
        first = weighted([(matrix[p, i] + matrix[p, 7 - i]) / 2 for i in range(4)], sums)
        second = weighted([(matrix[p, i] - matrix[p, 7 - i]) / 2 for i in range(4)], gaps)
        out[p] = second + first
        out[7 - p] = second - first
    return out


def x_modes(values, basis, signs):
    sums = [values[i] + values[9 - i] for i in range(5)]
    gaps = [values[i] - values[9 - i] for i in range(5)]
    return [
        weighted([basis[i, mode] for i in range(5)], sums if signs[mode] > 0 else gaps)
        for mode in range(10)
    ]


def x_unmodes(values, basis, signs):
    evens = [mode for mode in range(10) if signs[mode] > 0]
    odds = [mode for mode in range(10) if signs[mode] < 0]
    out = [None] * 8
    for i in range(1, 5):
        first = weighted([basis[i, mode] for mode in evens], [values[mode] for mode in evens])
        second = weighted([basis[i, mode] for mode in odds], [values[mode] for mode in odds])
        out[i - 1] = first + second
        out[8 - i] = first - second
    return out


def dot(first, second):
    return jnp.dot(first, second, preferred_element_type=F32)


def halves(values):
    high = values.astype(BF16)
    return (high, (values - high.astype(F32)).astype(BF16))


def left_mul(table, first, second):
    values = jnp.concatenate([first, second], axis=1)
    high = values.astype(BF16).astype(F32)
    rows = values.shape[0]
    parts = [high, values - high, high]
    if 3 * rows < 128:
        parts.append(jnp.zeros((128 - 3 * rows, values.shape[1]), F32))
    return dot(table, jnp.concatenate(parts, axis=0).astype(BF16))


def right_mul(values, table):
    high, low = halves(values)
    out = dot(jnp.concatenate([high, low], axis=1), table)
    return out[:, :128] + out[:, 128:]


def fold_rows(values):
    return jnp.sum(values.reshape(values.shape[0] // 8, 8, 128), axis=0)


def all_sum(values):
    lanes = jnp.sum(jnp.sum(values, axis=0, keepdims=True), axis=1, keepdims=True)
    return jnp.broadcast_to(lanes, (8, 128))


def times_tile(values, tile):
    return (values.reshape(values.shape[0] // 8, 8, 128) * tile[None]).reshape(values.shape)


def message_rows(direction, layers, extra):
    sx, sy = direction
    rows = 8 * layers if sx and sy else 32 * layers if sx else 16 * layers
    return rows + (8 if extra else 0)


def message_offsets(layers, extra):
    offsets = [0]
    for direction in DIRS:
        offsets.append(offsets[-1] + message_rows(direction, layers, extra))
    return offsets


OUT_NAMES = ("z0", "z1", "r1", "az", "p0", "sol", "steps")
ROUNDS = (("rhs", 2, True), ("sol", 1, False), ("sch0", 1, False), ("sti0", 2, False), ("sch1", 1, False), ("sti1", 1, False))


def body(sizes, *refs):
    n_grp, n_low, n_high = sizes
    n_dev = n_low * n_high
    (rhs_h, coef_h, sol_h, dif_h, flags_h, crow_h) = refs[:6]
    refs = refs[6:]
    tab_h = refs[: len(TABLE_NAMES)]
    refs = refs[len(TABLE_NAMES) :]
    outs = dict(zip(OUT_NAMES, refs))
    refs = refs[len(OUT_NAMES) :]
    names = ("rhs", "kc", "kd", "sol", "solraw", "pin", "y1", "u", "v", "x2")
    names += ("s", "z0", "b", "p0", "w", "z1", "r1", "a1", "ct")
    buf = dict(zip(names, refs))
    refs = refs[len(names) :]
    send_bufs = dict(zip([r[0] for r in ROUNDS], refs[:6]))
    recv_bufs = dict(zip([r[0] for r in ROUNDS], refs[6:12]))
    g_send, g_recv, halo_send_sem, halo_recv_sem, g_send_sem, g_recv_sem = refs[12:18]
    load_sem, store_sem, flags_ref, crow_ref, steps_ref = refs[18:23]
    tab = dict(zip(TABLE_NAMES, refs[23:]))

    grp = lax.axis_index("grp")
    dev = lax.axis_index("dev")
    low = dev & (n_low - 1)
    high = lax.shift_right_logical(dev, n_low.bit_length() - 1)
    x_lo = jnp.where(grp > 0, 1.0, 0.0).astype(F32)
    x_hi = jnp.where(grp < n_grp - 1, 1.0, 0.0).astype(F32)
    y_lo = jnp.where(dev > 0, 1.0, 0.0).astype(F32)
    y_hi = jnp.where(dev < n_dev - 1, 1.0, 0.0).astype(F32)

    def neighbour(direction):
        return ((grp + direction[0]) & (n_grp - 1), (dev + direction[1]) & (n_dev - 1))

    def stage_partner(stage, step):
        if stage == 0:
            return (grp, high * n_low + ((low + step) & (n_low - 1)))
        if stage == 1:
            return (grp, ((high + step) & (n_high - 1)) * n_low + low)
        return ((grp + step) & (n_grp - 1), dev)

    stage_sizes = (n_low, n_high, n_grp)

    def steps_of(stage):
        size = stage_sizes[stage]
        return sorted(range(1, size), key=lambda step: -min(step, size - step))

    barrier = pltpu.get_barrier_semaphore()
    partners = [neighbour(direction) for direction in DIRS]
    for stage in range(3):
        partners += [stage_partner(stage, step) for step in steps_of(stage)]
    for partner in partners:
        pl.semaphore_signal(barrier, inc=1, device_id=partner, device_id_type=MESH_ID)
    loads = {}
    wanted = [("rhs", rhs_h, buf["rhs"]), ("crow", crow_h, crow_ref)]
    wanted += [("sol", sol_h, buf["sol"]), ("kd", dif_h, buf["kd"]), ("flags", flags_h, flags_ref)]
    wanted += [(name, source, tab[name]) for name, source in zip(TABLE_NAMES, tab_h)]
    wanted += [("kc", coef_h, buf["kc"])]
    for at, (name, source, target) in enumerate(wanted):
        loads[name] = pltpu.make_async_copy(source, target, load_sem.at[at])
        loads[name].start()

    row32 = lax.broadcasted_iota(jnp.int32, (32, 128), 0)
    lane32 = lax.broadcasted_iota(jnp.int32, (32, 128), 1)
    keep_z = jnp.where((lane32 > 0) & (lane32 < 127), 1.0, 0.0).astype(F32)
    share_z = jnp.where(((lane32 % 8 == 0) | (lane32 % 8 == 7)) & (lane32 > 0) & (lane32 < 127), 0.5, 1.0).astype(F32)
    lane_up = jnp.where((lane32 % 8 == 7) & (lane32 < 127), 1.0, 0.0).astype(F32)
    lane_down = jnp.where((lane32 % 8 == 0) & (lane32 > 0), 1.0, 0.0).astype(F32)
    row_up = jnp.where((row32 % 8 == 7) & (row32 < 31), 1.0, 0.0).astype(F32)
    row_down = jnp.where((row32 % 8 == 0) & (row32 > 0), 1.0, 0.0).astype(F32)
    edge_y = jnp.where(row32 == 0, y_lo, jnp.where(row32 == 31, y_hi, 1.0)).astype(F32)
    inner_y = jnp.where((row32 % 8 == 0) | (row32 % 8 == 7), 0.5, 1.0).astype(F32)
    face_y = jnp.where((row32 == 0) | (row32 == 31), 0.5, 1.0).astype(F32) * edge_y
    share_y = inner_y * edge_y
    tile_row = lax.broadcasted_iota(jnp.int32, (8, 128), 0)
    tile_lane = lax.broadcasted_iota(jnp.int32, (8, 128), 1)
    tile_index = tile_row * 128 + tile_lane

    def share_x(plane):
        if plane == 0:
            return 0.5 * x_lo
        if plane == 15:
            return 0.5 * x_hi
        return 0.5 if plane in (7, 8) else 1.0

    def x_times(values, factor):
        return values if isinstance(factor, float) and factor == 1.0 else values * factor

    def z_assembled(values):
        return (
            values
            + lane_up * pltpu.roll(values, 127, 1)
            + lane_down * pltpu.roll(values, 1, 1)
        )

    def y_assembled(values):
        return (
            values + row_up * pltpu.roll(values, 31, 0) + row_down * pltpu.roll(values, 1, 0)
        )

    halo_copies = {}

    def exchange(name, src, tile=None):
        at_round = [r[0] for r in ROUNDS].index(name)
        layers, extra = ROUNDS[at_round][1:]
        offsets = message_offsets(layers, extra)
        send, recv = send_bufs[name], recv_bufs[name]
        copies = []
        for at, direction in enumerate(DIRS):
            sx, sy = direction
            base = offsets[at]
            rows = message_rows(direction, layers, False)
            if sx and sy:
                for layer in range(layers):
                    plane = layer if sx < 0 else 16 - layers + layer
                    start = 32 * plane + (0 if sy < 0 else 24)
                    send[base + 8 * layer : base + 8 * layer + 8, :] = src[start : start + 8, :]
            elif sx:
                start = 0 if sx < 0 else 32 * (16 - layers)
                send[base : base + rows, :] = src[start : start + rows, :]
            else:
                for layer in range(layers):
                    row = layer if sy < 0 else 32 - layers + layer
                    send[base + 16 * layer : base + 16 * layer + 16, :] = src[
                        pl.ds(row, 16, stride=32), :
                    ]
            if extra:
                send[base + rows : base + rows + 8, :] = tile
            total = message_rows(direction, layers, extra)
            copy = pltpu.make_async_remote_copy(
                src_ref=send.at[pl.ds(base, total)],
                dst_ref=recv.at[pl.ds(base, total)],
                send_sem=halo_send_sem.at[8 * at_round + at],
                recv_sem=halo_recv_sem.at[8 * at_round + at],
                device_id=neighbour(direction),
                device_id_type=MESH_ID,
            )
            copy.start()
            copies.append(copy)
        halo_copies[name] = copies

    def arrived(name):
        for copy in halo_copies[name]:
            copy.wait_recv()

    def part(name, direction, layer=0):
        at_round = [r[0] for r in ROUNDS].index(name)
        layers, extra = ROUNDS[at_round][1:]
        offsets = message_offsets(layers, extra)
        at = DIRS.index((-direction[0], -direction[1]))
        unit = 8 if direction[0] and direction[1] else 32 if direction[0] else 16
        start = offsets[at] + unit * layer
        return recv_bufs[name][start : start + unit, :]

    def part_row(name, direction, layer, last):
        at_round = [r[0] for r in ROUNDS].index(name)
        layers, extra = ROUNDS[at_round][1:]
        at = DIRS.index((-direction[0], -direction[1]))
        start = message_offsets(layers, extra)[at] + 8 * layer + last
        return recv_bufs[name][start : start + 1, :]

    def add_faces(name, ref, masked):
        def scale(values, first, second):
            if not masked:
                return values
            return values * (first * second if first is not None and second is not None else second if first is None else first)

        ref[0:32, :] += scale(part(name, (-1, 0)), x_lo, None)
        ref[480:512, :] += scale(part(name, (1, 0)), x_hi, None)
        ref[pl.ds(0, 16, stride=32), :] += scale(part(name, (0, -1)), y_lo, None)
        ref[pl.ds(31, 16, stride=32), :] += scale(part(name, (0, 1)), y_hi, None)
        ref[0:1, :] += scale(part_row(name, (-1, -1), 0, 7), x_lo, y_lo)
        ref[31:32, :] += scale(part_row(name, (-1, 1), 0, 0), x_lo, y_hi)
        ref[480:481, :] += scale(part_row(name, (1, -1), 0, 7), x_hi, y_lo)
        ref[511:512, :] += scale(part_row(name, (1, 1), 0, 0), x_hi, y_hi)

    def add_arrived(name, ref):
        arrived(name)
        add_faces(name, ref, False)

    g_copies = []
    g_pending = {}

    def g_start(which, stage, tile):
        slot = 3 * which + stage
        g_send[8 * slot : 8 * slot + 8, :] = tile
        copies = []
        for step in steps_of(stage):
            at = 7 * slot + step - 1
            copy = pltpu.make_async_remote_copy(
                src_ref=g_send.at[pl.ds(8 * slot, 8)],
                dst_ref=g_recv.at[pl.ds(8 * at, 8)],
                send_sem=g_send_sem.at[at],
                recv_sem=g_recv_sem.at[at],
                device_id=stage_partner(stage, step),
                device_id_type=MESH_ID,
            )
            copy.start()
            copies.append(copy)
        g_copies.extend(copies)
        g_pending[slot] = (tile, copies)

    def g_finish(which, stage):
        slot = 3 * which + stage
        tile, copies = g_pending[slot]
        for copy in copies:
            copy.wait_recv()
        for step in steps_of(stage):
            at = 7 * slot + step - 1
            tile = tile + g_recv[8 * at : 8 * at + 8, :]
        return tile

    def g_forward(which, stage):
        g_start(which, stage + 1, g_finish(which, stage))

    def scalar_spot(at):
        return jnp.where(tile_index == 4 * 128 + at, 1.0, 0.0).astype(F32)

    def read_scalar(tile, at):
        return all_sum(tile * scalar_spot(at))

    def coarse_tile(ref):
        middle = None
        for plane in range(16):
            piece = x_times(ref[32 * plane : 32 * plane + 32, :], share_x(plane))
            middle = piece if middle is None else middle + piece
        tile = jnp.zeros((8, 128), F32)
        rows = {
            -1: ref[0:32, :] * (0.5 * x_lo),
            0: middle,
            1: ref[480:512, :] * (0.5 * x_hi),
        }
        for dx in (-1, 0, 1):
            field = rows[dx] * keep_z
            own = fold_rows(field * share_y)
            before = field[0:8] * jnp.where(tile_row == 0, 0.5 * y_lo, 0.0)
            after = field[24:32] * jnp.where(tile_row == 7, 0.5 * y_hi, 0.0)
            for dy, values in ((-1, before), (0, own), (1, after)):
                spot = ((grp + dx) & (n_grp - 1)) * n_dev + ((dev + dy) & (n_dev - 1))
                tile = tile + jnp.where(tile_index == spot, all_sum(values), 0.0)
        return tile

    q_scale = 1.0 / math.sqrt(LOCAL_X * LOCAL_Y * LOCAL_Z)

    def coarse_patterns(tile):
        values = {}
        for dx in (-1, 0, 1):
            for dy in (-1, 0, 1):
                if dx == 0 and dy == 0:
                    row = buf["ct"][...]
                else:
                    direction = (dx, dy)
                    layers, extra = ROUNDS[0][1:]
                    at = DIRS.index((-dx, -dy))
                    start = message_offsets(layers, extra)[at] + message_rows((dx, dy), layers, False)
                    row = recv_bufs["rhs"][start : start + 8, :]
                values[dx, dy] = all_sum(row * tile) * q_scale
        lines = {}
        for dx in (-1, 0, 1):
            centre = jnp.concatenate([values[dx, 0]] * 4, axis=0)
            first = jnp.concatenate([values[dx, -1]] * 4, axis=0)
            last = jnp.concatenate([values[dx, 1]] * 4, axis=0)
            line = jnp.where(row32 == 0, (centre + first) * (0.5 * y_lo), centre)
            line = jnp.where(row32 == 31, (centre + last) * (0.5 * y_hi), line)
            lines[dx] = line * keep_z
        return (
            (lines[0] + lines[-1]) * (0.5 * x_lo),
            lines[0],
            (lines[0] + lines[1]) * (0.5 * x_hi),
        )

    def build_pin(name, src):
        pin = buf["pin"]
        zero8 = jnp.zeros((8, 128), F32)
        for plane in range(18):
            pin[40 * plane + 32 : 40 * plane + 40, :] = zero8
        for plane in range(16):
            pin[40 * (plane + 1) : 40 * (plane + 1) + 32, :] = src[32 * plane : 32 * plane + 32, :]
        pin[40:72, :] += part(name, (-1, 0), 1)
        pin[640:672, :] += part(name, (1, 0), 0)
        pin[pl.ds(40, 16, stride=40), :] += part(name, (0, -1), 1)
        pin[pl.ds(71, 16, stride=40), :] += part(name, (0, 1), 0)
        pin[pl.ds(72, 16, stride=40), :] = part(name, (0, -1), 0)
        pin[pl.ds(73, 16, stride=40), :] = part(name, (0, 1), 1)
        for at_plane, dx, layer in ((1, -1, 1), (16, 1, 0), (0, -1, 0), (17, 1, 1)):
            base = 40 * at_plane
            if at_plane in (0, 17):
                pin[base : base + 32, :] = part(name, (dx, 0), layer)
            pin[base : base + 1, :] += part_row(name, (dx, -1), layer, 7)
            pin[base + 31 : base + 32, :] += part_row(name, (dx, 1), layer, 0)
            pin[base + 32 : base + 33, :] += part_row(name, (dx, -1), layer, 6)
            pin[base + 33 : base + 34, :] += part_row(name, (dx, 1), layer, 1)

    row40 = lax.broadcasted_iota(jnp.int32, (40, 128), 0)
    edge40 = jnp.where(
        (row40 == 0) | (row40 == 32), y_lo, jnp.where((row40 == 31) | (row40 == 33), y_hi, 1.0)
    ).astype(F32)

    def pin_plane(plane):
        values = buf["pin"][40 * plane : 40 * plane + 40, :] * edge40
        if plane < 2:
            values = values * x_lo
        if plane > 15:
            values = values * x_hi
        return values

    def assembled_own(plane):
        return z_assembled(pin_plane(plane + 1)[0:32]) * keep_z

    basis, _ = fdm_tables()
    signs = parity_signs(basis)
    deriv = derivative_table()
    sources = ([0, 1, 2, 3, 4, 5, 6, 7, 8, 10], [7, 9, 10, 11, 12, 13, 14, 15, 16, 17])

    def schwarz(dst):
        y1, u, v, x2 = buf["y1"], buf["u"], buf["v"], buf["x2"]
        yf, yb = tab["yf"][...], tab["yb"][...]
        for pair in range(9):
            out = left_mul(yf, pin_plane(2 * pair), pin_plane(2 * pair + 1))
            y1[80 * pair : 80 * pair + 40, :] = out[0:40, :128]
            y1[80 * pair + 40 : 80 * pair + 80, :] = out[0:40, 128:]
        for element in range(2):
            for tile in range(5):
                values = [y1[40 * p + 8 * tile : 40 * p + 8 * tile + 8, :] for p in sources[element]]
                for mode, piece in enumerate(x_modes(values, basis, signs)):
                    start = 40 * (10 * element + mode) + 8 * tile
                    u[start : start + 8, :] = piece
        for element in range(2):
            block = u[400 * element : 400 * element + 400, :]
            first, second = halves(block)
            modes = dot(jnp.concatenate([first, second], axis=1), tab["zf1"][...])
            modes = (modes + dot(first, tab["zf2"][...])) * tab["recip"][...]
            first, second = halves(modes)
            back = dot(first, tab["zb1"][...])
            v[400 * element : 400 * element + 400, :] = (
                back[:, :128] + back[:, 128:] + dot(second, tab["zb1"][:, 0:128])
            )
        for tile in range(5):
            outs = []
            for element in range(2):
                starts = [40 * (10 * element + mode) + 8 * tile for mode in range(10)]
                outs += x_unmodes([v[s : s + 8, :] for s in starts], basis, signs)
            shared = (outs[7] + outs[8]) * 0.5
            outs[7] = shared
            outs[8] = shared
            outs[0] = outs[0] * (0.5 * x_lo)
            outs[15] = outs[15] * (0.5 * x_hi)
            for plane in range(16):
                x2[40 * plane + 8 * tile : 40 * plane + 8 * tile + 8, :] = outs[plane]
        for pair in range(8):
            out = left_mul(yb, x2[80 * pair : 80 * pair + 40, :], x2[80 * pair + 40 : 80 * pair + 80, :])
            dst[64 * pair : 64 * pair + 32, :] = out[:, :128] * face_y
            dst[64 * pair + 32 : 64 * pair + 64, :] = out[:, 128:] * face_y

    def stiff(src, coef, dst, extra=None):
        energy = jnp.zeros((8, 128), F32)
        for chunk in range(2):
            at = slice(256 * chunk, 256 * chunk + 256)
            grad = right_mul(src[at, :], tab["zd"][...])
            flow = grad * coef[at, :]
            energy = energy + fold_rows(grad * flow)
            dst[at, :] = right_mul(flow, tab["zdt"][...])
        for pair in range(8):
            one = slice(64 * pair, 64 * pair + 32)
            two = slice(64 * pair + 32, 64 * pair + 64)
            grad = left_mul(tab["yd"][...], src[one, :], src[two, :])
            flow_one = grad[:, :128] * coef[one, :]
            flow_two = grad[:, 128:] * coef[two, :]
            energy = energy + fold_rows(grad[:, :128] * flow_one) + fold_rows(grad[:, 128:] * flow_two)
            back = left_mul(tab["ydt"][...], flow_one, flow_two)
            dst[one, :] += back[:, :128]
            dst[two, :] += back[:, 128:]
        for tile in range(4):
            sums = []
            for element in range(2):
                starts = [32 * (8 * element + i) + 8 * tile for i in range(8)]
                grads = x_derive([src[s : s + 8, :] for s in starts], deriv)
                flows = [grad * coef[s : s + 8, :] for grad, s in zip(grads, starts)]
                for grad, flow in zip(grads, flows):
                    energy = energy + grad * flow
                backs = x_derive(flows, deriv.T)
                for s, back in zip(starts, backs):
                    value = dst[s : s + 8, :] + back
                    if extra is not None:
                        value = value + extra[s : s + 8, :]
                    sums.append(value)
            shared = sums[7] + sums[8]
            sums[7] = shared
            sums[8] = shared
            for plane in range(16):
                dst[32 * plane + 8 * tile : 32 * plane + 8 * tile + 8, :] = sums[plane]
        for plane in range(16):
            at = slice(32 * plane, 32 * plane + 32)
            dst[at, :] = y_assembled(dst[at, :])
        return energy

    weights = GLL_WEIGHTS + GLL_WEIGHTS

    loads["rhs"].wait()
    loads["crow"].wait()
    for plane in range(16):
        at = slice(32 * plane, 32 * plane + 32)
        values = buf["rhs"][at, :]
        if plane == 7:
            values = values + buf["rhs"][256:288, :]
        if plane == 8:
            values = values + buf["rhs"][224:256, :]
        buf["s"][at, :] = y_assembled(values)
    ct = buf["ct"]
    ct[...] = jnp.zeros((8, 128), F32)
    count = n_grp * n_dev
    for chunk in range((count + 127) // 128):
        width = min(128, count - 128 * chunk)
        ct[chunk : chunk + 1, 0:width] = crow_ref[:, 128 * chunk : 128 * chunk + width]
    first_tile = coarse_tile(buf["s"])

    pl.semaphore_wait(barrier, len(partners))
    g_start(0, 0, first_tile)
    exchange("rhs", buf["s"], ct[...])

    for name in ("sol", "kd", "flags", "wyz", "spread", "zd", "zdt", "yd", "ydt"):
        loads[name].wait()
    wyz = tab["wyz"][...]
    flags = jnp.concatenate([flags_ref[0], flags_ref[1]], axis=0).astype(F32).astype(BF16)
    flag_rows = dot(flags, tab["spread"][...])
    weight_column = GLL_WEIGHTS
    row8 = tile_row
    w_rows = jnp.zeros((8, 128), F32)
    for at, weight in enumerate(weight_column):
        w_rows = jnp.where(row8 == at, weight, w_rows)
    for plane in range(16):
        at = slice(32 * plane, 32 * plane + 32)
        buf["kd"][at, :] = buf["kd"][at, :] * (wyz * weights[plane])
        flux = jnp.concatenate(
            [
                flag_rows[4 * (plane // 8) + ey : 4 * (plane // 8) + ey + 1, :] * w_rows
                for ey in range(4)
            ],
            axis=0,
        )
        factor = wyz * (MASS_RATE * weights[plane]) + flux * (GROWTH * SEGREGATION * weights[plane])
        buf["x2"][at, :] = buf["sol"][at, :] * factor
    stiff(buf["sol"], buf["kd"], buf["solraw"], extra=buf["x2"])

    exchange("sol", buf["solraw"])
    for name in ("kc", "yf", "yb", "zf1", "zf2", "zb1", "recip"):
        loads[name].wait()
    for plane in range(16):
        at = slice(32 * plane, 32 * plane + 32)
        buf["kc"][at, :] = buf["kc"][at, :] * (wyz * weights[plane])

    stores = []

    def store(name, ref):
        copy = pltpu.make_async_copy(ref, outs[name], store_sem.at[OUT_NAMES.index(name)])
        copy.start()
        stores.append(copy)

    g_forward(0, 0)
    arrived("rhs")
    build_pin("rhs", buf["s"])
    schwarz(buf["z0"])
    exchange("sch0", buf["z0"])
    g_forward(0, 1)
    for plane in range(16):
        buf["b"][32 * plane : 32 * plane + 32, :] = assembled_own(plane)
    add_arrived("sch0", buf["z0"])
    patterns = coarse_patterns(g_finish(0, 2))

    def finish_precond(ref, patterns):
        for plane in range(16):
            at = slice(32 * plane, 32 * plane + 32)
            ref[at, :] += patterns[0 if plane == 0 else 2 if plane == 15 else 1]

    finish_precond(buf["z0"], patterns)
    share_yz = share_y * share_z

    def energy_of(first, second):
        tile = jnp.zeros((8, 128), F32)
        for plane in range(16):
            at = slice(32 * plane, 32 * plane + 32)
            piece = x_times(first[at, :] * second[at, :] * share_yz, share_x(plane))
            tile = tile + fold_rows(piece)
        return all_sum(tile)

    curve = all_sum(stiff(buf["z0"], buf["kc"], buf["a1"]))
    rz = energy_of(buf["b"], buf["z0"])
    tile = coarse_tile(buf["a1"])
    tile = tile + scalar_spot(0) * rz + scalar_spot(1) * curve
    g_start(1, 0, tile)
    exchange("sti0", buf["a1"])

    arrived("sol")
    add_faces("sol", buf["solraw"], True)
    for plane in range(16):
        at = slice(32 * plane, 32 * plane + 32)
        buf["solraw"][at, :] = z_assembled(buf["solraw"][at, :])
    store("sol", buf["solraw"])

    g_forward(1, 0)
    arrived("sti0")
    build_pin("sti0", buf["a1"])
    schwarz(buf["w"])
    exchange("sch1", buf["w"])
    g_forward(1, 1)
    for plane in range(16):
        buf["p0"][32 * plane : 32 * plane + 32, :] = assembled_own(plane)
    add_arrived("sch1", buf["w"])
    total = g_finish(1, 2)
    patterns = coarse_patterns(total)
    rz0 = read_scalar(total, 0)
    curve0 = read_scalar(total, 1)
    alpha0 = rz0 / curve0
    for plane in range(16):
        at = slice(32 * plane, 32 * plane + 32)
        buf["r1"][at, :] = buf["b"][at, :] - times_tile(buf["p0"][at, :], alpha0)
    finish_precond(buf["w"], patterns)
    for plane in range(16):
        at = slice(32 * plane, 32 * plane + 32)
        buf["z1"][at, :] = buf["z0"][at, :] - times_tile(buf["w"][at, :], alpha0)
    curve = all_sum(stiff(buf["z1"], buf["kc"], buf["rhs"]))
    rz = energy_of(buf["r1"], buf["z1"])
    cross = energy_of(buf["p0"], buf["z1"])
    g_start(2, 0, scalar_spot(0) * rz + scalar_spot(1) * curve + scalar_spot(2) * cross)
    exchange("sti1", buf["rhs"])
    for name in ("z0", "z1", "r1", "p0"):
        store(name, buf[name])
    g_forward(2, 0)
    add_arrived("sti1", buf["rhs"])
    g_forward(2, 1)
    for plane in range(16):
        at = slice(32 * plane, 32 * plane + 32)
        values = z_assembled(buf["rhs"][at, :]) * keep_z * edge_y
        if plane == 0:
            values = values * x_lo
        if plane == 15:
            values = values * x_hi
        buf["rhs"][at, :] = values
    store("az", buf["rhs"])
    total = g_finish(2, 2)
    rz1 = read_scalar(total, 0)
    curve1 = read_scalar(total, 1)
    cross1 = read_scalar(total, 2)
    beta = rz1 / rz0
    full = curve1 + 2.0 * beta * cross1 + beta * beta * curve0
    alpha1 = rz1 / full
    steps_ref[0:8, :] = alpha0 + alpha1 * beta
    steps_ref[8:16, :] = alpha1
    steps_ref[16:24, :] = alpha1 * beta
    store("steps", steps_ref)
    for name in halo_copies:
        for copy in halo_copies[name]:
            copy.wait_send()
    for copy in g_copies:
        copy.wait_send()
    for copy in stores:
        copy.wait()


def finish_body(*refs):
    count = len(OUT_NAMES)
    sources, targets, bufs, load_sem, store_sem = refs[:count], refs[count : count + 3], refs[count + 3 : 2 * count + 3], refs[-2], refs[-1]
    loads = {}
    for at in (6, 0, 1, 2, 3, 4, 5):
        loads[OUT_NAMES[at]] = pltpu.make_async_copy(sources[at], bufs[at], load_sem.at[at])
        loads[OUT_NAMES[at]].start()
    z0, z1, r1, az, p0, sol, steps = bufs
    for name in ("steps", "z0", "z1"):
        loads[name].wait()
    old, new, back = steps[0:8, :], steps[8:16, :], steps[16:24, :]
    for plane in range(LOCAL_X):
        at = slice(32 * plane, 32 * plane + 32)
        z0[at, :] = times_tile(z0[at, :], old) + times_tile(z1[at, :], new)
    stores = [pltpu.make_async_copy(z0, targets[0], store_sem.at[0])]
    stores[0].start()
    for name in ("r1", "az", "p0"):
        loads[name].wait()
    for plane in range(LOCAL_X):
        at = slice(32 * plane, 32 * plane + 32)
        r1[at, :] = r1[at, :] - times_tile(az[at, :], new) - times_tile(p0[at, :], back)
    stores.append(pltpu.make_async_copy(r1, targets[1], store_sem.at[1]))
    stores[1].start()
    loads["sol"].wait()
    stores.append(pltpu.make_async_copy(sol, targets[2], store_sem.at[2]))
    stores[2].start()
    for copy in stores:
        copy.wait()


def finish(fields):
    far = pl.BlockSpec(memory_space=pltpu.HBM)
    return pl.pallas_call(
        finish_body,
        out_shape=[jax.ShapeDtypeStruct((ROWS, LOCAL_Z), F32)] * 3,
        in_specs=[far] * len(OUT_NAMES),
        out_specs=[far] * 3,
        scratch_shapes=[pltpu.VMEM(v.shape, F32) for v in fields]
        + [pltpu.SemaphoreType.DMA((len(OUT_NAMES),)), pltpu.SemaphoreType.DMA((3,))],
        compiler_params=pltpu.CompilerParams(vmem_limit_bytes=63 * 1024 * 1024),
    )(*fields)


def run_kernel(sizes, fields, flags, coarse_row, tables):
    constants = [jnp.asarray(tables[name]) for name in TABLE_NAMES]
    far = pl.BlockSpec(memory_space=pltpu.HBM)
    field = pltpu.VMEM((ROWS, LOCAL_Z), F32)

    def rows(count):
        return pltpu.VMEM((count, LOCAL_Z), F32)

    halo = [rows(message_offsets(layers, extra)[-1]) for _, layers, extra in ROUNDS]
    scratch = (
        [field] * 5
        + [rows(720), rows(720), rows(800), rows(800), rows(640)]
        + [field] * 8
        + [rows(8)]
        + halo
        + halo
        + [rows(72), rows(8 * 63)]
        + [pltpu.SemaphoreType.DMA((count,)) for count in (48, 48, 63, 63, 6 + len(constants), len(OUT_NAMES))]
        + [pltpu.VMEM(flags.shape, jnp.int32), pltpu.VMEM(coarse_row.shape, F32), rows(24)]
        + [pltpu.VMEM(table.shape, table.dtype) for table in constants]
    )
    return pl.pallas_call(
        functools.partial(body, sizes),
        out_shape=[
            jax.ShapeDtypeStruct((24 if name == "steps" else ROWS, LOCAL_Z), F32) for name in OUT_NAMES
        ],
        in_specs=[far] * (6 + len(constants)),
        out_specs=[far] * len(OUT_NAMES),
        scratch_shapes=scratch,
        compiler_params=pltpu.CompilerParams(
            collective_id=0, has_side_effects=True, vmem_limit_bytes=63 * 1024 * 1024
        ),
    )(*fields, flags, coarse_row, *constants)


def solution(mesh):
    n_grp, n_dev = (mesh.shape["grp"], mesh.shape["dev"])
    n_low = 8 if n_dev % 8 == 0 else 2
    sizes = (n_grp, n_low, n_dev // n_low)
    tables = make_tables()

    def shards(right_side, coefficient, solute, diffusivity, interface_flags, coarse_inverse):
        fields = [v.reshape(ROWS, LOCAL_Z) for v in (right_side, coefficient, solute, diffusivity)]
        outs = run_kernel(sizes, fields, interface_flags, coarse_inverse, tables)
        return tuple(v.reshape(LOCAL_X, LOCAL_Y, LOCAL_Z) for v in finish(outs))

    placed = (
        P("grp", "dev", None),
        P("grp", "dev", None),
        P("grp", "dev", None),
        P("grp", "dev", None),
        P("grp", "dev", None),
        P(("grp", "dev"), None),
    )
    return jax.shard_map(
        shards,
        mesh=mesh,
        in_specs=placed,
        out_specs=(P("grp", "dev", None), P("grp", "dev", None), P("grp", "dev", None)),
        check_vma=False,
    )
```

```python
import functools
import math

import jax
import jax.numpy as jnp
import ml_dtypes
import numpy as np
from jax import lax
from jax.experimental import pallas as pl
from jax.experimental.pallas import tpu as pltpu
from jax.sharding import PartitionSpec as P

GLL_POINTS = [
    -1.0,
    -0.8717401485096066,
    -0.5917001814331423,
    -0.2092992179024789,
    0.2092992179024789,
    0.5917001814331423,
    0.8717401485096066,
    1.0,
]
GLL_WEIGHTS = [
    0.0357142857142857,
    0.2107042271435061,
    0.3411226924835044,
    0.4124587946587038,
    0.4124587946587038,
    0.3411226924835044,
    0.2107042271435061,
    0.0357142857142857,
]
SHIFT_MASS = 0.5
MASS_RATE = 2.0
GROWTH = 40.0
SEGREGATION = 0.7


def derivative_table():
    products = []
    for row_at in range(8):
        value = 1.0
        for other in range(8):
            if other != row_at:
                value = value * (GLL_POINTS[row_at] - GLL_POINTS[other])
        products.append(value)
    table = [[0.0] * 8 for row_at in range(8)]
    for row_at in range(8):
        total = 0.0
        for other in range(8):
            if other != row_at:
                entry = (
                    products[row_at] / products[other] / (GLL_POINTS[row_at] - GLL_POINTS[other])
                )
                table[row_at][other] = entry
                total = total + entry
        table[row_at][row_at] = -total
    return np.array(table)


def margin_matrices():
    deriv_np = derivative_table()
    spacing = GLL_POINTS[1] - GLL_POINTS[0]
    stiffness = [[0.0] * 10 for row_at in range(10)]
    masses = [0.0] * 10
    for row_at in range(8):
        masses[row_at + 1] = GLL_WEIGHTS[row_at]
        for other in range(8):
            total = 0.0
            for point in range(8):
                total = (
                    total + deriv_np[point, row_at] * GLL_WEIGHTS[point] * deriv_np[point, other]
                )
            stiffness[row_at + 1][other + 1] = total
    for outer_end, inner_end in ((0, 1), (9, 8)):
        stiffness[outer_end][outer_end] += 1.0 / spacing
        stiffness[inner_end][inner_end] += 1.0 / spacing
        stiffness[outer_end][inner_end] -= 1.0 / spacing
        stiffness[inner_end][outer_end] -= 1.0 / spacing
        masses[outer_end] += 0.5 * spacing
        masses[inner_end] += 0.5 * spacing
    return (stiffness, masses)


def jacobi_eigen(matrix_rows):
    count_in = len(matrix_rows)
    work = [list(row_now) for row_now in matrix_rows]
    vectors = [
        [1.0 if other == row_at else 0.0 for other in range(count_in)] for row_at in range(count_in)
    ]
    for sweep in range(15):
        for first in range(count_in):
            for second in range(first + 1, count_in):
                entry = work[first][second]
                if entry != 0.0:
                    theta = (work[second][second] - work[first][first]) / (2.0 * entry)
                    sign_now = 1.0 if theta >= 0.0 else -1.0
                    tangent = sign_now / (abs(theta) + math.sqrt(theta * theta + 1.0))
                    cosine = 1.0 / math.sqrt(tangent * tangent + 1.0)
                    sine = tangent * cosine
                    for index in range(count_in):
                        left_val = work[index][first]
                        right_val = work[index][second]
                        work[index][first] = cosine * left_val - sine * right_val
                        work[index][second] = sine * left_val + cosine * right_val
                    for index in range(count_in):
                        left_val = work[first][index]
                        right_val = work[second][index]
                        work[first][index] = cosine * left_val - sine * right_val
                        work[second][index] = sine * left_val + cosine * right_val
                    for index in range(count_in):
                        left_val = vectors[index][first]
                        right_val = vectors[index][second]
                        vectors[index][first] = cosine * left_val - sine * right_val
                        vectors[index][second] = sine * left_val + cosine * right_val
    return ([work[index][index] for index in range(10 if count_in == 10 else count_in)], vectors)


def fdm_tables():
    stiffness, masses = margin_matrices()
    scaled = [
        [
            stiffness[row_at][other] / math.sqrt(masses[row_at] * masses[other])
            for other in range(10)
        ]
        for row_at in range(10)
    ]
    values, vectors = jacobi_eigen(scaled)
    basis = np.array(
        [
            [vectors[row_at][other] / math.sqrt(masses[row_at]) for other in range(10)]
            for row_at in range(10)
        ]
    )
    return (basis, np.array(values))


def z_forward_table(elements):
    basis, values = fdm_tables()
    extend_np = np.zeros((8 * elements, 10 * elements))
    for element in range(elements):
        for slot_in in range(10):
            source = 8 * element + slot_in - 1
            if slot_in == 0:
                source = 8 * element - 2
            if slot_in == 9:
                source = 8 * element + 9
            if 0 <= source < 8 * elements:
                extend_np[source, 10 * element + slot_in] = 1.0
    return extend_np @ np.kron(np.eye(elements), basis)


def z_backward_table(elements):
    basis, values = fdm_tables()
    return np.kron(np.eye(elements), basis[1:9].T)


def z_derivative(elements):
    return np.kron(np.eye(elements), derivative_table().T)


def z_pairs(elements):
    pairs_np = np.eye(8 * elements)
    for element in range(elements - 1):
        pairs_np[8 * element + 7, 8 * element + 8] = 1.0
        pairs_np[8 * element + 8, 8 * element + 7] = 1.0
    return pairs_np


LOCAL_X, LOCAL_Y, LOCAL_Z = (16, 32, 128)
ROWS = LOCAL_X * LOCAL_Y
DIRS = ((-1, -1), (-1, 1), (1, -1), (1, 1), (0, -1), (0, 1), (-1, 0), (1, 0))
F32 = jnp.float32
BF16 = jnp.bfloat16
MESH_ID = pl.DeviceIdType.MESH


def split_np(table):
    high = np.asarray(table, np.float32).astype(ml_dtypes.bfloat16)
    low = (np.asarray(table, np.float64) - high.astype(np.float64)).astype(ml_dtypes.bfloat16)
    return (high, low)


def left_table(matrix, rows):
    high, low = split_np(matrix)
    joined = np.concatenate([high, high, low], axis=1)
    out = np.zeros((rows, 128), ml_dtypes.bfloat16)
    out[: joined.shape[0], : joined.shape[1]] = joined
    return out


def y_pairs():
    pairs = np.eye(LOCAL_Y)
    for element in range(LOCAL_Y // 8 - 1):
        pairs[8 * element + 7, 8 * element + 8] = 1.0
        pairs[8 * element + 8, 8 * element + 7] = 1.0
    return pairs


def inner_share(count_in):
    share = np.ones(count_in)
    for position in range(count_in):
        if position % 8 in (0, 7) and position not in (0, count_in - 1):
            share[position] = 0.5
    return share


def padded_to(matrix, rows, columns):
    out = np.zeros((rows, columns))
    out[: matrix.shape[0], : matrix.shape[1]] = matrix
    return out


def make_tables():
    basis, values = fdm_tables()
    deriv = derivative_table()
    ends = np.ones(LOCAL_Z)
    ends[0] = 0.0
    ends[-1] = 0.0
    pairs_z = z_pairs(LOCAL_Z // 8)
    fore = pairs_z @ np.diag(ends) @ z_forward_table(LOCAL_Z // 8)
    back = z_backward_table(LOCAL_Z // 8) @ pairs_z @ np.diag(ends * inner_share(LOCAL_Z))
    fore_hi, fore_lo = split_np(padded_to(fore, 128, 256))
    back_hi, back_lo = split_np(padded_to(back, 256, 128))
    zf1 = np.concatenate([fore_hi, fore_hi], axis=0)
    zb1 = np.concatenate([back_hi, back_lo], axis=1)

    def square(matrix):
        high, low = split_np(matrix)
        return np.concatenate([np.concatenate([high, low], axis=1)] * 2, axis=0)

    deriv_z = np.kron(np.eye(LOCAL_Z // 8), deriv.T)
    deriv_y = np.kron(np.eye(LOCAL_Y // 8), deriv)
    count_y = LOCAL_Y // 8
    extend = np.zeros((10 * count_y, 40))
    for element in range(count_y):
        for slot in range(10):
            source = 8 * element + slot - 1
            if slot == 0:
                source = 8 * element - 2 if element else 32
            if slot == 9:
                source = 8 * element + 9 if element + 1 < count_y else 33
            extend[10 * element + slot, source] = 1.0
    y_fore = np.kron(np.eye(count_y), basis.T) @ extend
    y_back = np.diag(inner_share(LOCAL_Y)) @ y_pairs() @ np.kron(np.eye(count_y), basis[1:9])
    sums = (
        values[:, None, None]
        + np.tile(values, count_y)[None, :, None]
        + np.tile(values, LOCAL_Z // 8)[None, None, :]
        + SHIFT_MASS
    )
    recip = np.zeros((10 * 40, 256), np.float32)
    recip[:, :160] = (1.0 / sums).reshape(400, 160)
    weights = np.array(GLL_WEIGHTS)
    wyz = np.tile(weights, count_y)[:, None] * np.tile(weights, LOCAL_Z // 8)[None, :]
    steep = np.zeros((24, LOCAL_Z), np.float32)
    steep[0:8, 0:8] = deriv[:, 0] ** 2
    steep[0:8, LOCAL_Z - 8 :] = deriv[:, 7] ** 2
    steep[8:16] = deriv[:, 0:1] ** 2
    steep[16:24] = deriv[:, 7:8] ** 2
    spread = np.zeros((LOCAL_Z // 8, LOCAL_Z), ml_dtypes.bfloat16)
    for element in range(LOCAL_Z // 8):
        spread[element, 8 * element] = 1.0
    return dict(
        yf=left_table(y_fore, 48),
        yb=left_table(y_back, 32),
        yd=left_table(deriv_y, 32),
        ydt=left_table(deriv_y.T, 32),
        zf1=zf1,
        zf2=fore_lo,
        zb1=zb1,
        zd=square(deriv_z),
        zdt=square(deriv_z.T),
        wyz=wyz.astype(np.float32),
        spread=spread,
        steep=steep,
        recip=recip,
    )


TABLE_NAMES = ("yf", "yb", "yd", "ydt", "zf1", "zf2", "zb1", "zd", "zdt", "wyz", "spread", "steep", "recip")


def parity_signs(basis):
    signs = []
    for mode in range(10):
        even = np.abs(basis[:, mode] - basis[::-1, mode]).max()
        odd = np.abs(basis[:, mode] + basis[::-1, mode]).max()
        signs.append(1 if even < odd else -1)
    return signs


def weighted(coefficients, terms):
    total = None
    for coefficient, term in zip(coefficients, terms):
        piece = term * float(coefficient)
        total = piece if total is None else total + piece
    return total


def x_derive(values, matrix):
    sums = [values[i] + values[7 - i] for i in range(4)]
    gaps = [values[i] - values[7 - i] for i in range(4)]
    out = [None] * 8
    for p in range(4):
        first = weighted([(matrix[p, i] + matrix[p, 7 - i]) / 2 for i in range(4)], sums)
        second = weighted([(matrix[p, i] - matrix[p, 7 - i]) / 2 for i in range(4)], gaps)
        out[p] = second + first
        out[7 - p] = second - first
    return out


def x_modes(values, basis, signs):
    sums = [values[i] + values[9 - i] for i in range(5)]
    gaps = [values[i] - values[9 - i] for i in range(5)]
    return [
        weighted([basis[i, mode] for i in range(5)], sums if signs[mode] > 0 else gaps)
        for mode in range(10)
    ]


def x_unmodes(values, basis, signs):
    evens = [mode for mode in range(10) if signs[mode] > 0]
    odds = [mode for mode in range(10) if signs[mode] < 0]
    out = [None] * 8
    for i in range(1, 5):
        first = weighted([basis[i, mode] for mode in evens], [values[mode] for mode in evens])
        second = weighted([basis[i, mode] for mode in odds], [values[mode] for mode in odds])
        out[i - 1] = first + second
        out[8 - i] = first - second
    return out


def dot(first, second):
    return jnp.dot(first, second, preferred_element_type=F32)


def halves(values):
    high = values.astype(BF16)
    return (high, (values - high.astype(F32)).astype(BF16))


def left_mul(table, first, second):
    values = jnp.concatenate([first, second], axis=1)
    high = values.astype(BF16).astype(F32)
    rows = values.shape[0]
    parts = [high, values - high, high]
    if 3 * rows < 128:
        parts.append(jnp.zeros((128 - 3 * rows, values.shape[1]), F32))
    return dot(table, jnp.concatenate(parts, axis=0).astype(BF16))


def right_mul(values, table):
    high, low = halves(values)
    out = dot(jnp.concatenate([high, low], axis=1), table)
    return out[:, :128] + out[:, 128:]


def fold_rows(values):
    return jnp.sum(values.reshape(values.shape[0] // 8, 8, 128), axis=0)


def all_sum(values):
    lanes = jnp.sum(jnp.sum(values, axis=0, keepdims=True), axis=1, keepdims=True)
    return jnp.broadcast_to(lanes, (8, 128))


def times_tile(values, tile):
    return (values.reshape(values.shape[0] // 8, 8, 128) * tile[None]).reshape(values.shape)


def message_rows(direction, layers, extra):
    sx, sy = direction
    rows = 8 * layers if sx and sy else 32 * layers if sx else 16 * layers
    return rows + (8 if extra else 0)


def message_offsets(layers, extra):
    offsets = [0]
    for direction in DIRS:
        offsets.append(offsets[-1] + message_rows(direction, layers, extra))
    return offsets


OUT_NAMES = ("z0", "w", "b", "aw", "p0", "sol", "steps")
ROUNDS = (("rhs", 2, True), ("sol", 1, False), ("sch0", 1, False), ("sti0", 2, False), ("sch1", 1, False), ("sti1", 1, False))


def body(sizes, *refs):
    n_grp, n_low, n_high = sizes
    n_dev = n_low * n_high
    (rhs_h, coef_h, sol_h, dif_h, flags_h, crow_h) = refs[:6]
    refs = refs[6:]
    tab_h = refs[: len(TABLE_NAMES)]
    refs = refs[len(TABLE_NAMES) :]
    outs = dict(zip(OUT_NAMES, refs))
    refs = refs[len(OUT_NAMES) :]
    names = ("rhs", "kc", "kd", "sol", "solraw", "pin", "y1", "u", "v", "x2")
    names += ("s", "z0", "b", "p0", "w", "a1", "ct")
    buf = dict(zip(names, refs))
    refs = refs[len(names) :]
    send_bufs = dict(zip([r[0] for r in ROUNDS], refs[:6]))
    recv_bufs = dict(zip([r[0] for r in ROUNDS], refs[6:12]))
    g_send, g_recv, halo_send_sem, halo_recv_sem, g_send_sem, g_recv_sem = refs[12:18]
    load_sem, store_sem, flags_ref, crow_ref, steps_ref = refs[18:23]
    tab = dict(zip(TABLE_NAMES, refs[23:]))

    grp = lax.axis_index("grp")
    dev = lax.axis_index("dev")
    low = dev & (n_low - 1)
    high = lax.shift_right_logical(dev, n_low.bit_length() - 1)
    x_lo = jnp.where(grp > 0, 1.0, 0.0).astype(F32)
    x_hi = jnp.where(grp < n_grp - 1, 1.0, 0.0).astype(F32)
    y_lo = jnp.where(dev > 0, 1.0, 0.0).astype(F32)
    y_hi = jnp.where(dev < n_dev - 1, 1.0, 0.0).astype(F32)

    def neighbour(direction):
        return ((grp + direction[0]) & (n_grp - 1), (dev + direction[1]) & (n_dev - 1))

    def stage_partner(stage, step):
        if stage == 0:
            return (grp, high * n_low + ((low + step) & (n_low - 1)))
        if stage == 1:
            return (grp, ((high + step) & (n_high - 1)) * n_low + low)
        return ((grp + step) & (n_grp - 1), dev)

    stage_sizes = (n_low, n_high, n_grp)

    def steps_of(stage):
        size = stage_sizes[stage]
        return sorted(range(1, size), key=lambda step: -min(step, size - step))

    barrier = pltpu.get_barrier_semaphore()
    partners = [neighbour(direction) for direction in DIRS]
    for stage in range(3):
        partners += [stage_partner(stage, step) for step in steps_of(stage)]
    for partner in partners:
        pl.semaphore_signal(barrier, inc=1, device_id=partner, device_id_type=MESH_ID)
    loads = {}
    wanted = [("rhs", rhs_h, buf["rhs"]), ("crow", crow_h, crow_ref)]
    wanted += [("sol", sol_h, buf["sol"]), ("kd", dif_h, buf["kd"]), ("flags", flags_h, flags_ref)]
    wanted += [(name, source, tab[name]) for name, source in zip(TABLE_NAMES, tab_h)]
    wanted += [("kc", coef_h, buf["kc"])]
    for at, (name, source, target) in enumerate(wanted):
        loads[name] = pltpu.make_async_copy(source, target, load_sem.at[at])
        loads[name].start()

    row32 = lax.broadcasted_iota(jnp.int32, (32, 128), 0)
    lane32 = lax.broadcasted_iota(jnp.int32, (32, 128), 1)
    keep_z = jnp.where((lane32 > 0) & (lane32 < 127), 1.0, 0.0).astype(F32)
    share_z = jnp.where(((lane32 % 8 == 0) | (lane32 % 8 == 7)) & (lane32 > 0) & (lane32 < 127), 0.5, 1.0).astype(F32)
    lane_up = jnp.where((lane32 % 8 == 7) & (lane32 < 127), 1.0, 0.0).astype(F32)
    lane_down = jnp.where((lane32 % 8 == 0) & (lane32 > 0), 1.0, 0.0).astype(F32)
    row_up = jnp.where((row32 % 8 == 7) & (row32 < 31), 1.0, 0.0).astype(F32)
    row_down = jnp.where((row32 % 8 == 0) & (row32 > 0), 1.0, 0.0).astype(F32)
    edge_y = jnp.where(row32 == 0, y_lo, jnp.where(row32 == 31, y_hi, 1.0)).astype(F32)
    inner_y = jnp.where((row32 % 8 == 0) | (row32 % 8 == 7), 0.5, 1.0).astype(F32)
    face_y = jnp.where((row32 == 0) | (row32 == 31), 0.5, 1.0).astype(F32) * edge_y
    share_y = inner_y * edge_y
    tile_row = lax.broadcasted_iota(jnp.int32, (8, 128), 0)
    tile_lane = lax.broadcasted_iota(jnp.int32, (8, 128), 1)
    tile_index = tile_row * 128 + tile_lane

    def share_x(plane):
        if plane == 0:
            return 0.5 * x_lo
        if plane == 15:
            return 0.5 * x_hi
        return 0.5 if plane in (7, 8) else 1.0

    def x_times(values, factor):
        return values if isinstance(factor, float) and factor == 1.0 else values * factor

    def z_assembled(values):
        return (
            values
            + lane_up * pltpu.roll(values, 127, 1)
            + lane_down * pltpu.roll(values, 1, 1)
        )

    def y_assembled(values):
        return (
            values + row_up * pltpu.roll(values, 31, 0) + row_down * pltpu.roll(values, 1, 0)
        )

    halo_copies = {}

    def exchange(name, src, tile=None):
        at_round = [r[0] for r in ROUNDS].index(name)
        layers, extra = ROUNDS[at_round][1:]
        offsets = message_offsets(layers, extra)
        send, recv = send_bufs[name], recv_bufs[name]
        copies = []
        for at, direction in enumerate(DIRS):
            sx, sy = direction
            base = offsets[at]
            rows = message_rows(direction, layers, False)
            if sx and sy:
                for layer in range(layers):
                    plane = layer if sx < 0 else 16 - layers + layer
                    start = 32 * plane + (0 if sy < 0 else 24)
                    send[base + 8 * layer : base + 8 * layer + 8, :] = src[start : start + 8, :]
            elif sx:
                start = 0 if sx < 0 else 32 * (16 - layers)
                send[base : base + rows, :] = src[start : start + rows, :]
            else:
                for layer in range(layers):
                    row = layer if sy < 0 else 32 - layers + layer
                    send[base + 16 * layer : base + 16 * layer + 16, :] = src[
                        pl.ds(row, 16, stride=32), :
                    ]
            if extra:
                send[base + rows : base + rows + 8, :] = tile
            total = message_rows(direction, layers, extra)
            copy = pltpu.make_async_remote_copy(
                src_ref=send.at[pl.ds(base, total)],
                dst_ref=recv.at[pl.ds(base, total)],
                send_sem=halo_send_sem.at[8 * at_round + at],
                recv_sem=halo_recv_sem.at[8 * at_round + at],
                device_id=neighbour(direction),
                device_id_type=MESH_ID,
            )
            copy.start()
            copies.append(copy)
        halo_copies[name] = copies

    def arrived(name):
        for copy in halo_copies[name]:
            copy.wait_recv()

    def part(name, direction, layer=0):
        at_round = [r[0] for r in ROUNDS].index(name)
        layers, extra = ROUNDS[at_round][1:]
        offsets = message_offsets(layers, extra)
        at = DIRS.index((-direction[0], -direction[1]))
        unit = 8 if direction[0] and direction[1] else 32 if direction[0] else 16
        start = offsets[at] + unit * layer
        return recv_bufs[name][start : start + unit, :]

    def part_row(name, direction, layer, last):
        at_round = [r[0] for r in ROUNDS].index(name)
        layers, extra = ROUNDS[at_round][1:]
        at = DIRS.index((-direction[0], -direction[1]))
        start = message_offsets(layers, extra)[at] + 8 * layer + last
        return recv_bufs[name][start : start + 1, :]

    def add_faces(name, ref, masked):
        def scale(values, first, second):
            if not masked:
                return values
            return values * (first * second if first is not None and second is not None else second if first is None else first)

        ref[0:32, :] += scale(part(name, (-1, 0)), x_lo, None)
        ref[480:512, :] += scale(part(name, (1, 0)), x_hi, None)
        ref[pl.ds(0, 16, stride=32), :] += scale(part(name, (0, -1)), y_lo, None)
        ref[pl.ds(31, 16, stride=32), :] += scale(part(name, (0, 1)), y_hi, None)
        ref[0:1, :] += scale(part_row(name, (-1, -1), 0, 7), x_lo, y_lo)
        ref[31:32, :] += scale(part_row(name, (-1, 1), 0, 0), x_lo, y_hi)
        ref[480:481, :] += scale(part_row(name, (1, -1), 0, 7), x_hi, y_lo)
        ref[511:512, :] += scale(part_row(name, (1, 1), 0, 0), x_hi, y_hi)

    def add_arrived(name, ref):
        arrived(name)
        add_faces(name, ref, False)

    g_copies = []
    g_pending = {}
    reach = n_low + 2

    def g_send_rows(which, stage, values):
        slot = 3 * which + stage
        rows = values.shape[0]
        g_send[8 * slot : 8 * slot + rows, :] = values
        copies = {}
        for step in steps_of(stage):
            at = 7 * slot + step - 1
            copy = pltpu.make_async_remote_copy(
                src_ref=g_send.at[pl.ds(8 * slot, rows)],
                dst_ref=g_recv.at[pl.ds(8 * at, rows)],
                send_sem=g_send_sem.at[at],
                recv_sem=g_recv_sem.at[at],
                device_id=stage_partner(stage, step),
                device_id_type=MESH_ID,
            )
            copy.start()
            copies[step] = copy
        g_copies.extend(copies.values())
        g_pending[slot] = (values, copies)

    def g_rows(which, stage):
        slot = 3 * which + stage
        values, copies = g_pending[slot]
        out = {0: values}
        for step in reversed(steps_of(stage)):
            copies[step].wait_recv()
        for step in steps_of(stage):
            at = 7 * slot + step - 1
            out[step] = g_recv[8 * at : 8 * at + values.shape[0], :]
        return out

    def total_of(rows):
        total = None
        for values in rows.values():
            total = values if total is None else total + values
        return total

    def scalar_spot(start, at):
        return tile_lane == start + at

    def g_start(which, sums, scalars):
        tile = jnp.zeros((8, 128), F32)
        for (dx, dy), value in sums.items():
            tile = jnp.where(tile_lane == reach * (dx + 1) + low + dy + 1, value, tile)
        for at, value in enumerate(scalars):
            tile = jnp.where(scalar_spot(32, at), value, tile)
        g_send_rows(which, 0, tile[0:1])

    lane2 = lax.broadcasted_iota(jnp.int32, (1, 128), 1)

    def g_second(which):
        row = total_of(g_rows(which, 0))

        def moved(part, base):
            inside = (lane2 >= reach * part) & (lane2 < reach * (part + 1))
            shift = (high * n_low + (base - 1 - reach * part) + 256) & 127
            return pltpu.roll(jnp.where(inside, row, 0.0), shift, 1)

        scalars = pltpu.roll(jnp.where(lane2 >= 32, row, 0.0), 32, 1)
        scalars = jnp.where((lane2 >= 64) & (lane2 < 72), scalars, 0.0)
        one = moved(0, 0) + moved(1, 64)
        two = moved(2, 0) + scalars
        g_send_rows(which, 1, jnp.concatenate([one, two], axis=0))

    def g_third(which):
        g_send_rows(which, 2, total_of(g_rows(which, 1)))

    def g_finish(which):
        rows = g_rows(which, 2)
        sides = jnp.zeros((8, 128), F32)
        middle = jnp.zeros((8, 128), F32)
        scalars = None
        for step, values in rows.items():
            source = (grp - step) & (n_grp - 1)
            one = jnp.broadcast_to(values[0:1], (8, 128))
            two = jnp.broadcast_to(values[1:2], (8, 128))
            sides = sides + jnp.where(tile_row == ((source - 1) & (n_grp - 1)), one, 0.0)
            sides = sides + jnp.where(tile_row == ((source + 1) & (n_grp - 1)), two, 0.0)
            middle = middle + jnp.where(tile_row == source, one, 0.0)
            scalars = two if scalars is None else scalars + two
        return (sides + pltpu.roll(middle, 64, 1), scalars)

    def read_scalar(tile, at):
        lanes = jnp.sum(jnp.where(tile_lane == at, tile, 0.0), axis=1, keepdims=True)
        return jnp.broadcast_to(lanes, (8, 128))

    def coarse_sums(ref):
        middle = None
        for plane in range(16):
            piece = x_times(ref[32 * plane : 32 * plane + 32, :], share_x(plane))
            middle = piece if middle is None else middle + piece
        rows = {
            -1: ref[0:32, :] * (0.5 * x_lo),
            0: middle,
            1: ref[480:512, :] * (0.5 * x_hi),
        }
        sums = {}
        for dx in (-1, 0, 1):
            field = rows[dx] * keep_z
            sums[dx, 0] = all_sum(fold_rows(field * share_y))
            sums[dx, -1] = all_sum(field[0:8] * jnp.where(tile_row == 0, 0.5 * y_lo, 0.0))
            sums[dx, 1] = all_sum(field[24:32] * jnp.where(tile_row == 7, 0.5 * y_hi, 0.0))
        return sums

    def mass_kind(one, two):
        if one == "c":
            return two
        return one if two in ("c", one) else None

    def steep_kind(one, two):
        return "d" + one if one == two != "c" else None

    def coarse_energies():
        coef = buf["kc"]
        steep_z, steep_first, steep_last = [tab["steep"][8 * i : 8 * i + 8, :] for i in range(3)]
        planes = [coef[32 * plane : 32 * plane + 32, :] for plane in range(16)]
        along_x = {
            "c": weighted([1.0] * 16, planes),
            "0": planes[0],
            "1": planes[15],
            "d0": weighted(deriv[:, 0] ** 2, planes[:8]),
            "d1": weighted(deriv[:, 7] ** 2, planes[8:]),
        }
        z_mass = keep_z[0:8]

        def reduced(x_kind, y_kind, z_part):
            values = along_x[x_kind]
            if y_kind == "c":
                values = fold_rows(values)
            elif y_kind == "0":
                values = jnp.where(tile_row == 0, values[0:8], 0.0)
            elif y_kind == "1":
                values = jnp.where(tile_row == 7, values[24:32], 0.0)
            elif y_kind == "d0":
                values = values[0:8] * steep_first
            else:
                values = values[24:32] * steep_last
            return all_sum(values * z_part)

        kinds = ("c", "0", "1")
        pieces = {}
        for one in kinds:
            for two in kinds:
                pieces[one, two] = reduced(one, two, steep_z)
        for steep in ("d0", "d1"):
            for kind in kinds:
                pieces[steep, kind] = reduced(steep, kind, z_mass)
                pieces[kind, steep] = reduced(kind, steep, z_mass)
        energies = {}
        for a in kinds:
            for b in kinds:
                for c in kinds:
                    for d in kinds:
                        keys = (
                            (mass_kind(a, c), mass_kind(b, d)),
                            (steep_kind(a, c), mass_kind(b, d)),
                            (mass_kind(a, c), steep_kind(b, d)),
                        )
                        found = [pieces[key] for key in keys if key in pieces]
                        if found:
                            energies[a, b, c, d] = weighted([1.0] * len(found), found)
        return energies

    def coarse_image(energies, values):
        kinds = ("c", "0", "1")
        half_x = (0.5 * x_lo, 0.5 * x_hi)
        half_y = (0.5 * y_lo, 0.5 * y_hi)

        def split(before, own, after, half):
            return {
                "c": own,
                "0": before * half[0] + own * (half[0] - 1.0),
                "1": after * half[1] + own * (half[1] - 1.0),
            }

        def joined(parts, half):
            own = parts["c"] + parts["0"] * (half[0] - 1.0) + parts["1"] * (half[1] - 1.0)
            return (parts["0"] * half[0], own, parts["1"] * half[1])

        by_x = {dy: split(*[values[dx, dy] for dx in (-1, 0, 1)], half_x) for dy in (-1, 0, 1)}
        steps = {a: split(*[by_x[dy][a] for dy in (-1, 0, 1)], half_y) for a in kinds}
        image = {}
        for a in kinds:
            parts = {}
            for b in kinds:
                terms = [
                    energies[a, b, c, d] * steps[c][d]
                    for c in kinds
                    for d in kinds
                    if (a, b, c, d) in energies
                ]
                parts[b] = weighted([1.0] * len(terms), terms)
            image[a] = joined(parts, half_y)
        out = {}
        for at, dy in enumerate((-1, 0, 1)):
            for dx, value in zip((-1, 0, 1), joined({a: image[a][at] for a in kinds}, half_x)):
                out[dx, dy] = value
        return out

    def paired(values, sums):
        total = None
        for key in values:
            piece = values[key] * sums[key]
            total = piece if total is None else total + piece
        return total

    q_scale = 1.0 / math.sqrt(LOCAL_X * LOCAL_Y * LOCAL_Z)

    def coarse_values(tile):
        values = {}
        for dx in (-1, 0, 1):
            for dy in (-1, 0, 1):
                if dx == 0 and dy == 0:
                    row = buf["ct"][...]
                else:
                    layers, extra = ROUNDS[0][1:]
                    at = DIRS.index((-dx, -dy))
                    start = message_offsets(layers, extra)[at] + message_rows((dx, dy), layers, False)
                    row = recv_bufs["rhs"][start : start + 8, :]
                values[dx, dy] = all_sum(row * tile) * q_scale
        return values

    def coarse_patterns(values):
        lines = {}
        for dx in (-1, 0, 1):
            centre = jnp.concatenate([values[dx, 0]] * 4, axis=0)
            first = jnp.concatenate([values[dx, -1]] * 4, axis=0)
            last = jnp.concatenate([values[dx, 1]] * 4, axis=0)
            line = jnp.where(row32 == 0, (centre + first) * (0.5 * y_lo), centre)
            line = jnp.where(row32 == 31, (centre + last) * (0.5 * y_hi), line)
            lines[dx] = line * keep_z
        return (
            (lines[0] + lines[-1]) * (0.5 * x_lo),
            lines[0],
            (lines[0] + lines[1]) * (0.5 * x_hi),
        )

    def build_pin(name, src):
        pin = buf["pin"]
        zero8 = jnp.zeros((8, 128), F32)
        for plane in range(18):
            pin[40 * plane + 32 : 40 * plane + 40, :] = zero8
        for plane in range(16):
            pin[40 * (plane + 1) : 40 * (plane + 1) + 32, :] = src[32 * plane : 32 * plane + 32, :]
        pin[40:72, :] += part(name, (-1, 0), 1)
        pin[640:672, :] += part(name, (1, 0), 0)
        pin[pl.ds(40, 16, stride=40), :] += part(name, (0, -1), 1)
        pin[pl.ds(71, 16, stride=40), :] += part(name, (0, 1), 0)
        pin[pl.ds(72, 16, stride=40), :] = part(name, (0, -1), 0)
        pin[pl.ds(73, 16, stride=40), :] = part(name, (0, 1), 1)
        for at_plane, dx, layer in ((1, -1, 1), (16, 1, 0), (0, -1, 0), (17, 1, 1)):
            base = 40 * at_plane
            if at_plane in (0, 17):
                pin[base : base + 32, :] = part(name, (dx, 0), layer)
            pin[base : base + 1, :] += part_row(name, (dx, -1), layer, 7)
            pin[base + 31 : base + 32, :] += part_row(name, (dx, 1), layer, 0)
            pin[base + 32 : base + 33, :] += part_row(name, (dx, -1), layer, 6)
            pin[base + 33 : base + 34, :] += part_row(name, (dx, 1), layer, 1)

    row40 = lax.broadcasted_iota(jnp.int32, (40, 128), 0)
    edge40 = jnp.where(
        (row40 == 0) | (row40 == 32), y_lo, jnp.where((row40 == 31) | (row40 == 33), y_hi, 1.0)
    ).astype(F32)

    def pin_plane(plane):
        values = buf["pin"][40 * plane : 40 * plane + 40, :] * edge40
        if plane < 2:
            values = values * x_lo
        if plane > 15:
            values = values * x_hi
        return values

    def assembled_own(plane):
        return z_assembled(pin_plane(plane + 1)[0:32]) * keep_z

    basis, _ = fdm_tables()
    signs = parity_signs(basis)
    deriv = derivative_table()
    sources = ([0, 1, 2, 3, 4, 5, 6, 7, 8, 10], [7, 9, 10, 11, 12, 13, 14, 15, 16, 17])

    def schwarz(dst):
        y1, u, v, x2 = buf["y1"], buf["u"], buf["v"], buf["x2"]
        yf, yb = tab["yf"][...], tab["yb"][...]
        for pair in range(9):
            out = left_mul(yf, pin_plane(2 * pair), pin_plane(2 * pair + 1))
            y1[80 * pair : 80 * pair + 40, :] = out[0:40, :128]
            y1[80 * pair + 40 : 80 * pair + 80, :] = out[0:40, 128:]
        for element in range(2):
            for tile in range(5):
                values = [y1[40 * p + 8 * tile : 40 * p + 8 * tile + 8, :] for p in sources[element]]
                for mode, piece in enumerate(x_modes(values, basis, signs)):
                    start = 40 * (10 * element + mode) + 8 * tile
                    u[start : start + 8, :] = piece
        for element in range(2):
            block = u[400 * element : 400 * element + 400, :]
            first, second = halves(block)
            modes = dot(jnp.concatenate([first, second], axis=1), tab["zf1"][...])
            modes = (modes + dot(first, tab["zf2"][...])) * tab["recip"][...]
            first, second = halves(modes)
            back = dot(first, tab["zb1"][...])
            v[400 * element : 400 * element + 400, :] = (
                back[:, :128] + back[:, 128:] + dot(second, tab["zb1"][:, 0:128])
            )
        for tile in range(5):
            outs = []
            for element in range(2):
                starts = [40 * (10 * element + mode) + 8 * tile for mode in range(10)]
                outs += x_unmodes([v[s : s + 8, :] for s in starts], basis, signs)
            shared = (outs[7] + outs[8]) * 0.5
            outs[7] = shared
            outs[8] = shared
            outs[0] = outs[0] * (0.5 * x_lo)
            outs[15] = outs[15] * (0.5 * x_hi)
            for plane in range(16):
                x2[40 * plane + 8 * tile : 40 * plane + 8 * tile + 8, :] = outs[plane]
        for pair in range(8):
            out = left_mul(yb, x2[80 * pair : 80 * pair + 40, :], x2[80 * pair + 40 : 80 * pair + 80, :])
            dst[64 * pair : 64 * pair + 32, :] = out[:, :128] * face_y
            dst[64 * pair + 32 : 64 * pair + 64, :] = out[:, 128:] * face_y

    def stiff(src, coef, dst, extra=None):
        energy = jnp.zeros((8, 128), F32)
        for chunk in range(2):
            at = slice(256 * chunk, 256 * chunk + 256)
            grad = right_mul(src[at, :], tab["zd"][...])
            flow = grad * coef[at, :]
            energy = energy + fold_rows(grad * flow)
            dst[at, :] = right_mul(flow, tab["zdt"][...])
        for pair in range(8):
            one = slice(64 * pair, 64 * pair + 32)
            two = slice(64 * pair + 32, 64 * pair + 64)
            grad = left_mul(tab["yd"][...], src[one, :], src[two, :])
            flow_one = grad[:, :128] * coef[one, :]
            flow_two = grad[:, 128:] * coef[two, :]
            energy = energy + fold_rows(grad[:, :128] * flow_one) + fold_rows(grad[:, 128:] * flow_two)
            back = left_mul(tab["ydt"][...], flow_one, flow_two)
            dst[one, :] += back[:, :128]
            dst[two, :] += back[:, 128:]
        for tile in range(4):
            sums = []
            for element in range(2):
                starts = [32 * (8 * element + i) + 8 * tile for i in range(8)]
                grads = x_derive([src[s : s + 8, :] for s in starts], deriv)
                flows = [grad * coef[s : s + 8, :] for grad, s in zip(grads, starts)]
                for grad, flow in zip(grads, flows):
                    energy = energy + grad * flow
                backs = x_derive(flows, deriv.T)
                for s, back in zip(starts, backs):
                    value = dst[s : s + 8, :] + back
                    if extra is not None:
                        value = value + extra[s : s + 8, :]
                    sums.append(value)
            shared = sums[7] + sums[8]
            sums[7] = shared
            sums[8] = shared
            for plane in range(16):
                dst[32 * plane + 8 * tile : 32 * plane + 8 * tile + 8, :] = sums[plane]
        for plane in range(16):
            at = slice(32 * plane, 32 * plane + 32)
            dst[at, :] = y_assembled(dst[at, :])
        return energy

    weights = GLL_WEIGHTS + GLL_WEIGHTS

    loads["rhs"].wait()
    loads["crow"].wait()
    for plane in range(16):
        at = slice(32 * plane, 32 * plane + 32)
        values = buf["rhs"][at, :]
        if plane == 7:
            values = values + buf["rhs"][256:288, :]
        if plane == 8:
            values = values + buf["rhs"][224:256, :]
        buf["s"][at, :] = y_assembled(values)
    ct = buf["ct"]
    ct[...] = jnp.zeros((8, 128), F32)
    count = n_grp * n_dev
    for at in range(n_grp):
        start = n_dev * at
        if count >= 128:
            row = crow_ref[:, start // 128 * 128 : start // 128 * 128 + 128]
        else:
            row = jnp.concatenate([crow_ref[...], jnp.zeros((1, 128 - count), F32)], axis=1)
        if start % 128:
            row = pltpu.roll(row, 128 - start % 128, 1)
        ct[at : at + 1, :] = jnp.where(lane2 < n_dev, row, 0.0)
    right_sums = coarse_sums(buf["s"])

    pl.semaphore_wait(barrier, len(partners))
    g_start(0, right_sums, [])
    exchange("rhs", buf["s"], ct[...])

    for name in ("sol", "kd", "flags", "wyz", "spread", "zd", "zdt", "yd", "ydt"):
        loads[name].wait()
    wyz = tab["wyz"][...]
    flags = jnp.concatenate([flags_ref[0], flags_ref[1]], axis=0).astype(F32).astype(BF16)
    flag_rows = dot(flags, tab["spread"][...])
    weight_column = GLL_WEIGHTS
    row8 = tile_row
    w_rows = jnp.zeros((8, 128), F32)
    for at, weight in enumerate(weight_column):
        w_rows = jnp.where(row8 == at, weight, w_rows)
    for plane in range(16):
        at = slice(32 * plane, 32 * plane + 32)
        buf["kd"][at, :] = buf["kd"][at, :] * (wyz * weights[plane])
        flux = jnp.concatenate(
            [
                flag_rows[4 * (plane // 8) + ey : 4 * (plane // 8) + ey + 1, :] * w_rows
                for ey in range(4)
            ],
            axis=0,
        )
        factor = wyz * (MASS_RATE * weights[plane]) + flux * (GROWTH * SEGREGATION * weights[plane])
        buf["x2"][at, :] = buf["sol"][at, :] * factor
    stiff(buf["sol"], buf["kd"], buf["solraw"], extra=buf["x2"])

    exchange("sol", buf["solraw"])
    for name in ("kc", "steep", "yf", "yb", "zf1", "zf2", "zb1", "recip"):
        loads[name].wait()
    for plane in range(16):
        at = slice(32 * plane, 32 * plane + 32)
        buf["kc"][at, :] = buf["kc"][at, :] * (wyz * weights[plane])
    energies = coarse_energies()

    stores = []

    def store(name, ref):
        copy = pltpu.make_async_copy(ref, outs[name], store_sem.at[OUT_NAMES.index(name)])
        copy.start()
        stores.append(copy)

    g_second(0)
    arrived("rhs")
    build_pin("rhs", buf["s"])
    schwarz(buf["z0"])
    exchange("sch0", buf["z0"])
    g_third(0)
    for plane in range(16):
        buf["b"][32 * plane : 32 * plane + 32, :] = assembled_own(plane)
    share_yz = share_y * share_z

    def product_of(first, second):
        tile = jnp.zeros((8, 128), F32)
        for plane in range(16):
            at = slice(32 * plane, 32 * plane + 32)
            piece = x_times(first[at, :] * second[at, :] * share_yz, share_x(plane))
            tile = tile + fold_rows(piece)
        return all_sum(tile)

    def add_coarse(ref, values):
        patterns = coarse_patterns(values)
        for plane in range(16):
            at = slice(32 * plane, 32 * plane + 32)
            ref[at, :] += patterns[0 if plane == 0 else 2 if plane == 15 else 1]

    add_arrived("sch0", buf["z0"])
    curve = all_sum(stiff(buf["z0"], buf["kc"], buf["a1"]))
    sums = coarse_sums(buf["a1"])
    rz = product_of(buf["b"], buf["z0"])
    total, _ = g_finish(0)
    coarse = coarse_values(total)
    image = coarse_image(energies, coarse)
    applied_sums = {key: sums[key] + image[key] for key in sums}
    rz = rz + paired(coarse, right_sums)
    curve = curve + paired(coarse, {key: sums[key] + applied_sums[key] for key in sums})
    g_start(1, applied_sums, [rz, curve])
    add_coarse(buf["z0"], coarse)
    stiff(buf["z0"], buf["kc"], buf["a1"])
    exchange("sti0", buf["a1"])

    arrived("sol")
    add_faces("sol", buf["solraw"], True)
    for plane in range(16):
        at = slice(32 * plane, 32 * plane + 32)
        buf["solraw"][at, :] = z_assembled(buf["solraw"][at, :])
    store("sol", buf["solraw"])

    g_second(1)
    arrived("sti0")
    build_pin("sti0", buf["a1"])
    schwarz(buf["w"])
    exchange("sch1", buf["w"])
    g_third(1)
    for plane in range(16):
        buf["p0"][32 * plane : 32 * plane + 32, :] = assembled_own(plane)
    add_arrived("sch1", buf["w"])
    w_curve = all_sum(stiff(buf["w"], buf["kc"], buf["rhs"]))
    sums = coarse_sums(buf["rhs"])
    b_w = product_of(buf["b"], buf["w"])
    p_w = product_of(buf["p0"], buf["w"])
    total, scalars = g_finish(1)
    coarse = coarse_values(total)
    image = coarse_image(energies, coarse)
    b_w = b_w + paired(coarse, right_sums)
    p_w = p_w + paired(coarse, applied_sums)
    w_curve = w_curve + paired(coarse, {key: 2.0 * sums[key] + image[key] for key in sums})
    tile = jnp.zeros((8, 128), F32)
    for at, value in enumerate((b_w, p_w, w_curve)):
        tile = jnp.where(tile_lane == at, value, tile)
    g_send_rows(2, 0, tile[0:1])
    rz0 = read_scalar(scalars, 64)
    curve0 = read_scalar(scalars, 65)
    alpha0 = rz0 / curve0
    add_coarse(buf["w"], coarse)
    stiff(buf["w"], buf["kc"], buf["rhs"])
    exchange("sti1", buf["rhs"])
    for name in ("z0", "w", "b", "p0"):
        store(name, buf[name])
    g_send_rows(2, 1, total_of(g_rows(2, 0)))
    add_arrived("sti1", buf["rhs"])
    g_send_rows(2, 2, total_of(g_rows(2, 1)))
    for plane in range(16):
        at = slice(32 * plane, 32 * plane + 32)
        values = z_assembled(buf["rhs"][at, :]) * keep_z * edge_y
        if plane == 0:
            values = values * x_lo
        if plane == 15:
            values = values * x_hi
        buf["rhs"][at, :] = values
    store("aw", buf["rhs"])
    total = jnp.broadcast_to(total_of(g_rows(2, 2)), (8, 128))
    b_w, p_w, w_curve = [read_scalar(total, at) for at in range(3)]
    rz1 = alpha0 * (alpha0 * p_w - b_w)
    cross1 = curve0 - alpha0 * p_w
    curve1 = cross1 - alpha0 * (p_w - alpha0 * w_curve)
    beta = rz1 / rz0
    alpha1 = rz1 / (curve1 + beta * (2.0 * cross1 + beta * curve0))
    steps_ref[0:8, :] = alpha0 + alpha1 * (1.0 + beta)
    steps_ref[8:16, :] = alpha0 * alpha1
    store("steps", steps_ref)
    for name in halo_copies:
        for copy in halo_copies[name]:
            copy.wait_send()
    for copy in g_copies:
        copy.wait_send()
    for copy in stores:
        copy.wait()


def finish_body(*refs):
    count = len(OUT_NAMES)
    sources, targets, bufs, load_sem, store_sem = refs[:count], refs[count : count + 3], refs[count + 3 : 2 * count + 3], refs[-2], refs[-1]
    loads = {}
    for at in (6, 0, 1, 2, 3, 4, 5):
        loads[OUT_NAMES[at]] = pltpu.make_async_copy(sources[at], bufs[at], load_sem.at[at])
        loads[OUT_NAMES[at]].start()
    z0, w, b, aw, p0, sol, steps = bufs
    for name in ("steps", "z0", "w"):
        loads[name].wait()
    first, second = steps[0:8, :], steps[8:16, :]
    for plane in range(LOCAL_X):
        at = slice(32 * plane, 32 * plane + 32)
        z0[at, :] = times_tile(z0[at, :], first) - times_tile(w[at, :], second)
    stores = [pltpu.make_async_copy(z0, targets[0], store_sem.at[0])]
    stores[0].start()
    for name in ("b", "aw", "p0"):
        loads[name].wait()
    for plane in range(LOCAL_X):
        at = slice(32 * plane, 32 * plane + 32)
        b[at, :] = b[at, :] - times_tile(p0[at, :], first) + times_tile(aw[at, :], second)
    stores.append(pltpu.make_async_copy(b, targets[1], store_sem.at[1]))
    stores[1].start()
    loads["sol"].wait()
    stores.append(pltpu.make_async_copy(sol, targets[2], store_sem.at[2]))
    stores[2].start()
    for copy in stores:
        copy.wait()


def finish(fields):
    far = pl.BlockSpec(memory_space=pltpu.HBM)
    return pl.pallas_call(
        finish_body,
        out_shape=[jax.ShapeDtypeStruct((ROWS, LOCAL_Z), F32)] * 3,
        in_specs=[far] * len(OUT_NAMES),
        out_specs=[far] * 3,
        scratch_shapes=[pltpu.VMEM(v.shape, F32) for v in fields]
        + [pltpu.SemaphoreType.DMA((len(OUT_NAMES),)), pltpu.SemaphoreType.DMA((3,))],
        compiler_params=pltpu.CompilerParams(vmem_limit_bytes=63 * 1024 * 1024),
    )(*fields)


def run_kernel(sizes, fields, flags, coarse_row, tables):
    constants = [jnp.asarray(tables[name]) for name in TABLE_NAMES]
    far = pl.BlockSpec(memory_space=pltpu.HBM)
    field = pltpu.VMEM((ROWS, LOCAL_Z), F32)

    def rows(count):
        return pltpu.VMEM((count, LOCAL_Z), F32)

    halo = [rows(message_offsets(layers, extra)[-1]) for _, layers, extra in ROUNDS]
    scratch = (
        [field] * 5
        + [rows(720), rows(720), rows(800), rows(800), rows(640)]
        + [field] * 6
        + [rows(8)]
        + halo
        + halo
        + [rows(72), rows(8 * 63)]
        + [pltpu.SemaphoreType.DMA((count,)) for count in (48, 48, 63, 63, 6 + len(constants), len(OUT_NAMES))]
        + [pltpu.VMEM(flags.shape, jnp.int32), pltpu.VMEM(coarse_row.shape, F32), rows(16)]
        + [pltpu.VMEM(table.shape, table.dtype) for table in constants]
    )
    return pl.pallas_call(
        functools.partial(body, sizes),
        out_shape=[
            jax.ShapeDtypeStruct((16 if name == "steps" else ROWS, LOCAL_Z), F32) for name in OUT_NAMES
        ],
        in_specs=[far] * (6 + len(constants)),
        out_specs=[far] * len(OUT_NAMES),
        scratch_shapes=scratch,
        compiler_params=pltpu.CompilerParams(
            collective_id=0, has_side_effects=True, vmem_limit_bytes=63 * 1024 * 1024
        ),
    )(*fields, flags, coarse_row, *constants)


def solution(mesh):
    n_grp, n_dev = (mesh.shape["grp"], mesh.shape["dev"])
    n_low = 8 if n_dev % 8 == 0 else 2
    sizes = (n_grp, n_low, n_dev // n_low)
    tables = make_tables()

    def shards(right_side, coefficient, solute, diffusivity, interface_flags, coarse_inverse):
        fields = [v.reshape(ROWS, LOCAL_Z) for v in (right_side, coefficient, solute, diffusivity)]
        outs = run_kernel(sizes, fields, interface_flags, coarse_inverse, tables)
        return tuple(v.reshape(LOCAL_X, LOCAL_Y, LOCAL_Z) for v in finish(outs))

    placed = (
        P("grp", "dev", None),
        P("grp", "dev", None),
        P("grp", "dev", None),
        P("grp", "dev", None),
        P("grp", "dev", None),
        P(("grp", "dev"), None),
    )
    return jax.shard_map(
        shards,
        mesh=mesh,
        in_specs=placed,
        out_specs=(P("grp", "dev", None), P("grp", "dev", None), P("grp", "dev", None)),
        check_vma=False,
    )
```

```python
import functools
import math

import jax
import jax.numpy as jnp
import ml_dtypes
import numpy as np
from jax import lax
from jax.experimental import pallas as pl
from jax.experimental.pallas import tpu as pltpu
from jax.sharding import PartitionSpec as P

GLL_POINTS = [
    -1.0,
    -0.8717401485096066,
    -0.5917001814331423,
    -0.2092992179024789,
    0.2092992179024789,
    0.5917001814331423,
    0.8717401485096066,
    1.0,
]
GLL_WEIGHTS = [
    0.0357142857142857,
    0.2107042271435061,
    0.3411226924835044,
    0.4124587946587038,
    0.4124587946587038,
    0.3411226924835044,
    0.2107042271435061,
    0.0357142857142857,
]
SHIFT_MASS = 0.5
MASS_RATE = 2.0
GROWTH = 40.0
SEGREGATION = 0.7


def derivative_table():
    products = []
    for row_at in range(8):
        value = 1.0
        for other in range(8):
            if other != row_at:
                value = value * (GLL_POINTS[row_at] - GLL_POINTS[other])
        products.append(value)
    table = [[0.0] * 8 for row_at in range(8)]
    for row_at in range(8):
        total = 0.0
        for other in range(8):
            if other != row_at:
                entry = (
                    products[row_at] / products[other] / (GLL_POINTS[row_at] - GLL_POINTS[other])
                )
                table[row_at][other] = entry
                total = total + entry
        table[row_at][row_at] = -total
    return np.array(table)


def margin_matrices():
    deriv_np = derivative_table()
    spacing = GLL_POINTS[1] - GLL_POINTS[0]
    stiffness = [[0.0] * 10 for row_at in range(10)]
    masses = [0.0] * 10
    for row_at in range(8):
        masses[row_at + 1] = GLL_WEIGHTS[row_at]
        for other in range(8):
            total = 0.0
            for point in range(8):
                total = (
                    total + deriv_np[point, row_at] * GLL_WEIGHTS[point] * deriv_np[point, other]
                )
            stiffness[row_at + 1][other + 1] = total
    for outer_end, inner_end in ((0, 1), (9, 8)):
        stiffness[outer_end][outer_end] += 1.0 / spacing
        stiffness[inner_end][inner_end] += 1.0 / spacing
        stiffness[outer_end][inner_end] -= 1.0 / spacing
        stiffness[inner_end][outer_end] -= 1.0 / spacing
        masses[outer_end] += 0.5 * spacing
        masses[inner_end] += 0.5 * spacing
    return (stiffness, masses)


def jacobi_eigen(matrix_rows):
    count_in = len(matrix_rows)
    work = [list(row_now) for row_now in matrix_rows]
    vectors = [
        [1.0 if other == row_at else 0.0 for other in range(count_in)] for row_at in range(count_in)
    ]
    for sweep in range(15):
        for first in range(count_in):
            for second in range(first + 1, count_in):
                entry = work[first][second]
                if entry != 0.0:
                    theta = (work[second][second] - work[first][first]) / (2.0 * entry)
                    sign_now = 1.0 if theta >= 0.0 else -1.0
                    tangent = sign_now / (abs(theta) + math.sqrt(theta * theta + 1.0))
                    cosine = 1.0 / math.sqrt(tangent * tangent + 1.0)
                    sine = tangent * cosine
                    for index in range(count_in):
                        left_val = work[index][first]
                        right_val = work[index][second]
                        work[index][first] = cosine * left_val - sine * right_val
                        work[index][second] = sine * left_val + cosine * right_val
                    for index in range(count_in):
                        left_val = work[first][index]
                        right_val = work[second][index]
                        work[first][index] = cosine * left_val - sine * right_val
                        work[second][index] = sine * left_val + cosine * right_val
                    for index in range(count_in):
                        left_val = vectors[index][first]
                        right_val = vectors[index][second]
                        vectors[index][first] = cosine * left_val - sine * right_val
                        vectors[index][second] = sine * left_val + cosine * right_val
    return ([work[index][index] for index in range(10 if count_in == 10 else count_in)], vectors)


def fdm_tables():
    stiffness, masses = margin_matrices()
    scaled = [
        [
            stiffness[row_at][other] / math.sqrt(masses[row_at] * masses[other])
            for other in range(10)
        ]
        for row_at in range(10)
    ]
    values, vectors = jacobi_eigen(scaled)
    basis = np.array(
        [
            [vectors[row_at][other] / math.sqrt(masses[row_at]) for other in range(10)]
            for row_at in range(10)
        ]
    )
    return (basis, np.array(values))


def z_forward_table(elements):
    basis, values = fdm_tables()
    extend_np = np.zeros((8 * elements, 10 * elements))
    for element in range(elements):
        for slot_in in range(10):
            source = 8 * element + slot_in - 1
            if slot_in == 0:
                source = 8 * element - 2
            if slot_in == 9:
                source = 8 * element + 9
            if 0 <= source < 8 * elements:
                extend_np[source, 10 * element + slot_in] = 1.0
    return extend_np @ np.kron(np.eye(elements), basis)


def z_backward_table(elements):
    basis, values = fdm_tables()
    return np.kron(np.eye(elements), basis[1:9].T)


def z_derivative(elements):
    return np.kron(np.eye(elements), derivative_table().T)


def z_pairs(elements):
    pairs_np = np.eye(8 * elements)
    for element in range(elements - 1):
        pairs_np[8 * element + 7, 8 * element + 8] = 1.0
        pairs_np[8 * element + 8, 8 * element + 7] = 1.0
    return pairs_np


LOCAL_X, LOCAL_Y, LOCAL_Z = (16, 32, 128)
ROWS = LOCAL_X * LOCAL_Y
DIRS = ((-1, -1), (-1, 1), (1, -1), (1, 1), (0, -1), (0, 1), (-1, 0), (1, 0))
F32 = jnp.float32
BF16 = jnp.bfloat16
MESH_ID = pl.DeviceIdType.MESH


def split_np(table):
    high = np.asarray(table, np.float32).astype(ml_dtypes.bfloat16)
    low = (np.asarray(table, np.float64) - high.astype(np.float64)).astype(ml_dtypes.bfloat16)
    return (high, low)


def left_table(matrix, rows):
    high, low = split_np(matrix)
    joined = np.concatenate([high, high, low], axis=1)
    out = np.zeros((rows, 128), ml_dtypes.bfloat16)
    out[: joined.shape[0], : joined.shape[1]] = joined
    return out


def y_pairs():
    pairs = np.eye(LOCAL_Y)
    for element in range(LOCAL_Y // 8 - 1):
        pairs[8 * element + 7, 8 * element + 8] = 1.0
        pairs[8 * element + 8, 8 * element + 7] = 1.0
    return pairs


def inner_share(count_in):
    share = np.ones(count_in)
    for position in range(count_in):
        if position % 8 in (0, 7) and position not in (0, count_in - 1):
            share[position] = 0.5
    return share


def padded_to(matrix, rows, columns):
    out = np.zeros((rows, columns))
    out[: matrix.shape[0], : matrix.shape[1]] = matrix
    return out


def make_tables():
    basis, values = fdm_tables()
    deriv = derivative_table()
    ends = np.ones(LOCAL_Z)
    ends[0] = 0.0
    ends[-1] = 0.0
    pairs_z = z_pairs(LOCAL_Z // 8)
    fore = pairs_z @ np.diag(ends) @ z_forward_table(LOCAL_Z // 8)
    back = z_backward_table(LOCAL_Z // 8) @ pairs_z @ np.diag(ends * inner_share(LOCAL_Z))
    fore_hi, fore_lo = split_np(padded_to(fore, 128, 256))
    back_hi, back_lo = split_np(padded_to(back, 256, 128))
    zf1 = np.concatenate([fore_hi, fore_hi], axis=0)
    zb1 = np.concatenate([back_hi, back_lo], axis=1)

    def square(matrix):
        high, low = split_np(matrix)
        return np.concatenate([np.concatenate([high, low], axis=1)] * 2, axis=0)

    deriv_z = np.kron(np.eye(LOCAL_Z // 8), deriv.T)
    deriv_y = np.kron(np.eye(LOCAL_Y // 8), deriv)
    count_y = LOCAL_Y // 8
    extend = np.zeros((10 * count_y, 40))
    for element in range(count_y):
        for slot in range(10):
            source = 8 * element + slot - 1
            if slot == 0:
                source = 8 * element - 2 if element else 32
            if slot == 9:
                source = 8 * element + 9 if element + 1 < count_y else 33
            extend[10 * element + slot, source] = 1.0
    y_fore = np.kron(np.eye(count_y), basis.T) @ extend
    y_back = np.diag(inner_share(LOCAL_Y)) @ y_pairs() @ np.kron(np.eye(count_y), basis[1:9])
    sums = (
        values[:, None, None]
        + np.tile(values, count_y)[None, :, None]
        + np.tile(values, LOCAL_Z // 8)[None, None, :]
        + SHIFT_MASS
    )
    recip = np.zeros((10 * 40, 256), np.float32)
    recip[:, :160] = (1.0 / sums).reshape(400, 160)
    weights = np.array(GLL_WEIGHTS)
    wyz = np.tile(weights, count_y)[:, None] * np.tile(weights, LOCAL_Z // 8)[None, :]
    steep = np.zeros((24, LOCAL_Z), np.float32)
    steep[0:8, 0:8] = deriv[:, 0] ** 2
    steep[0:8, LOCAL_Z - 8 :] = deriv[:, 7] ** 2
    steep[8:16] = deriv[:, 0:1] ** 2
    steep[16:24] = deriv[:, 7:8] ** 2
    spread = np.zeros((LOCAL_Z // 8, LOCAL_Z), ml_dtypes.bfloat16)
    for element in range(LOCAL_Z // 8):
        spread[element, 8 * element] = 1.0
    return dict(
        yf=left_table(y_fore, 48),
        yb=left_table(y_back, 32),
        yd=left_table(deriv_y, 32),
        ydt=left_table(deriv_y.T, 32),
        zf1=zf1,
        zf2=fore_lo,
        zb1=zb1,
        zd=square(deriv_z),
        zdt=square(deriv_z.T),
        wyz=wyz.astype(np.float32),
        spread=spread,
        steep=steep,
        recip=recip,
    )


TABLE_NAMES = ("yf", "yb", "yd", "ydt", "zf1", "zf2", "zb1", "zd", "zdt", "wyz", "spread", "steep", "recip")


def parity_signs(basis):
    signs = []
    for mode in range(10):
        even = np.abs(basis[:, mode] - basis[::-1, mode]).max()
        odd = np.abs(basis[:, mode] + basis[::-1, mode]).max()
        signs.append(1 if even < odd else -1)
    return signs


def weighted(coefficients, terms):
    total = None
    for coefficient, term in zip(coefficients, terms):
        piece = term * float(coefficient)
        total = piece if total is None else total + piece
    return total


def x_derive(values, matrix):
    sums = [values[i] + values[7 - i] for i in range(4)]
    gaps = [values[i] - values[7 - i] for i in range(4)]
    out = [None] * 8
    for p in range(4):
        first = weighted([(matrix[p, i] + matrix[p, 7 - i]) / 2 for i in range(4)], sums)
        second = weighted([(matrix[p, i] - matrix[p, 7 - i]) / 2 for i in range(4)], gaps)
        out[p] = second + first
        out[7 - p] = second - first
    return out


def x_modes(values, basis, signs):
    sums = [values[i] + values[9 - i] for i in range(5)]
    gaps = [values[i] - values[9 - i] for i in range(5)]
    return [
        weighted([basis[i, mode] for i in range(5)], sums if signs[mode] > 0 else gaps)
        for mode in range(10)
    ]


def x_unmodes(values, basis, signs):
    evens = [mode for mode in range(10) if signs[mode] > 0]
    odds = [mode for mode in range(10) if signs[mode] < 0]
    out = [None] * 8
    for i in range(1, 5):
        first = weighted([basis[i, mode] for mode in evens], [values[mode] for mode in evens])
        second = weighted([basis[i, mode] for mode in odds], [values[mode] for mode in odds])
        out[i - 1] = first + second
        out[8 - i] = first - second
    return out


def dot(first, second):
    return jnp.dot(first, second, preferred_element_type=F32)


def halves(values):
    high = values.astype(BF16)
    return (high, (values - high.astype(F32)).astype(BF16))


def left_mul(table, first, second):
    values = jnp.concatenate([first, second], axis=1)
    high = values.astype(BF16).astype(F32)
    rows = values.shape[0]
    parts = [high, values - high, high]
    if 3 * rows < 128:
        parts.append(jnp.zeros((128 - 3 * rows, values.shape[1]), F32))
    return dot(table, jnp.concatenate(parts, axis=0).astype(BF16))


def right_mul(values, table):
    high, low = halves(values)
    out = dot(jnp.concatenate([high, low], axis=1), table)
    return out[:, :128] + out[:, 128:]


def fold_rows(values):
    return jnp.sum(values.reshape(values.shape[0] // 8, 8, 128), axis=0)


def all_sum(values):
    lanes = jnp.sum(jnp.sum(values, axis=0, keepdims=True), axis=1, keepdims=True)
    return jnp.broadcast_to(lanes, (8, 128))


def times_tile(values, tile):
    return (values.reshape(values.shape[0] // 8, 8, 128) * tile[None]).reshape(values.shape)


def message_rows(direction, layers, extra):
    sx, sy = direction
    rows = 8 * layers if sx and sy else 32 * layers if sx else 16 * layers
    return rows + (8 if extra else 0)


def message_offsets(layers, extra):
    offsets = [0]
    for direction in DIRS:
        offsets.append(offsets[-1] + message_rows(direction, layers, extra))
    return offsets


OUT_NAMES = ("z0", "w", "b", "aw", "p0", "sol", "steps")
ROUNDS = (("rhs", 2, True), ("sol", 1, False), ("sch0", 1, False), ("sti0", 2, False), ("sch1", 1, False), ("sti1", 1, False))


def body(sizes, *refs):
    n_grp, n_low, n_high = sizes
    n_dev = n_low * n_high
    (rhs_h, coef_h, sol_h, dif_h, flags_h, crow_h) = refs[:6]
    refs = refs[6:]
    tab_h = refs[: len(TABLE_NAMES)]
    refs = refs[len(TABLE_NAMES) :]
    outs = dict(zip(OUT_NAMES, refs))
    refs = refs[len(OUT_NAMES) :]
    names = ("rhs", "kc", "kd", "sol", "solraw", "pin", "y1", "u", "v", "x2")
    names += ("s", "z0", "b", "p0", "w", "a1", "ct")
    buf = dict(zip(names, refs))
    refs = refs[len(names) :]
    send_bufs = dict(zip([r[0] for r in ROUNDS], refs[:6]))
    recv_bufs = dict(zip([r[0] for r in ROUNDS], refs[6:12]))
    g_send, g_recv, halo_send_sem, halo_recv_sem, g_send_sem, g_recv_sem = refs[12:18]
    load_sem, store_sem, flags_ref, crow_ref, steps_ref = refs[18:23]
    tab = dict(zip(TABLE_NAMES, refs[23:]))

    grp = lax.axis_index("grp")
    dev = lax.axis_index("dev")
    low = dev & (n_low - 1)
    high = lax.shift_right_logical(dev, n_low.bit_length() - 1)
    x_lo = jnp.where(grp > 0, 1.0, 0.0).astype(F32)
    x_hi = jnp.where(grp < n_grp - 1, 1.0, 0.0).astype(F32)
    y_lo = jnp.where(dev > 0, 1.0, 0.0).astype(F32)
    y_hi = jnp.where(dev < n_dev - 1, 1.0, 0.0).astype(F32)

    def neighbour(direction):
        return ((grp + direction[0]) & (n_grp - 1), (dev + direction[1]) & (n_dev - 1))

    def stage_partner(stage, step):
        if stage == 0:
            return (grp, high * n_low + ((low + step) & (n_low - 1)))
        if stage == 1:
            return (grp, ((high + step) & (n_high - 1)) * n_low + low)
        return ((grp + step) & (n_grp - 1), dev)

    stage_sizes = (n_low, n_high, n_grp)

    def steps_of(stage):
        size = stage_sizes[stage]
        return sorted(range(1, size), key=lambda step: -min(step, size - step))

    loads = {}
    wanted = [("rhs", rhs_h, buf["rhs"]), ("crow", crow_h, crow_ref)]
    wanted += [("sol", sol_h, buf["sol"]), ("kd", dif_h, buf["kd"]), ("flags", flags_h, flags_ref)]
    wanted += [(name, source, tab[name]) for name, source in zip(TABLE_NAMES, tab_h)]
    wanted += [("kc", coef_h, buf["kc"])]
    for at, (name, source, target) in enumerate(wanted):
        loads[name] = pltpu.make_async_copy(source, target, load_sem.at[at])
    for name in ("rhs", "crow"):
        loads[name].start()
    barrier = pltpu.get_barrier_semaphore()
    far = [(-min(step, stage_sizes[stage] - step), stage, step) for stage in (2, 1) for step in steps_of(stage)]
    partners = [stage_partner(stage, step) for _, stage, step in sorted(far)]
    partners += [neighbour(direction) for direction in DIRS]
    partners += [stage_partner(0, step) for step in steps_of(0)]
    for partner in partners:
        pl.semaphore_signal(barrier, inc=1, device_id=partner, device_id_type=MESH_ID)
    for name, _, _ in wanted[2:]:
        loads[name].start()

    row32 = lax.broadcasted_iota(jnp.int32, (32, 128), 0)
    lane32 = lax.broadcasted_iota(jnp.int32, (32, 128), 1)
    keep_z = jnp.where((lane32 > 0) & (lane32 < 127), 1.0, 0.0).astype(F32)
    share_z = jnp.where(((lane32 % 8 == 0) | (lane32 % 8 == 7)) & (lane32 > 0) & (lane32 < 127), 0.5, 1.0).astype(F32)
    lane_up = jnp.where((lane32 % 8 == 7) & (lane32 < 127), 1.0, 0.0).astype(F32)
    lane_down = jnp.where((lane32 % 8 == 0) & (lane32 > 0), 1.0, 0.0).astype(F32)
    row_up = jnp.where((row32 % 8 == 7) & (row32 < 31), 1.0, 0.0).astype(F32)
    row_down = jnp.where((row32 % 8 == 0) & (row32 > 0), 1.0, 0.0).astype(F32)
    edge_y = jnp.where(row32 == 0, y_lo, jnp.where(row32 == 31, y_hi, 1.0)).astype(F32)
    inner_y = jnp.where((row32 % 8 == 0) | (row32 % 8 == 7), 0.5, 1.0).astype(F32)
    face_y = jnp.where((row32 == 0) | (row32 == 31), 0.5, 1.0).astype(F32) * edge_y
    share_y = inner_y * edge_y
    tile_row = lax.broadcasted_iota(jnp.int32, (8, 128), 0)
    tile_lane = lax.broadcasted_iota(jnp.int32, (8, 128), 1)
    tile_index = tile_row * 128 + tile_lane

    def share_x(plane):
        if plane == 0:
            return 0.5 * x_lo
        if plane == 15:
            return 0.5 * x_hi
        return 0.5 if plane in (7, 8) else 1.0

    def x_times(values, factor):
        return values if isinstance(factor, float) and factor == 1.0 else values * factor

    def z_assembled(values):
        return (
            values
            + lane_up * pltpu.roll(values, 127, 1)
            + lane_down * pltpu.roll(values, 1, 1)
        )

    def y_assembled(values):
        return (
            values + row_up * pltpu.roll(values, 31, 0) + row_down * pltpu.roll(values, 1, 0)
        )

    halo_copies = {}

    def exchange(name, src, tile=None):
        at_round = [r[0] for r in ROUNDS].index(name)
        layers, extra = ROUNDS[at_round][1:]
        offsets = message_offsets(layers, extra)
        send, recv = send_bufs[name], recv_bufs[name]
        copies = []
        for at, direction in enumerate(DIRS):
            sx, sy = direction
            base = offsets[at]
            rows = message_rows(direction, layers, False)
            if sx and sy:
                for layer in range(layers):
                    plane = layer if sx < 0 else 16 - layers + layer
                    start = 32 * plane + (0 if sy < 0 else 24)
                    send[base + 8 * layer : base + 8 * layer + 8, :] = src[start : start + 8, :]
            elif sx:
                start = 0 if sx < 0 else 32 * (16 - layers)
                send[base : base + rows, :] = src[start : start + rows, :]
            else:
                for layer in range(layers):
                    row = layer if sy < 0 else 32 - layers + layer
                    send[base + 16 * layer : base + 16 * layer + 16, :] = src[
                        pl.ds(row, 16, stride=32), :
                    ]
            if extra:
                send[base + rows : base + rows + 8, :] = tile
            total = message_rows(direction, layers, extra)
            copy = pltpu.make_async_remote_copy(
                src_ref=send.at[pl.ds(base, total)],
                dst_ref=recv.at[pl.ds(base, total)],
                send_sem=halo_send_sem.at[8 * at_round + at],
                recv_sem=halo_recv_sem.at[8 * at_round + at],
                device_id=neighbour(direction),
                device_id_type=MESH_ID,
            )
            copy.start()
            copies.append(copy)
        halo_copies[name] = copies

    def arrived(name):
        for copy in halo_copies[name]:
            copy.wait_recv()

    def part(name, direction, layer=0):
        at_round = [r[0] for r in ROUNDS].index(name)
        layers, extra = ROUNDS[at_round][1:]
        offsets = message_offsets(layers, extra)
        at = DIRS.index((-direction[0], -direction[1]))
        unit = 8 if direction[0] and direction[1] else 32 if direction[0] else 16
        start = offsets[at] + unit * layer
        return recv_bufs[name][start : start + unit, :]

    def part_row(name, direction, layer, last):
        at_round = [r[0] for r in ROUNDS].index(name)
        layers, extra = ROUNDS[at_round][1:]
        at = DIRS.index((-direction[0], -direction[1]))
        start = message_offsets(layers, extra)[at] + 8 * layer + last
        return recv_bufs[name][start : start + 1, :]

    def add_faces(name, ref, masked):
        def scale(values, first, second):
            if not masked:
                return values
            return values * (first * second if first is not None and second is not None else second if first is None else first)

        ref[0:32, :] += scale(part(name, (-1, 0)), x_lo, None)
        ref[480:512, :] += scale(part(name, (1, 0)), x_hi, None)
        ref[pl.ds(0, 16, stride=32), :] += scale(part(name, (0, -1)), y_lo, None)
        ref[pl.ds(31, 16, stride=32), :] += scale(part(name, (0, 1)), y_hi, None)
        ref[0:1, :] += scale(part_row(name, (-1, -1), 0, 7), x_lo, y_lo)
        ref[31:32, :] += scale(part_row(name, (-1, 1), 0, 0), x_lo, y_hi)
        ref[480:481, :] += scale(part_row(name, (1, -1), 0, 7), x_hi, y_lo)
        ref[511:512, :] += scale(part_row(name, (1, 1), 0, 0), x_hi, y_hi)

    def add_arrived(name, ref):
        arrived(name)
        add_faces(name, ref, False)

    g_copies = []
    g_pending = {}
    reach = n_low + 2

    def g_send_rows(which, stage, values):
        slot = 3 * which + stage
        rows = values.shape[0]
        g_send[8 * slot : 8 * slot + rows, :] = values
        copies = {}
        for step in steps_of(stage):
            at = 7 * slot + step - 1
            copy = pltpu.make_async_remote_copy(
                src_ref=g_send.at[pl.ds(8 * slot, rows)],
                dst_ref=g_recv.at[pl.ds(8 * at, rows)],
                send_sem=g_send_sem.at[at],
                recv_sem=g_recv_sem.at[at],
                device_id=stage_partner(stage, step),
                device_id_type=MESH_ID,
            )
            copy.start()
            copies[step] = copy
        g_copies.extend(copies.values())
        g_pending[slot] = (values, copies)

    def g_rows(which, stage):
        slot = 3 * which + stage
        values, copies = g_pending[slot]
        out = {0: values}
        for step in reversed(steps_of(stage)):
            copies[step].wait_recv()
        for step in steps_of(stage):
            at = 7 * slot + step - 1
            out[step] = g_recv[8 * at : 8 * at + values.shape[0], :]
        return out

    def total_of(rows):
        total = None
        for values in rows.values():
            total = values if total is None else total + values
        return total

    def scalar_spot(start, at):
        return tile_lane == start + at

    def g_start(which, sums, scalars):
        tile = jnp.zeros((8, 128), F32)
        for (dx, dy), value in sums.items():
            tile = jnp.where(tile_lane == reach * (dx + 1) + low + dy + 1, value, tile)
        for at, value in enumerate(scalars):
            tile = jnp.where(scalar_spot(32, at), value, tile)
        g_send_rows(which, 0, tile[0:1])

    lane2 = lax.broadcasted_iota(jnp.int32, (1, 128), 1)

    def g_second(which):
        row = total_of(g_rows(which, 0))

        def moved(part, base):
            inside = (lane2 >= reach * part) & (lane2 < reach * (part + 1))
            shift = (high * n_low + (base - 1 - reach * part) + 256) & 127
            return pltpu.roll(jnp.where(inside, row, 0.0), shift, 1)

        scalars = pltpu.roll(jnp.where(lane2 >= 32, row, 0.0), 32, 1)
        scalars = jnp.where((lane2 >= 64) & (lane2 < 72), scalars, 0.0)
        one = moved(0, 0) + moved(1, 64)
        two = moved(2, 0) + scalars
        g_send_rows(which, 1, jnp.concatenate([one, two], axis=0))

    def g_third(which):
        g_send_rows(which, 2, total_of(g_rows(which, 1)))

    def g_finish(which):
        rows = g_rows(which, 2)
        sides = jnp.zeros((8, 128), F32)
        middle = jnp.zeros((8, 128), F32)
        scalars = None
        for step, values in rows.items():
            source = (grp - step) & (n_grp - 1)
            one = jnp.broadcast_to(values[0:1], (8, 128))
            two = jnp.broadcast_to(values[1:2], (8, 128))
            sides = sides + jnp.where(tile_row == ((source - 1) & (n_grp - 1)), one, 0.0)
            sides = sides + jnp.where(tile_row == ((source + 1) & (n_grp - 1)), two, 0.0)
            middle = middle + jnp.where(tile_row == source, one, 0.0)
            scalars = two if scalars is None else scalars + two
        return (sides + pltpu.roll(middle, 64, 1), scalars)

    def read_scalar(tile, at):
        lanes = jnp.sum(jnp.where(tile_lane == at, tile, 0.0), axis=1, keepdims=True)
        return jnp.broadcast_to(lanes, (8, 128))

    def coarse_sums(ref):
        middle = None
        for plane in range(16):
            piece = x_times(ref[32 * plane : 32 * plane + 32, :], share_x(plane))
            middle = piece if middle is None else middle + piece
        rows = {
            -1: ref[0:32, :] * (0.5 * x_lo),
            0: middle,
            1: ref[480:512, :] * (0.5 * x_hi),
        }
        sums = {}
        for dx in (-1, 0, 1):
            field = rows[dx] * keep_z
            sums[dx, 0] = all_sum(fold_rows(field * share_y))
            sums[dx, -1] = all_sum(field[0:8] * jnp.where(tile_row == 0, 0.5 * y_lo, 0.0))
            sums[dx, 1] = all_sum(field[24:32] * jnp.where(tile_row == 7, 0.5 * y_hi, 0.0))
        return sums

    def mass_kind(one, two):
        if one == "c":
            return two
        return one if two in ("c", one) else None

    def steep_kind(one, two):
        return "d" + one if one == two != "c" else None

    def coarse_energies():
        coef = buf["kc"]
        steep_z, steep_first, steep_last = [tab["steep"][8 * i : 8 * i + 8, :] for i in range(3)]
        planes = [coef[32 * plane : 32 * plane + 32, :] for plane in range(16)]
        along_x = {
            "c": weighted([1.0] * 16, planes),
            "0": planes[0],
            "1": planes[15],
            "d0": weighted(deriv[:, 0] ** 2, planes[:8]),
            "d1": weighted(deriv[:, 7] ** 2, planes[8:]),
        }
        z_mass = keep_z[0:8]

        def reduced(x_kind, y_kind, z_part):
            values = along_x[x_kind]
            if y_kind == "c":
                values = fold_rows(values)
            elif y_kind == "0":
                values = jnp.where(tile_row == 0, values[0:8], 0.0)
            elif y_kind == "1":
                values = jnp.where(tile_row == 7, values[24:32], 0.0)
            elif y_kind == "d0":
                values = values[0:8] * steep_first
            else:
                values = values[24:32] * steep_last
            return all_sum(values * z_part)

        kinds = ("c", "0", "1")
        pieces = {}
        for one in kinds:
            for two in kinds:
                pieces[one, two] = reduced(one, two, steep_z)
        for steep in ("d0", "d1"):
            for kind in kinds:
                pieces[steep, kind] = reduced(steep, kind, z_mass)
                pieces[kind, steep] = reduced(kind, steep, z_mass)
        energies = {}
        for a in kinds:
            for b in kinds:
                for c in kinds:
                    for d in kinds:
                        keys = (
                            (mass_kind(a, c), mass_kind(b, d)),
                            (steep_kind(a, c), mass_kind(b, d)),
                            (mass_kind(a, c), steep_kind(b, d)),
                        )
                        found = [pieces[key] for key in keys if key in pieces]
                        if found:
                            energies[a, b, c, d] = weighted([1.0] * len(found), found)
        return energies

    def coarse_image(energies, values):
        kinds = ("c", "0", "1")
        half_x = (0.5 * x_lo, 0.5 * x_hi)
        half_y = (0.5 * y_lo, 0.5 * y_hi)

        def split(before, own, after, half):
            return {
                "c": own,
                "0": before * half[0] + own * (half[0] - 1.0),
                "1": after * half[1] + own * (half[1] - 1.0),
            }

        def joined(parts, half):
            own = parts["c"] + parts["0"] * (half[0] - 1.0) + parts["1"] * (half[1] - 1.0)
            return (parts["0"] * half[0], own, parts["1"] * half[1])

        by_x = {dy: split(*[values[dx, dy] for dx in (-1, 0, 1)], half_x) for dy in (-1, 0, 1)}
        steps = {a: split(*[by_x[dy][a] for dy in (-1, 0, 1)], half_y) for a in kinds}
        image = {}
        for a in kinds:
            parts = {}
            for b in kinds:
                terms = [
                    energies[a, b, c, d] * steps[c][d]
                    for c in kinds
                    for d in kinds
                    if (a, b, c, d) in energies
                ]
                parts[b] = weighted([1.0] * len(terms), terms)
            image[a] = joined(parts, half_y)
        out = {}
        for at, dy in enumerate((-1, 0, 1)):
            for dx, value in zip((-1, 0, 1), joined({a: image[a][at] for a in kinds}, half_x)):
                out[dx, dy] = value
        return out

    def paired(values, sums):
        total = None
        for key in values:
            piece = values[key] * sums[key]
            total = piece if total is None else total + piece
        return total

    q_scale = 1.0 / math.sqrt(LOCAL_X * LOCAL_Y * LOCAL_Z)

    def coarse_values(tile):
        values = {}
        for dx in (-1, 0, 1):
            for dy in (-1, 0, 1):
                if dx == 0 and dy == 0:
                    row = buf["ct"][...]
                else:
                    layers, extra = ROUNDS[0][1:]
                    at = DIRS.index((-dx, -dy))
                    start = message_offsets(layers, extra)[at] + message_rows((dx, dy), layers, False)
                    row = recv_bufs["rhs"][start : start + 8, :]
                values[dx, dy] = all_sum(row * tile) * q_scale
        return values

    def coarse_patterns(values):
        lines = {}
        for dx in (-1, 0, 1):
            centre = jnp.concatenate([values[dx, 0]] * 4, axis=0)
            first = jnp.concatenate([values[dx, -1]] * 4, axis=0)
            last = jnp.concatenate([values[dx, 1]] * 4, axis=0)
            line = jnp.where(row32 == 0, (centre + first) * (0.5 * y_lo), centre)
            line = jnp.where(row32 == 31, (centre + last) * (0.5 * y_hi), line)
            lines[dx] = line * keep_z
        return (
            (lines[0] + lines[-1]) * (0.5 * x_lo),
            lines[0],
            (lines[0] + lines[1]) * (0.5 * x_hi),
        )

    def build_pin(name, src):
        pin = buf["pin"]
        zero8 = jnp.zeros((8, 128), F32)
        for plane in range(18):
            pin[40 * plane + 32 : 40 * plane + 40, :] = zero8
        for plane in range(16):
            pin[40 * (plane + 1) : 40 * (plane + 1) + 32, :] = src[32 * plane : 32 * plane + 32, :]
        pin[40:72, :] += part(name, (-1, 0), 1)
        pin[640:672, :] += part(name, (1, 0), 0)
        pin[pl.ds(40, 16, stride=40), :] += part(name, (0, -1), 1)
        pin[pl.ds(71, 16, stride=40), :] += part(name, (0, 1), 0)
        pin[pl.ds(72, 16, stride=40), :] = part(name, (0, -1), 0)
        pin[pl.ds(73, 16, stride=40), :] = part(name, (0, 1), 1)
        for at_plane, dx, layer in ((1, -1, 1), (16, 1, 0), (0, -1, 0), (17, 1, 1)):
            base = 40 * at_plane
            if at_plane in (0, 17):
                pin[base : base + 32, :] = part(name, (dx, 0), layer)
            pin[base : base + 1, :] += part_row(name, (dx, -1), layer, 7)
            pin[base + 31 : base + 32, :] += part_row(name, (dx, 1), layer, 0)
            pin[base + 32 : base + 33, :] += part_row(name, (dx, -1), layer, 6)
            pin[base + 33 : base + 34, :] += part_row(name, (dx, 1), layer, 1)

    row40 = lax.broadcasted_iota(jnp.int32, (40, 128), 0)
    edge40 = jnp.where(
        (row40 == 0) | (row40 == 32), y_lo, jnp.where((row40 == 31) | (row40 == 33), y_hi, 1.0)
    ).astype(F32)

    def pin_plane(plane):
        values = buf["pin"][40 * plane : 40 * plane + 40, :] * edge40
        if plane < 2:
            values = values * x_lo
        if plane > 15:
            values = values * x_hi
        return values

    def assembled_own(plane):
        return z_assembled(pin_plane(plane + 1)[0:32]) * keep_z

    basis, _ = fdm_tables()
    signs = parity_signs(basis)
    deriv = derivative_table()
    sources = ([0, 1, 2, 3, 4, 5, 6, 7, 8, 10], [7, 9, 10, 11, 12, 13, 14, 15, 16, 17])

    def schwarz(dst):
        y1, u, v, x2 = buf["y1"], buf["u"], buf["v"], buf["x2"]
        yf, yb = tab["yf"][...], tab["yb"][...]
        for pair in range(9):
            out = left_mul(yf, pin_plane(2 * pair), pin_plane(2 * pair + 1))
            y1[80 * pair : 80 * pair + 40, :] = out[0:40, :128]
            y1[80 * pair + 40 : 80 * pair + 80, :] = out[0:40, 128:]
        for element in range(2):
            for tile in range(5):
                values = [y1[40 * p + 8 * tile : 40 * p + 8 * tile + 8, :] for p in sources[element]]
                for mode, piece in enumerate(x_modes(values, basis, signs)):
                    start = 40 * (10 * element + mode) + 8 * tile
                    u[start : start + 8, :] = piece
        for element in range(2):
            block = u[400 * element : 400 * element + 400, :]
            first, second = halves(block)
            modes = dot(jnp.concatenate([first, second], axis=1), tab["zf1"][...])
            modes = (modes + dot(first, tab["zf2"][...])) * tab["recip"][...]
            first, second = halves(modes)
            back = dot(first, tab["zb1"][...])
            v[400 * element : 400 * element + 400, :] = (
                back[:, :128] + back[:, 128:] + dot(second, tab["zb1"][:, 0:128])
            )
        for tile in range(5):
            outs = []
            for element in range(2):
                starts = [40 * (10 * element + mode) + 8 * tile for mode in range(10)]
                outs += x_unmodes([v[s : s + 8, :] for s in starts], basis, signs)
            shared = (outs[7] + outs[8]) * 0.5
            outs[7] = shared
            outs[8] = shared
            outs[0] = outs[0] * (0.5 * x_lo)
            outs[15] = outs[15] * (0.5 * x_hi)
            for plane in range(16):
                x2[40 * plane + 8 * tile : 40 * plane + 8 * tile + 8, :] = outs[plane]
        for pair in range(8):
            out = left_mul(yb, x2[80 * pair : 80 * pair + 40, :], x2[80 * pair + 40 : 80 * pair + 80, :])
            dst[64 * pair : 64 * pair + 32, :] = out[:, :128] * face_y
            dst[64 * pair + 32 : 64 * pair + 64, :] = out[:, 128:] * face_y

    def stiff(src, coef, dst, extra=None):
        energy = jnp.zeros((8, 128), F32)
        for chunk in range(2):
            at = slice(256 * chunk, 256 * chunk + 256)
            grad = right_mul(src[at, :], tab["zd"][...])
            flow = grad * coef[at, :]
            energy = energy + fold_rows(grad * flow)
            dst[at, :] = right_mul(flow, tab["zdt"][...])
        for pair in range(8):
            one = slice(64 * pair, 64 * pair + 32)
            two = slice(64 * pair + 32, 64 * pair + 64)
            grad = left_mul(tab["yd"][...], src[one, :], src[two, :])
            flow_one = grad[:, :128] * coef[one, :]
            flow_two = grad[:, 128:] * coef[two, :]
            energy = energy + fold_rows(grad[:, :128] * flow_one) + fold_rows(grad[:, 128:] * flow_two)
            back = left_mul(tab["ydt"][...], flow_one, flow_two)
            dst[one, :] += back[:, :128]
            dst[two, :] += back[:, 128:]
        for tile in range(4):
            sums = []
            for element in range(2):
                starts = [32 * (8 * element + i) + 8 * tile for i in range(8)]
                grads = x_derive([src[s : s + 8, :] for s in starts], deriv)
                flows = [grad * coef[s : s + 8, :] for grad, s in zip(grads, starts)]
                for grad, flow in zip(grads, flows):
                    energy = energy + grad * flow
                backs = x_derive(flows, deriv.T)
                for s, back in zip(starts, backs):
                    value = dst[s : s + 8, :] + back
                    if extra is not None:
                        value = value + extra[s : s + 8, :]
                    sums.append(value)
            shared = sums[7] + sums[8]
            sums[7] = shared
            sums[8] = shared
            for plane in range(16):
                dst[32 * plane + 8 * tile : 32 * plane + 8 * tile + 8, :] = sums[plane]
        for plane in range(16):
            at = slice(32 * plane, 32 * plane + 32)
            dst[at, :] = y_assembled(dst[at, :])
        return energy

    weights = GLL_WEIGHTS + GLL_WEIGHTS

    loads["rhs"].wait()
    loads["crow"].wait()
    for plane in range(16):
        at = slice(32 * plane, 32 * plane + 32)
        values = buf["rhs"][at, :]
        if plane == 7:
            values = values + buf["rhs"][256:288, :]
        if plane == 8:
            values = values + buf["rhs"][224:256, :]
        buf["s"][at, :] = y_assembled(values)
    ct = buf["ct"]
    ct[...] = jnp.zeros((8, 128), F32)
    count = n_grp * n_dev
    for at in range(n_grp):
        start = n_dev * at
        if count >= 128:
            row = crow_ref[:, start // 128 * 128 : start // 128 * 128 + 128]
        else:
            row = jnp.concatenate([crow_ref[...], jnp.zeros((1, 128 - count), F32)], axis=1)
        if start % 128:
            row = pltpu.roll(row, 128 - start % 128, 1)
        ct[at : at + 1, :] = jnp.where(lane2 < n_dev, row, 0.0)
    right_sums = coarse_sums(buf["s"])

    pl.semaphore_wait(barrier, len(partners))
    g_start(0, right_sums, [])
    exchange("rhs", buf["s"], ct[...])

    for name in ("sol", "kd", "flags", "wyz", "spread", "zd", "zdt", "yd", "ydt"):
        loads[name].wait()
    wyz = tab["wyz"][...]
    flags = jnp.concatenate([flags_ref[0], flags_ref[1]], axis=0).astype(F32).astype(BF16)
    flag_rows = dot(flags, tab["spread"][...])
    weight_column = GLL_WEIGHTS
    row8 = tile_row
    w_rows = jnp.zeros((8, 128), F32)
    for at, weight in enumerate(weight_column):
        w_rows = jnp.where(row8 == at, weight, w_rows)
    for plane in range(16):
        at = slice(32 * plane, 32 * plane + 32)
        buf["kd"][at, :] = buf["kd"][at, :] * (wyz * weights[plane])
        flux = jnp.concatenate(
            [
                flag_rows[4 * (plane // 8) + ey : 4 * (plane // 8) + ey + 1, :] * w_rows
                for ey in range(4)
            ],
            axis=0,
        )
        factor = wyz * (MASS_RATE * weights[plane]) + flux * (GROWTH * SEGREGATION * weights[plane])
        buf["x2"][at, :] = buf["sol"][at, :] * factor
    stiff(buf["sol"], buf["kd"], buf["solraw"], extra=buf["x2"])

    exchange("sol", buf["solraw"])
    for name in ("kc", "steep", "yf", "yb", "zf1", "zf2", "zb1", "recip"):
        loads[name].wait()
    for plane in range(16):
        at = slice(32 * plane, 32 * plane + 32)
        buf["kc"][at, :] = buf["kc"][at, :] * (wyz * weights[plane])
    energies = coarse_energies()

    stores = []

    def store(name, ref):
        copy = pltpu.make_async_copy(ref, outs[name], store_sem.at[OUT_NAMES.index(name)])
        copy.start()
        stores.append(copy)

    g_second(0)
    arrived("rhs")
    build_pin("rhs", buf["s"])
    schwarz(buf["z0"])
    exchange("sch0", buf["z0"])
    g_third(0)
    for plane in range(16):
        buf["b"][32 * plane : 32 * plane + 32, :] = assembled_own(plane)
    share_yz = share_y * share_z

    def product_of(first, second):
        tile = jnp.zeros((8, 128), F32)
        for plane in range(16):
            at = slice(32 * plane, 32 * plane + 32)
            piece = x_times(first[at, :] * second[at, :] * share_yz, share_x(plane))
            tile = tile + fold_rows(piece)
        return all_sum(tile)

    def add_coarse(ref, values):
        patterns = coarse_patterns(values)
        for plane in range(16):
            at = slice(32 * plane, 32 * plane + 32)
            ref[at, :] += patterns[0 if plane == 0 else 2 if plane == 15 else 1]

    add_arrived("sch0", buf["z0"])
    curve = all_sum(stiff(buf["z0"], buf["kc"], buf["a1"]))
    sums = coarse_sums(buf["a1"])
    rz = product_of(buf["b"], buf["z0"])
    total, _ = g_finish(0)
    coarse = coarse_values(total)
    image = coarse_image(energies, coarse)
    applied_sums = {key: sums[key] + image[key] for key in sums}
    rz = rz + paired(coarse, right_sums)
    curve = curve + paired(coarse, {key: sums[key] + applied_sums[key] for key in sums})
    g_start(1, applied_sums, [rz, curve])
    add_coarse(buf["z0"], coarse)
    stiff(buf["z0"], buf["kc"], buf["a1"])
    exchange("sti0", buf["a1"])

    arrived("sol")
    add_faces("sol", buf["solraw"], True)
    for plane in range(16):
        at = slice(32 * plane, 32 * plane + 32)
        buf["solraw"][at, :] = z_assembled(buf["solraw"][at, :])
    store("sol", buf["solraw"])

    g_second(1)
    arrived("sti0")
    build_pin("sti0", buf["a1"])
    schwarz(buf["w"])
    exchange("sch1", buf["w"])
    g_third(1)
    for plane in range(16):
        buf["p0"][32 * plane : 32 * plane + 32, :] = assembled_own(plane)
    add_arrived("sch1", buf["w"])
    w_curve = all_sum(stiff(buf["w"], buf["kc"], buf["rhs"]))
    sums = coarse_sums(buf["rhs"])
    b_w = product_of(buf["b"], buf["w"])
    p_w = product_of(buf["p0"], buf["w"])
    total, scalars = g_finish(1)
    coarse = coarse_values(total)
    image = coarse_image(energies, coarse)
    b_w = b_w + paired(coarse, right_sums)
    p_w = p_w + paired(coarse, applied_sums)
    w_curve = w_curve + paired(coarse, {key: 2.0 * sums[key] + image[key] for key in sums})
    tile = jnp.zeros((8, 128), F32)
    for at, value in enumerate((b_w, p_w, w_curve)):
        tile = jnp.where(tile_lane == at, value, tile)
    g_send_rows(2, 0, tile[0:1])
    rz0 = read_scalar(scalars, 64)
    curve0 = read_scalar(scalars, 65)
    alpha0 = rz0 / curve0
    add_coarse(buf["w"], coarse)
    stiff(buf["w"], buf["kc"], buf["rhs"])
    exchange("sti1", buf["rhs"])
    for name in ("z0", "w", "b", "p0"):
        store(name, buf[name])
    g_send_rows(2, 1, total_of(g_rows(2, 0)))
    add_arrived("sti1", buf["rhs"])
    g_send_rows(2, 2, total_of(g_rows(2, 1)))
    for plane in range(16):
        at = slice(32 * plane, 32 * plane + 32)
        values = z_assembled(buf["rhs"][at, :]) * keep_z * edge_y
        if plane == 0:
            values = values * x_lo
        if plane == 15:
            values = values * x_hi
        buf["rhs"][at, :] = values
    store("aw", buf["rhs"])
    for name in halo_copies:
        for copy in halo_copies[name]:
            copy.wait_send()
    for copy in g_copies:
        copy.wait_send()
    for copy in stores:
        copy.wait()
    inverse = 1.0 / rz0
    total = jnp.broadcast_to(total_of(g_rows(2, 2)), (8, 128))
    b_w, p_w, w_curve = [read_scalar(total, at) for at in range(3)]
    rz1 = alpha0 * (alpha0 * p_w - b_w)
    cross1 = curve0 - alpha0 * p_w
    curve1 = cross1 - alpha0 * (p_w - alpha0 * w_curve)
    beta = rz1 * inverse
    alpha1 = rz1 / (curve1 + beta * (2.0 * cross1 + beta * curve0))
    steps_ref[0:8, :] = alpha0 + alpha1 * (1.0 + beta)
    steps_ref[8:16, :] = alpha0 * alpha1
    store("steps", steps_ref)
    stores[-1].wait()


def finish_body(*refs):
    count = len(OUT_NAMES)
    sources, targets, bufs, load_sem, store_sem = refs[:count], refs[count : count + 3], refs[count + 3 : 2 * count + 3], refs[-2], refs[-1]
    loads = {}
    for at in (6, 0, 1, 2, 3, 4, 5):
        loads[OUT_NAMES[at]] = pltpu.make_async_copy(sources[at], bufs[at], load_sem.at[at])
        loads[OUT_NAMES[at]].start()
    z0, w, b, aw, p0, sol, steps = bufs
    for name in ("steps", "z0", "w"):
        loads[name].wait()
    first, second = steps[0:8, :], steps[8:16, :]
    for plane in range(LOCAL_X):
        at = slice(32 * plane, 32 * plane + 32)
        z0[at, :] = times_tile(z0[at, :], first) - times_tile(w[at, :], second)
    stores = [pltpu.make_async_copy(z0, targets[0], store_sem.at[0])]
    stores[0].start()
    for name in ("b", "aw", "p0"):
        loads[name].wait()
    for plane in range(LOCAL_X):
        at = slice(32 * plane, 32 * plane + 32)
        b[at, :] = b[at, :] - times_tile(p0[at, :], first) + times_tile(aw[at, :], second)
    stores.append(pltpu.make_async_copy(b, targets[1], store_sem.at[1]))
    stores[1].start()
    loads["sol"].wait()
    stores.append(pltpu.make_async_copy(sol, targets[2], store_sem.at[2]))
    stores[2].start()
    for copy in stores:
        copy.wait()


def finish(fields):
    far = pl.BlockSpec(memory_space=pltpu.HBM)
    return pl.pallas_call(
        finish_body,
        out_shape=[jax.ShapeDtypeStruct((ROWS, LOCAL_Z), F32)] * 3,
        in_specs=[far] * len(OUT_NAMES),
        out_specs=[far] * 3,
        scratch_shapes=[pltpu.VMEM(v.shape, F32) for v in fields]
        + [pltpu.SemaphoreType.DMA((len(OUT_NAMES),)), pltpu.SemaphoreType.DMA((3,))],
        compiler_params=pltpu.CompilerParams(vmem_limit_bytes=63 * 1024 * 1024),
    )(*fields)


def run_kernel(sizes, fields, flags, coarse_row, tables):
    constants = [jnp.asarray(tables[name]) for name in TABLE_NAMES]
    far = pl.BlockSpec(memory_space=pltpu.HBM)
    field = pltpu.VMEM((ROWS, LOCAL_Z), F32)

    def rows(count):
        return pltpu.VMEM((count, LOCAL_Z), F32)

    halo = [rows(message_offsets(layers, extra)[-1]) for _, layers, extra in ROUNDS]
    scratch = (
        [field] * 5
        + [rows(720), rows(720), rows(800), rows(800), rows(640)]
        + [field] * 6
        + [rows(8)]
        + halo
        + halo
        + [rows(72), rows(8 * 63)]
        + [pltpu.SemaphoreType.DMA((count,)) for count in (48, 48, 63, 63, 6 + len(constants), len(OUT_NAMES))]
        + [pltpu.VMEM(flags.shape, jnp.int32), pltpu.VMEM(coarse_row.shape, F32), rows(16)]
        + [pltpu.VMEM(table.shape, table.dtype) for table in constants]
    )
    return pl.pallas_call(
        functools.partial(body, sizes),
        out_shape=[
            jax.ShapeDtypeStruct((16 if name == "steps" else ROWS, LOCAL_Z), F32) for name in OUT_NAMES
        ],
        in_specs=[far] * (6 + len(constants)),
        out_specs=[far] * len(OUT_NAMES),
        scratch_shapes=scratch,
        compiler_params=pltpu.CompilerParams(
            collective_id=0, has_side_effects=True, vmem_limit_bytes=63 * 1024 * 1024
        ),
    )(*fields, flags, coarse_row, *constants)


def solution(mesh):
    n_grp, n_dev = (mesh.shape["grp"], mesh.shape["dev"])
    n_low = 8 if n_dev % 8 == 0 else 2
    sizes = (n_grp, n_low, n_dev // n_low)
    tables = make_tables()

    def shards(right_side, coefficient, solute, diffusivity, interface_flags, coarse_inverse):
        fields = [v.reshape(ROWS, LOCAL_Z) for v in (right_side, coefficient, solute, diffusivity)]
        outs = run_kernel(sizes, fields, interface_flags, coarse_inverse, tables)
        return tuple(v.reshape(LOCAL_X, LOCAL_Y, LOCAL_Z) for v in finish(outs))

    placed = (
        P("grp", "dev", None),
        P("grp", "dev", None),
        P("grp", "dev", None),
        P("grp", "dev", None),
        P("grp", "dev", None),
        P(("grp", "dev"), None),
    )
    return jax.shard_map(
        shards,
        mesh=mesh,
        in_specs=placed,
        out_specs=(P("grp", "dev", None), P("grp", "dev", None), P("grp", "dev", None)),
        check_vma=False,
    )
```

```python
import functools
import math

import jax
import jax.numpy as jnp
import ml_dtypes
import numpy as np
from jax import lax
from jax.experimental import pallas as pl
from jax.experimental.pallas import tpu as pltpu
from jax.sharding import PartitionSpec as P

GLL_POINTS = [
    -1.0,
    -0.8717401485096066,
    -0.5917001814331423,
    -0.2092992179024789,
    0.2092992179024789,
    0.5917001814331423,
    0.8717401485096066,
    1.0,
]
GLL_WEIGHTS = [
    0.0357142857142857,
    0.2107042271435061,
    0.3411226924835044,
    0.4124587946587038,
    0.4124587946587038,
    0.3411226924835044,
    0.2107042271435061,
    0.0357142857142857,
]
SHIFT_MASS = 0.5
MASS_RATE = 2.0
GROWTH = 40.0
SEGREGATION = 0.7


def derivative_table():
    products = []
    for row_at in range(8):
        value = 1.0
        for other in range(8):
            if other != row_at:
                value = value * (GLL_POINTS[row_at] - GLL_POINTS[other])
        products.append(value)
    table = [[0.0] * 8 for row_at in range(8)]
    for row_at in range(8):
        total = 0.0
        for other in range(8):
            if other != row_at:
                entry = (
                    products[row_at] / products[other] / (GLL_POINTS[row_at] - GLL_POINTS[other])
                )
                table[row_at][other] = entry
                total = total + entry
        table[row_at][row_at] = -total
    return np.array(table)


def margin_matrices():
    deriv_np = derivative_table()
    spacing = GLL_POINTS[1] - GLL_POINTS[0]
    stiffness = [[0.0] * 10 for row_at in range(10)]
    masses = [0.0] * 10
    for row_at in range(8):
        masses[row_at + 1] = GLL_WEIGHTS[row_at]
        for other in range(8):
            total = 0.0
            for point in range(8):
                total = (
                    total + deriv_np[point, row_at] * GLL_WEIGHTS[point] * deriv_np[point, other]
                )
            stiffness[row_at + 1][other + 1] = total
    for outer_end, inner_end in ((0, 1), (9, 8)):
        stiffness[outer_end][outer_end] += 1.0 / spacing
        stiffness[inner_end][inner_end] += 1.0 / spacing
        stiffness[outer_end][inner_end] -= 1.0 / spacing
        stiffness[inner_end][outer_end] -= 1.0 / spacing
        masses[outer_end] += 0.5 * spacing
        masses[inner_end] += 0.5 * spacing
    return (stiffness, masses)


def jacobi_eigen(matrix_rows):
    count_in = len(matrix_rows)
    work = [list(row_now) for row_now in matrix_rows]
    vectors = [
        [1.0 if other == row_at else 0.0 for other in range(count_in)] for row_at in range(count_in)
    ]
    for sweep in range(15):
        for first in range(count_in):
            for second in range(first + 1, count_in):
                entry = work[first][second]
                if entry != 0.0:
                    theta = (work[second][second] - work[first][first]) / (2.0 * entry)
                    sign_now = 1.0 if theta >= 0.0 else -1.0
                    tangent = sign_now / (abs(theta) + math.sqrt(theta * theta + 1.0))
                    cosine = 1.0 / math.sqrt(tangent * tangent + 1.0)
                    sine = tangent * cosine
                    for index in range(count_in):
                        left_val = work[index][first]
                        right_val = work[index][second]
                        work[index][first] = cosine * left_val - sine * right_val
                        work[index][second] = sine * left_val + cosine * right_val
                    for index in range(count_in):
                        left_val = work[first][index]
                        right_val = work[second][index]
                        work[first][index] = cosine * left_val - sine * right_val
                        work[second][index] = sine * left_val + cosine * right_val
                    for index in range(count_in):
                        left_val = vectors[index][first]
                        right_val = vectors[index][second]
                        vectors[index][first] = cosine * left_val - sine * right_val
                        vectors[index][second] = sine * left_val + cosine * right_val
    return ([work[index][index] for index in range(10 if count_in == 10 else count_in)], vectors)


def fdm_tables():
    stiffness, masses = margin_matrices()
    scaled = [
        [
            stiffness[row_at][other] / math.sqrt(masses[row_at] * masses[other])
            for other in range(10)
        ]
        for row_at in range(10)
    ]
    values, vectors = jacobi_eigen(scaled)
    basis = np.array(
        [
            [vectors[row_at][other] / math.sqrt(masses[row_at]) for other in range(10)]
            for row_at in range(10)
        ]
    )
    return (basis, np.array(values))


def z_forward_table(elements):
    basis, values = fdm_tables()
    extend_np = np.zeros((8 * elements, 10 * elements))
    for element in range(elements):
        for slot_in in range(10):
            source = 8 * element + slot_in - 1
            if slot_in == 0:
                source = 8 * element - 2
            if slot_in == 9:
                source = 8 * element + 9
            if 0 <= source < 8 * elements:
                extend_np[source, 10 * element + slot_in] = 1.0
    return extend_np @ np.kron(np.eye(elements), basis)


def z_backward_table(elements):
    basis, values = fdm_tables()
    return np.kron(np.eye(elements), basis[1:9].T)


def z_derivative(elements):
    return np.kron(np.eye(elements), derivative_table().T)


def z_pairs(elements):
    pairs_np = np.eye(8 * elements)
    for element in range(elements - 1):
        pairs_np[8 * element + 7, 8 * element + 8] = 1.0
        pairs_np[8 * element + 8, 8 * element + 7] = 1.0
    return pairs_np


LOCAL_X, LOCAL_Y, LOCAL_Z = (16, 32, 128)
ROWS = LOCAL_X * LOCAL_Y
DIRS = ((-1, -1), (-1, 1), (1, -1), (1, 1), (0, -1), (0, 1), (-1, 0), (1, 0))
F32 = jnp.float32
BF16 = jnp.bfloat16
MESH_ID = pl.DeviceIdType.MESH


def split_np(table):
    high = np.asarray(table, np.float32).astype(ml_dtypes.bfloat16)
    low = (np.asarray(table, np.float64) - high.astype(np.float64)).astype(ml_dtypes.bfloat16)
    return (high, low)


def left_table(matrix, rows):
    high, low = split_np(matrix)
    joined = np.concatenate([high, high, low], axis=1)
    out = np.zeros((rows, 128), ml_dtypes.bfloat16)
    out[: joined.shape[0], : joined.shape[1]] = joined
    return out


def y_pairs():
    pairs = np.eye(LOCAL_Y)
    for element in range(LOCAL_Y // 8 - 1):
        pairs[8 * element + 7, 8 * element + 8] = 1.0
        pairs[8 * element + 8, 8 * element + 7] = 1.0
    return pairs


def inner_share(count_in):
    share = np.ones(count_in)
    for position in range(count_in):
        if position % 8 in (0, 7) and position not in (0, count_in - 1):
            share[position] = 0.5
    return share


def padded_to(matrix, rows, columns):
    out = np.zeros((rows, columns))
    out[: matrix.shape[0], : matrix.shape[1]] = matrix
    return out


def make_tables():
    basis, values = fdm_tables()
    deriv = derivative_table()
    ends = np.ones(LOCAL_Z)
    ends[0] = 0.0
    ends[-1] = 0.0
    pairs_z = z_pairs(LOCAL_Z // 8)
    fore = pairs_z @ np.diag(ends) @ z_forward_table(LOCAL_Z // 8)
    back = z_backward_table(LOCAL_Z // 8) @ pairs_z @ np.diag(ends * inner_share(LOCAL_Z))
    fore_hi, fore_lo = split_np(padded_to(fore, 128, 256))
    back_hi, back_lo = split_np(padded_to(back, 256, 128))
    zf1 = np.concatenate([fore_hi, fore_hi], axis=0)
    zb1 = np.concatenate([back_hi, back_lo], axis=1)

    def square(matrix):
        high, low = split_np(matrix)
        return np.concatenate([np.concatenate([high, low], axis=1)] * 2, axis=0)

    deriv_z = np.kron(np.eye(LOCAL_Z // 8), deriv.T)
    deriv_y = np.kron(np.eye(LOCAL_Y // 8), deriv)
    count_y = LOCAL_Y // 8
    extend = np.zeros((10 * count_y, 40))
    for element in range(count_y):
        for slot in range(10):
            source = 8 * element + slot - 1
            if slot == 0:
                source = 8 * element - 2 if element else 32
            if slot == 9:
                source = 8 * element + 9 if element + 1 < count_y else 33
            extend[10 * element + slot, source] = 1.0
    y_fore = np.kron(np.eye(count_y), basis.T) @ extend
    y_back = np.diag(inner_share(LOCAL_Y)) @ y_pairs() @ np.kron(np.eye(count_y), basis[1:9])
    sums = (
        values[:, None, None]
        + np.tile(values, count_y)[None, :, None]
        + np.tile(values, LOCAL_Z // 8)[None, None, :]
        + SHIFT_MASS
    )
    recip = np.zeros((10 * 40, 256), np.float32)
    recip[:, :160] = (1.0 / sums).reshape(400, 160)
    weights = np.array(GLL_WEIGHTS)
    wyz = np.tile(weights, count_y)[:, None] * np.tile(weights, LOCAL_Z // 8)[None, :]
    steep = np.zeros((24, LOCAL_Z), np.float32)
    steep[0:8, 0:8] = deriv[:, 0] ** 2
    steep[0:8, LOCAL_Z - 8 :] = deriv[:, 7] ** 2
    steep[8:16] = deriv[:, 0:1] ** 2
    steep[16:24] = deriv[:, 7:8] ** 2
    spread = np.zeros((LOCAL_Z // 8, LOCAL_Z), ml_dtypes.bfloat16)
    for element in range(LOCAL_Z // 8):
        spread[element, 8 * element] = 1.0
    return dict(
        yf=left_table(y_fore, 48),
        yb=left_table(y_back, 32),
        yd=left_table(deriv_y, 32),
        ydt=left_table(deriv_y.T, 32),
        zf1=zf1,
        zf2=fore_lo,
        zb1=zb1,
        zd=square(deriv_z),
        zdt=square(deriv_z.T),
        wyz=wyz.astype(np.float32),
        spread=spread,
        steep=steep,
        recip=recip,
    )


TABLE_NAMES = ("yf", "yb", "yd", "ydt", "zf1", "zf2", "zb1", "zd", "zdt", "wyz", "spread", "steep", "recip")


def parity_signs(basis):
    signs = []
    for mode in range(10):
        even = np.abs(basis[:, mode] - basis[::-1, mode]).max()
        odd = np.abs(basis[:, mode] + basis[::-1, mode]).max()
        signs.append(1 if even < odd else -1)
    return signs


def weighted(coefficients, terms):
    total = None
    for coefficient, term in zip(coefficients, terms):
        piece = term * float(coefficient)
        total = piece if total is None else total + piece
    return total


def x_derive(values, matrix):
    sums = [values[i] + values[7 - i] for i in range(4)]
    gaps = [values[i] - values[7 - i] for i in range(4)]
    out = [None] * 8
    for p in range(4):
        first = weighted([(matrix[p, i] + matrix[p, 7 - i]) / 2 for i in range(4)], sums)
        second = weighted([(matrix[p, i] - matrix[p, 7 - i]) / 2 for i in range(4)], gaps)
        out[p] = second + first
        out[7 - p] = second - first
    return out


def x_modes(values, basis, signs):
    sums = [values[i] + values[9 - i] for i in range(5)]
    gaps = [values[i] - values[9 - i] for i in range(5)]
    return [
        weighted([basis[i, mode] for i in range(5)], sums if signs[mode] > 0 else gaps)
        for mode in range(10)
    ]


def x_unmodes(values, basis, signs):
    evens = [mode for mode in range(10) if signs[mode] > 0]
    odds = [mode for mode in range(10) if signs[mode] < 0]
    out = [None] * 8
    for i in range(1, 5):
        first = weighted([basis[i, mode] for mode in evens], [values[mode] for mode in evens])
        second = weighted([basis[i, mode] for mode in odds], [values[mode] for mode in odds])
        out[i - 1] = first + second
        out[8 - i] = first - second
    return out


def dot(first, second):
    return jnp.dot(first, second, preferred_element_type=F32)


def halves(values):
    high = values.astype(BF16)
    return (high, (values - high.astype(F32)).astype(BF16))


def left_mul(table, first, second):
    values = jnp.concatenate([first, second], axis=1)
    high = values.astype(BF16).astype(F32)
    rows = values.shape[0]
    parts = [high, values - high, high]
    if 3 * rows < 128:
        parts.append(jnp.zeros((128 - 3 * rows, values.shape[1]), F32))
    return dot(table, jnp.concatenate(parts, axis=0).astype(BF16))


def right_mul(values, table):
    high, low = halves(values)
    out = dot(jnp.concatenate([high, low], axis=1), table)
    return out[:, :128] + out[:, 128:]


def fold_rows(values):
    return jnp.sum(values.reshape(values.shape[0] // 8, 8, 128), axis=0)


def all_sum(values):
    lanes = jnp.sum(jnp.sum(values, axis=0, keepdims=True), axis=1, keepdims=True)
    return jnp.broadcast_to(lanes, (8, 128))


def times_tile(values, tile):
    return (values.reshape(values.shape[0] // 8, 8, 128) * tile[None]).reshape(values.shape)


def message_rows(direction, layers, extra):
    sx, sy = direction
    rows = 8 * layers if sx and sy else 32 * layers if sx else 16 * layers
    return rows + (8 if extra else 0)


def message_offsets(layers, extra):
    offsets = [0]
    for direction in DIRS:
        offsets.append(offsets[-1] + message_rows(direction, layers, extra))
    return offsets


OUT_NAMES = ("z0", "w", "b", "aw", "p0", "sol", "steps")
ROUNDS = (("rhs", 2, True), ("sol", 1, False), ("sch0", 1, False), ("sti0", 2, False), ("sch1", 1, False), ("sti1", 1, False))


def body(sizes, *refs):
    n_grp, n_low, n_high = sizes
    n_dev = n_low * n_high
    (rhs_h, coef_h, sol_h, dif_h, flags_h, crow_h) = refs[:6]
    refs = refs[6:]
    tab_h = refs[: len(TABLE_NAMES)]
    refs = refs[len(TABLE_NAMES) :]
    outs = dict(zip(OUT_NAMES, refs))
    refs = refs[len(OUT_NAMES) :]
    names = ("rhs", "kc", "kd", "sol", "solraw", "pin", "y1", "u", "v", "x2")
    names += ("s", "z0", "b", "p0", "w", "a1", "ct")
    buf = dict(zip(names, refs))
    refs = refs[len(names) :]
    send_bufs = dict(zip([r[0] for r in ROUNDS], refs[:6]))
    recv_bufs = dict(zip([r[0] for r in ROUNDS], refs[6:12]))
    g_send, g_recv, halo_send_sem, halo_recv_sem, g_send_sem, g_recv_sem = refs[12:18]
    load_sem, store_sem, flags_ref, crow_ref, steps_ref = refs[18:23]
    wide_recv, wide_send_sem, wide_recv_sem = refs[23:26]
    tab = dict(zip(TABLE_NAMES, refs[26:]))

    grp = lax.axis_index("grp")
    dev = lax.axis_index("dev")
    low = dev & (n_low - 1)
    high = lax.shift_right_logical(dev, n_low.bit_length() - 1)
    x_lo = jnp.where(grp > 0, 1.0, 0.0).astype(F32)
    x_hi = jnp.where(grp < n_grp - 1, 1.0, 0.0).astype(F32)
    y_lo = jnp.where(dev > 0, 1.0, 0.0).astype(F32)
    y_hi = jnp.where(dev < n_dev - 1, 1.0, 0.0).astype(F32)

    def neighbour(direction):
        return ((grp + direction[0]) & (n_grp - 1), (dev + direction[1]) & (n_dev - 1))

    def stage_partner(stage, step):
        if stage == 0:
            return (grp, high * n_low + ((low + step) & (n_low - 1)))
        if stage == 1:
            return (grp, ((high + step) & (n_high - 1)) * n_low + low)
        return ((grp + step) & (n_grp - 1), dev)

    stage_sizes = (n_low, n_high, n_grp)

    def steps_of(stage):
        size = stage_sizes[stage]
        return sorted(range(1, size), key=lambda step: -min(step, size - step))

    loads = {}
    wanted = [("rhs", rhs_h, buf["rhs"]), ("crow", crow_h, crow_ref)]
    wanted += [("sol", sol_h, buf["sol"]), ("kd", dif_h, buf["kd"]), ("flags", flags_h, flags_ref)]
    wanted += [(name, source, tab[name]) for name, source in zip(TABLE_NAMES, tab_h)]
    wanted += [("kc", coef_h, buf["kc"])]
    for at, (name, source, target) in enumerate(wanted):
        loads[name] = pltpu.make_async_copy(source, target, load_sem.at[at])
    for name in ("rhs", "crow"):
        loads[name].start()
    barrier = pltpu.get_barrier_semaphore()
    far = [(-min(step, stage_sizes[stage] - step), stage, step) for stage in (2, 1) for step in steps_of(stage)]
    partners = [stage_partner(stage, step) for _, stage, step in sorted(far)]
    partners += [neighbour(direction) for direction in DIRS]
    partners += [stage_partner(0, step) for step in steps_of(0)]
    for partner in partners:
        pl.semaphore_signal(barrier, inc=1, device_id=partner, device_id_type=MESH_ID)
    for name, _, _ in wanted[2:]:
        loads[name].start()

    row32 = lax.broadcasted_iota(jnp.int32, (32, 128), 0)
    lane32 = lax.broadcasted_iota(jnp.int32, (32, 128), 1)
    keep_z = jnp.where((lane32 > 0) & (lane32 < 127), 1.0, 0.0).astype(F32)
    share_z = jnp.where(((lane32 % 8 == 0) | (lane32 % 8 == 7)) & (lane32 > 0) & (lane32 < 127), 0.5, 1.0).astype(F32)
    lane_up = jnp.where((lane32 % 8 == 7) & (lane32 < 127), 1.0, 0.0).astype(F32)
    lane_down = jnp.where((lane32 % 8 == 0) & (lane32 > 0), 1.0, 0.0).astype(F32)
    row_up = jnp.where((row32 % 8 == 7) & (row32 < 31), 1.0, 0.0).astype(F32)
    row_down = jnp.where((row32 % 8 == 0) & (row32 > 0), 1.0, 0.0).astype(F32)
    edge_y = jnp.where(row32 == 0, y_lo, jnp.where(row32 == 31, y_hi, 1.0)).astype(F32)
    inner_y = jnp.where((row32 % 8 == 0) | (row32 % 8 == 7), 0.5, 1.0).astype(F32)
    face_y = jnp.where((row32 == 0) | (row32 == 31), 0.5, 1.0).astype(F32) * edge_y
    share_y = inner_y * edge_y
    tile_row = lax.broadcasted_iota(jnp.int32, (8, 128), 0)
    tile_lane = lax.broadcasted_iota(jnp.int32, (8, 128), 1)
    tile_index = tile_row * 128 + tile_lane

    def share_x(plane):
        if plane == 0:
            return 0.5 * x_lo
        if plane == 15:
            return 0.5 * x_hi
        return 0.5 if plane in (7, 8) else 1.0

    def x_times(values, factor):
        return values if isinstance(factor, float) and factor == 1.0 else values * factor

    def z_assembled(values):
        return (
            values
            + lane_up * pltpu.roll(values, 127, 1)
            + lane_down * pltpu.roll(values, 1, 1)
        )

    def y_assembled(values):
        return (
            values + row_up * pltpu.roll(values, 31, 0) + row_down * pltpu.roll(values, 1, 0)
        )

    halo_copies = {}

    def exchange(name, src, tile=None):
        at_round = [r[0] for r in ROUNDS].index(name)
        layers, extra = ROUNDS[at_round][1:]
        offsets = message_offsets(layers, extra)
        send, recv = send_bufs[name], recv_bufs[name]
        copies = []
        for at, direction in enumerate(DIRS):
            sx, sy = direction
            base = offsets[at]
            rows = message_rows(direction, layers, False)
            if sx and sy:
                for layer in range(layers):
                    plane = layer if sx < 0 else 16 - layers + layer
                    start = 32 * plane + (0 if sy < 0 else 24)
                    send[base + 8 * layer : base + 8 * layer + 8, :] = src[start : start + 8, :]
            elif sx:
                start = 0 if sx < 0 else 32 * (16 - layers)
                send[base : base + rows, :] = src[start : start + rows, :]
            else:
                for layer in range(layers):
                    row = layer if sy < 0 else 32 - layers + layer
                    send[base + 16 * layer : base + 16 * layer + 16, :] = src[
                        pl.ds(row, 16, stride=32), :
                    ]
            if extra:
                send[base + rows : base + rows + 8, :] = tile
            total = message_rows(direction, layers, extra)
            copy = pltpu.make_async_remote_copy(
                src_ref=send.at[pl.ds(base, total)],
                dst_ref=recv.at[pl.ds(base, total)],
                send_sem=halo_send_sem.at[8 * at_round + at],
                recv_sem=halo_recv_sem.at[8 * at_round + at],
                device_id=neighbour(direction),
                device_id_type=MESH_ID,
            )
            copy.start()
            copies.append(copy)
        halo_copies[name] = copies

    def arrived(name):
        for copy in halo_copies[name]:
            copy.wait_recv()

    def part(name, direction, layer=0):
        at_round = [r[0] for r in ROUNDS].index(name)
        layers, extra = ROUNDS[at_round][1:]
        offsets = message_offsets(layers, extra)
        at = DIRS.index((-direction[0], -direction[1]))
        unit = 8 if direction[0] and direction[1] else 32 if direction[0] else 16
        start = offsets[at] + unit * layer
        return recv_bufs[name][start : start + unit, :]

    def part_row(name, direction, layer, last):
        at_round = [r[0] for r in ROUNDS].index(name)
        layers, extra = ROUNDS[at_round][1:]
        at = DIRS.index((-direction[0], -direction[1]))
        start = message_offsets(layers, extra)[at] + 8 * layer + last
        return recv_bufs[name][start : start + 1, :]

    def add_faces(name, ref, masked):
        def scale(values, first, second):
            if not masked:
                return values
            return values * (first * second if first is not None and second is not None else second if first is None else first)

        ref[0:32, :] += scale(part(name, (-1, 0)), x_lo, None)
        ref[480:512, :] += scale(part(name, (1, 0)), x_hi, None)
        ref[pl.ds(0, 16, stride=32), :] += scale(part(name, (0, -1)), y_lo, None)
        ref[pl.ds(31, 16, stride=32), :] += scale(part(name, (0, 1)), y_hi, None)
        ref[0:1, :] += scale(part_row(name, (-1, -1), 0, 7), x_lo, y_lo)
        ref[31:32, :] += scale(part_row(name, (-1, 1), 0, 0), x_lo, y_hi)
        ref[480:481, :] += scale(part_row(name, (1, -1), 0, 7), x_hi, y_lo)
        ref[511:512, :] += scale(part_row(name, (1, 1), 0, 0), x_hi, y_hi)

    def add_arrived(name, ref):
        arrived(name)
        add_faces(name, ref, False)

    g_copies = []
    g_pending = {}
    reach = n_low + 2

    def g_send_rows(which, stage, values):
        slot = 3 * which + stage
        rows = values.shape[0]
        g_send[8 * slot : 8 * slot + rows, :] = values
        copies = {}
        for step in steps_of(stage):
            at = 7 * slot + step - 1
            copy = pltpu.make_async_remote_copy(
                src_ref=g_send.at[pl.ds(8 * slot, rows)],
                dst_ref=g_recv.at[pl.ds(8 * at, rows)],
                send_sem=g_send_sem.at[at],
                recv_sem=g_recv_sem.at[at],
                device_id=stage_partner(stage, step),
                device_id_type=MESH_ID,
            )
            copy.start()
            copies[step] = copy
        g_copies.extend(copies.values())
        g_pending[slot] = (values, copies)

    def g_rows(which, stage):
        slot = 3 * which + stage
        values, copies = g_pending[slot]
        out = {0: values}
        for step in reversed(steps_of(stage)):
            copies[step].wait_recv()
        for step in steps_of(stage):
            at = 7 * slot + step - 1
            out[step] = g_recv[8 * at : 8 * at + values.shape[0], :]
        return out

    def total_of(rows):
        total = None
        for values in rows.values():
            total = values if total is None else total + values
        return total

    def scalar_spot(start, at):
        return tile_lane == start + at

    def g_start(which, sums, scalars):
        tile = jnp.zeros((8, 128), F32)
        for (dx, dy), value in sums.items():
            tile = jnp.where(tile_lane == reach * (dx + 1) + low + dy + 1, value, tile)
        for at, value in enumerate(scalars):
            tile = jnp.where(scalar_spot(32, at), value, tile)
        g_send_rows(which, 0, tile[0:1])

    lane2 = lax.broadcasted_iota(jnp.int32, (1, 128), 1)

    def g_second(which):
        row = total_of(g_rows(which, 0))

        def moved(part, base):
            inside = (lane2 >= reach * part) & (lane2 < reach * (part + 1))
            shift = (high * n_low + (base - 1 - reach * part) + 256) & 127
            return pltpu.roll(jnp.where(inside, row, 0.0), shift, 1)

        scalars = pltpu.roll(jnp.where(lane2 >= 32, row, 0.0), 32, 1)
        scalars = jnp.where((lane2 >= 64) & (lane2 < 72), scalars, 0.0)
        one = moved(0, 0) + moved(1, 64)
        two = moved(2, 0) + scalars
        g_send_rows(which, 1, jnp.concatenate([one, two], axis=0))

    def g_third(which):
        g_send_rows(which, 2, total_of(g_rows(which, 1)))

    def g_finish(which):
        rows = g_rows(which, 2)
        sides = jnp.zeros((8, 128), F32)
        middle = jnp.zeros((8, 128), F32)
        scalars = None
        for step, values in rows.items():
            source = (grp - step) & (n_grp - 1)
            one = jnp.broadcast_to(values[0:1], (8, 128))
            two = jnp.broadcast_to(values[1:2], (8, 128))
            sides = sides + jnp.where(tile_row == ((source - 1) & (n_grp - 1)), one, 0.0)
            sides = sides + jnp.where(tile_row == ((source + 1) & (n_grp - 1)), two, 0.0)
            middle = middle + jnp.where(tile_row == source, one, 0.0)
            scalars = two if scalars is None else scalars + two
        return (sides + pltpu.roll(middle, 64, 1), scalars)

    wide_steps = [(j, k) for j in range(n_grp) for k in range(n_high) if j or k]
    wide_steps.sort(key=lambda t: -min(t[0], n_grp - t[0]) - min(t[1], n_high - t[1]))

    def wide_start(which):
        row = total_of(g_rows(which, 0))
        slot = 3 * which + 1
        place = 64 * (which - 1) + high * 8 + grp
        g_send[8 * slot : 8 * slot + 1, :] = row
        wide_recv[pl.ds(place, 1), :] = row
        for j, k in wide_steps:
            pltpu.make_async_remote_copy(
                src_ref=g_send.at[pl.ds(8 * slot, 1)],
                dst_ref=wide_recv.at[pl.ds(place, 1)],
                send_sem=wide_send_sem.at[which - 1],
                recv_sem=wide_recv_sem.at[which - 1],
                device_id=(
                    (grp + j) & (n_grp - 1),
                    ((high + k) & (n_high - 1)) * n_low + low,
                ),
                device_id_type=MESH_ID,
            ).start()

    def wide_wait(which, sem):
        rows = wide_recv.at[pl.ds(64 * (which - 1), len(wide_steps))]
        pltpu.make_async_copy(rows, rows, sem.at[which - 1]).wait()

    def wide_tiles(which):
        wide_wait(which, wide_recv_sem)
        tiles = []
        for at in range(n_high):
            start = 64 * (which - 1) + 8 * at
            tiles.append(jnp.where(tile_row < n_grp, wide_recv[start : start + 8, :], 0.0))
        return tiles

    def row_sum(tiles):
        return jnp.broadcast_to(jnp.sum(weighted([1.0] * len(tiles), tiles), axis=0, keepdims=True), (8, 128))

    def wide_finish(which):
        tiles = wide_tiles(which)
        parts = []
        for part in range(3):
            total = jnp.zeros((8, 128), F32)
            for at, tile in enumerate(tiles):
                first = n_low * at - 1
                moved = pltpu.roll(tile, (first - reach * part + 256) % 128, 1)
                inside = (tile_lane >= first) & (tile_lane < first + reach)
                total = total + jnp.where(inside, moved, 0.0)
            parts.append(total)
        return (pltpu.roll(parts[0], 7, 0) + parts[1] + pltpu.roll(parts[2], 1, 0), row_sum(tiles))

    def read_scalar(tile, at):
        lanes = jnp.sum(jnp.where(tile_lane == at, tile, 0.0), axis=1, keepdims=True)
        return jnp.broadcast_to(lanes, (8, 128))

    def coarse_sums(ref):
        middle = None
        for plane in range(16):
            piece = x_times(ref[32 * plane : 32 * plane + 32, :], share_x(plane))
            middle = piece if middle is None else middle + piece
        rows = {
            -1: ref[0:32, :] * (0.5 * x_lo),
            0: middle,
            1: ref[480:512, :] * (0.5 * x_hi),
        }
        sums = {}
        for dx in (-1, 0, 1):
            field = rows[dx] * keep_z
            sums[dx, 0] = all_sum(fold_rows(field * share_y))
            sums[dx, -1] = all_sum(field[0:8] * jnp.where(tile_row == 0, 0.5 * y_lo, 0.0))
            sums[dx, 1] = all_sum(field[24:32] * jnp.where(tile_row == 7, 0.5 * y_hi, 0.0))
        return sums

    def mass_kind(one, two):
        if one == "c":
            return two
        return one if two in ("c", one) else None

    def steep_kind(one, two):
        return "d" + one if one == two != "c" else None

    def coarse_energies():
        coef = buf["kc"]
        steep_z, steep_first, steep_last = [tab["steep"][8 * i : 8 * i + 8, :] for i in range(3)]
        planes = [coef[32 * plane : 32 * plane + 32, :] for plane in range(16)]
        along_x = {
            "c": weighted([1.0] * 16, planes),
            "0": planes[0],
            "1": planes[15],
            "d0": weighted(deriv[:, 0] ** 2, planes[:8]),
            "d1": weighted(deriv[:, 7] ** 2, planes[8:]),
        }
        z_mass = keep_z[0:8]

        def reduced(x_kind, y_kind, z_part):
            values = along_x[x_kind]
            if y_kind == "c":
                values = fold_rows(values)
            elif y_kind == "0":
                values = jnp.where(tile_row == 0, values[0:8], 0.0)
            elif y_kind == "1":
                values = jnp.where(tile_row == 7, values[24:32], 0.0)
            elif y_kind == "d0":
                values = values[0:8] * steep_first
            else:
                values = values[24:32] * steep_last
            return all_sum(values * z_part)

        kinds = ("c", "0", "1")
        pieces = {}
        for one in kinds:
            for two in kinds:
                pieces[one, two] = reduced(one, two, steep_z)
        for steep in ("d0", "d1"):
            for kind in kinds:
                pieces[steep, kind] = reduced(steep, kind, z_mass)
                pieces[kind, steep] = reduced(kind, steep, z_mass)
        energies = {}
        for a in kinds:
            for b in kinds:
                for c in kinds:
                    for d in kinds:
                        keys = (
                            (mass_kind(a, c), mass_kind(b, d)),
                            (steep_kind(a, c), mass_kind(b, d)),
                            (mass_kind(a, c), steep_kind(b, d)),
                        )
                        found = [pieces[key] for key in keys if key in pieces]
                        if found:
                            energies[a, b, c, d] = weighted([1.0] * len(found), found)
        return energies

    def coarse_image(energies, values):
        kinds = ("c", "0", "1")
        half_x = (0.5 * x_lo, 0.5 * x_hi)
        half_y = (0.5 * y_lo, 0.5 * y_hi)

        def split(before, own, after, half):
            return {
                "c": own,
                "0": before * half[0] + own * (half[0] - 1.0),
                "1": after * half[1] + own * (half[1] - 1.0),
            }

        def joined(parts, half):
            own = parts["c"] + parts["0"] * (half[0] - 1.0) + parts["1"] * (half[1] - 1.0)
            return (parts["0"] * half[0], own, parts["1"] * half[1])

        by_x = {dy: split(*[values[dx, dy] for dx in (-1, 0, 1)], half_x) for dy in (-1, 0, 1)}
        steps = {a: split(*[by_x[dy][a] for dy in (-1, 0, 1)], half_y) for a in kinds}
        image = {}
        for a in kinds:
            parts = {}
            for b in kinds:
                terms = [
                    energies[a, b, c, d] * steps[c][d]
                    for c in kinds
                    for d in kinds
                    if (a, b, c, d) in energies
                ]
                parts[b] = weighted([1.0] * len(terms), terms)
            image[a] = joined(parts, half_y)
        out = {}
        for at, dy in enumerate((-1, 0, 1)):
            for dx, value in zip((-1, 0, 1), joined({a: image[a][at] for a in kinds}, half_x)):
                out[dx, dy] = value
        return out

    def paired(values, sums):
        total = None
        for key in values:
            piece = values[key] * sums[key]
            total = piece if total is None else total + piece
        return total

    q_scale = 1.0 / math.sqrt(LOCAL_X * LOCAL_Y * LOCAL_Z)

    def coarse_values(tile):
        values = {}
        for dx in (-1, 0, 1):
            for dy in (-1, 0, 1):
                if dx == 0 and dy == 0:
                    row = buf["ct"][...]
                else:
                    layers, extra = ROUNDS[0][1:]
                    at = DIRS.index((-dx, -dy))
                    start = message_offsets(layers, extra)[at] + message_rows((dx, dy), layers, False)
                    row = recv_bufs["rhs"][start : start + 8, :]
                values[dx, dy] = all_sum(row * tile) * q_scale
        return values

    def coarse_patterns(values):
        lines = {}
        for dx in (-1, 0, 1):
            centre = jnp.concatenate([values[dx, 0]] * 4, axis=0)
            first = jnp.concatenate([values[dx, -1]] * 4, axis=0)
            last = jnp.concatenate([values[dx, 1]] * 4, axis=0)
            line = jnp.where(row32 == 0, (centre + first) * (0.5 * y_lo), centre)
            line = jnp.where(row32 == 31, (centre + last) * (0.5 * y_hi), line)
            lines[dx] = line * keep_z
        return (
            (lines[0] + lines[-1]) * (0.5 * x_lo),
            lines[0],
            (lines[0] + lines[1]) * (0.5 * x_hi),
        )

    def build_pin(name, src):
        pin = buf["pin"]
        zero8 = jnp.zeros((8, 128), F32)
        for plane in range(18):
            pin[40 * plane + 32 : 40 * plane + 40, :] = zero8
        for plane in range(16):
            pin[40 * (plane + 1) : 40 * (plane + 1) + 32, :] = src[32 * plane : 32 * plane + 32, :]
        pin[40:72, :] += part(name, (-1, 0), 1)
        pin[640:672, :] += part(name, (1, 0), 0)
        pin[pl.ds(40, 16, stride=40), :] += part(name, (0, -1), 1)
        pin[pl.ds(71, 16, stride=40), :] += part(name, (0, 1), 0)
        pin[pl.ds(72, 16, stride=40), :] = part(name, (0, -1), 0)
        pin[pl.ds(73, 16, stride=40), :] = part(name, (0, 1), 1)
        for at_plane, dx, layer in ((1, -1, 1), (16, 1, 0), (0, -1, 0), (17, 1, 1)):
            base = 40 * at_plane
            if at_plane in (0, 17):
                pin[base : base + 32, :] = part(name, (dx, 0), layer)
            pin[base : base + 1, :] += part_row(name, (dx, -1), layer, 7)
            pin[base + 31 : base + 32, :] += part_row(name, (dx, 1), layer, 0)
            pin[base + 32 : base + 33, :] += part_row(name, (dx, -1), layer, 6)
            pin[base + 33 : base + 34, :] += part_row(name, (dx, 1), layer, 1)

    row40 = lax.broadcasted_iota(jnp.int32, (40, 128), 0)
    edge40 = jnp.where(
        (row40 == 0) | (row40 == 32), y_lo, jnp.where((row40 == 31) | (row40 == 33), y_hi, 1.0)
    ).astype(F32)

    def pin_plane(plane):
        values = buf["pin"][40 * plane : 40 * plane + 40, :] * edge40
        if plane < 2:
            values = values * x_lo
        if plane > 15:
            values = values * x_hi
        return values

    def assembled_own(plane):
        return z_assembled(pin_plane(plane + 1)[0:32]) * keep_z

    basis, _ = fdm_tables()
    signs = parity_signs(basis)
    deriv = derivative_table()
    sources = ([0, 1, 2, 3, 4, 5, 6, 7, 8, 10], [7, 9, 10, 11, 12, 13, 14, 15, 16, 17])

    def schwarz(dst):
        y1, u, v, x2 = buf["y1"], buf["u"], buf["v"], buf["x2"]
        yf, yb = tab["yf"][...], tab["yb"][...]
        for pair in range(9):
            out = left_mul(yf, pin_plane(2 * pair), pin_plane(2 * pair + 1))
            y1[80 * pair : 80 * pair + 40, :] = out[0:40, :128]
            y1[80 * pair + 40 : 80 * pair + 80, :] = out[0:40, 128:]
        for element in range(2):
            for tile in range(5):
                values = [y1[40 * p + 8 * tile : 40 * p + 8 * tile + 8, :] for p in sources[element]]
                for mode, piece in enumerate(x_modes(values, basis, signs)):
                    start = 40 * (10 * element + mode) + 8 * tile
                    u[start : start + 8, :] = piece
        for element in range(2):
            block = u[400 * element : 400 * element + 400, :]
            first, second = halves(block)
            modes = dot(jnp.concatenate([first, second], axis=1), tab["zf1"][...])
            modes = (modes + dot(first, tab["zf2"][...])) * tab["recip"][...]
            first, second = halves(modes)
            back = dot(first, tab["zb1"][...])
            v[400 * element : 400 * element + 400, :] = (
                back[:, :128] + back[:, 128:] + dot(second, tab["zb1"][:, 0:128])
            )
        for tile in range(5):
            outs = []
            for element in range(2):
                starts = [40 * (10 * element + mode) + 8 * tile for mode in range(10)]
                outs += x_unmodes([v[s : s + 8, :] for s in starts], basis, signs)
            shared = (outs[7] + outs[8]) * 0.5
            outs[7] = shared
            outs[8] = shared
            outs[0] = outs[0] * (0.5 * x_lo)
            outs[15] = outs[15] * (0.5 * x_hi)
            for plane in range(16):
                x2[40 * plane + 8 * tile : 40 * plane + 8 * tile + 8, :] = outs[plane]
        for pair in range(8):
            out = left_mul(yb, x2[80 * pair : 80 * pair + 40, :], x2[80 * pair + 40 : 80 * pair + 80, :])
            dst[64 * pair : 64 * pair + 32, :] = out[:, :128] * face_y
            dst[64 * pair + 32 : 64 * pair + 64, :] = out[:, 128:] * face_y

    def stiff(src, coef, dst, extra=None):
        energy = jnp.zeros((8, 128), F32)
        for chunk in range(2):
            at = slice(256 * chunk, 256 * chunk + 256)
            grad = right_mul(src[at, :], tab["zd"][...])
            flow = grad * coef[at, :]
            energy = energy + fold_rows(grad * flow)
            dst[at, :] = right_mul(flow, tab["zdt"][...])
        for pair in range(8):
            one = slice(64 * pair, 64 * pair + 32)
            two = slice(64 * pair + 32, 64 * pair + 64)
            grad = left_mul(tab["yd"][...], src[one, :], src[two, :])
            flow_one = grad[:, :128] * coef[one, :]
            flow_two = grad[:, 128:] * coef[two, :]
            energy = energy + fold_rows(grad[:, :128] * flow_one) + fold_rows(grad[:, 128:] * flow_two)
            back = left_mul(tab["ydt"][...], flow_one, flow_two)
            dst[one, :] += back[:, :128]
            dst[two, :] += back[:, 128:]
        for tile in range(4):
            sums = []
            for element in range(2):
                starts = [32 * (8 * element + i) + 8 * tile for i in range(8)]
                grads = x_derive([src[s : s + 8, :] for s in starts], deriv)
                flows = [grad * coef[s : s + 8, :] for grad, s in zip(grads, starts)]
                for grad, flow in zip(grads, flows):
                    energy = energy + grad * flow
                backs = x_derive(flows, deriv.T)
                for s, back in zip(starts, backs):
                    value = dst[s : s + 8, :] + back
                    if extra is not None:
                        value = value + extra[s : s + 8, :]
                    sums.append(value)
            shared = sums[7] + sums[8]
            sums[7] = shared
            sums[8] = shared
            for plane in range(16):
                dst[32 * plane + 8 * tile : 32 * plane + 8 * tile + 8, :] = sums[plane]
        for plane in range(16):
            at = slice(32 * plane, 32 * plane + 32)
            dst[at, :] = y_assembled(dst[at, :])
        return energy

    weights = GLL_WEIGHTS + GLL_WEIGHTS

    loads["rhs"].wait()
    loads["crow"].wait()
    for plane in range(16):
        at = slice(32 * plane, 32 * plane + 32)
        values = buf["rhs"][at, :]
        if plane == 7:
            values = values + buf["rhs"][256:288, :]
        if plane == 8:
            values = values + buf["rhs"][224:256, :]
        buf["s"][at, :] = y_assembled(values)
    ct = buf["ct"]
    ct[...] = jnp.zeros((8, 128), F32)
    count = n_grp * n_dev
    for at in range(n_grp):
        start = n_dev * at
        if count >= 128:
            row = crow_ref[:, start // 128 * 128 : start // 128 * 128 + 128]
        else:
            row = jnp.concatenate([crow_ref[...], jnp.zeros((1, 128 - count), F32)], axis=1)
        if start % 128:
            row = pltpu.roll(row, 128 - start % 128, 1)
        ct[at : at + 1, :] = jnp.where(lane2 < n_dev, row, 0.0)
    right_sums = coarse_sums(buf["s"])

    pl.semaphore_wait(barrier, len(partners))
    g_start(0, right_sums, [])
    exchange("rhs", buf["s"], ct[...])

    for name in ("sol", "kd", "flags", "wyz", "spread", "zd", "zdt", "yd", "ydt"):
        loads[name].wait()
    wyz = tab["wyz"][...]
    flags = jnp.concatenate([flags_ref[0], flags_ref[1]], axis=0).astype(F32).astype(BF16)
    flag_rows = dot(flags, tab["spread"][...])
    weight_column = GLL_WEIGHTS
    row8 = tile_row
    w_rows = jnp.zeros((8, 128), F32)
    for at, weight in enumerate(weight_column):
        w_rows = jnp.where(row8 == at, weight, w_rows)
    for plane in range(16):
        at = slice(32 * plane, 32 * plane + 32)
        buf["kd"][at, :] = buf["kd"][at, :] * (wyz * weights[plane])
        flux = jnp.concatenate(
            [
                flag_rows[4 * (plane // 8) + ey : 4 * (plane // 8) + ey + 1, :] * w_rows
                for ey in range(4)
            ],
            axis=0,
        )
        factor = wyz * (MASS_RATE * weights[plane]) + flux * (GROWTH * SEGREGATION * weights[plane])
        buf["x2"][at, :] = buf["sol"][at, :] * factor
    stiff(buf["sol"], buf["kd"], buf["solraw"], extra=buf["x2"])

    exchange("sol", buf["solraw"])
    for name in ("kc", "steep", "yf", "yb", "zf1", "zf2", "zb1", "recip"):
        loads[name].wait()
    for plane in range(16):
        at = slice(32 * plane, 32 * plane + 32)
        buf["kc"][at, :] = buf["kc"][at, :] * (wyz * weights[plane])
    energies = coarse_energies()

    stores = []

    def store(name, ref):
        copy = pltpu.make_async_copy(ref, outs[name], store_sem.at[OUT_NAMES.index(name)])
        copy.start()
        stores.append(copy)

    g_second(0)
    arrived("rhs")
    build_pin("rhs", buf["s"])
    schwarz(buf["z0"])
    exchange("sch0", buf["z0"])
    g_third(0)
    for plane in range(16):
        buf["b"][32 * plane : 32 * plane + 32, :] = assembled_own(plane)
    share_yz = share_y * share_z

    def product_of(first, second):
        tile = jnp.zeros((8, 128), F32)
        for plane in range(16):
            at = slice(32 * plane, 32 * plane + 32)
            piece = x_times(first[at, :] * second[at, :] * share_yz, share_x(plane))
            tile = tile + fold_rows(piece)
        return all_sum(tile)

    def add_coarse(ref, values):
        patterns = coarse_patterns(values)
        for plane in range(16):
            at = slice(32 * plane, 32 * plane + 32)
            ref[at, :] += patterns[0 if plane == 0 else 2 if plane == 15 else 1]

    add_arrived("sch0", buf["z0"])
    curve = all_sum(stiff(buf["z0"], buf["kc"], buf["a1"]))
    sums = coarse_sums(buf["a1"])
    rz = product_of(buf["b"], buf["z0"])
    total, _ = g_finish(0)
    coarse = coarse_values(total)
    image = coarse_image(energies, coarse)
    applied_sums = {key: sums[key] + image[key] for key in sums}
    rz = rz + paired(coarse, right_sums)
    curve = curve + paired(coarse, {key: sums[key] + applied_sums[key] for key in sums})
    g_start(1, applied_sums, [rz, curve])
    add_coarse(buf["z0"], coarse)
    stiff(buf["z0"], buf["kc"], buf["a1"])
    exchange("sti0", buf["a1"])

    arrived("sol")
    add_faces("sol", buf["solraw"], True)
    for plane in range(16):
        at = slice(32 * plane, 32 * plane + 32)
        buf["solraw"][at, :] = z_assembled(buf["solraw"][at, :])
    store("sol", buf["solraw"])

    wide_start(1)
    arrived("sti0")
    build_pin("sti0", buf["a1"])
    schwarz(buf["w"])
    exchange("sch1", buf["w"])
    for plane in range(16):
        buf["p0"][32 * plane : 32 * plane + 32, :] = assembled_own(plane)
    add_arrived("sch1", buf["w"])
    w_curve = all_sum(stiff(buf["w"], buf["kc"], buf["rhs"]))
    sums = coarse_sums(buf["rhs"])
    b_w = product_of(buf["b"], buf["w"])
    p_w = product_of(buf["p0"], buf["w"])
    total, scalars = wide_finish(1)
    coarse = coarse_values(total)
    image = coarse_image(energies, coarse)
    b_w = b_w + paired(coarse, right_sums)
    p_w = p_w + paired(coarse, applied_sums)
    w_curve = w_curve + paired(coarse, {key: 2.0 * sums[key] + image[key] for key in sums})
    tile = jnp.zeros((8, 128), F32)
    for at, value in enumerate((b_w, p_w, w_curve)):
        tile = jnp.where(tile_lane == at, value, tile)
    g_send_rows(2, 0, tile[0:1])
    rz0 = read_scalar(scalars, 32)
    curve0 = read_scalar(scalars, 33)
    alpha0 = rz0 / curve0
    add_coarse(buf["w"], coarse)
    stiff(buf["w"], buf["kc"], buf["rhs"])
    exchange("sti1", buf["rhs"])
    for name in ("z0", "w", "b", "p0"):
        store(name, buf[name])
    wide_start(2)
    add_arrived("sti1", buf["rhs"])
    for plane in range(16):
        at = slice(32 * plane, 32 * plane + 32)
        values = z_assembled(buf["rhs"][at, :]) * keep_z * edge_y
        if plane == 0:
            values = values * x_lo
        if plane == 15:
            values = values * x_hi
        buf["rhs"][at, :] = values
    store("aw", buf["rhs"])
    for name in halo_copies:
        for copy in halo_copies[name]:
            copy.wait_send()
    for copy in g_copies:
        copy.wait_send()
    for copy in stores:
        copy.wait()
    inverse = 1.0 / rz0
    for which in (1, 2):
        wide_wait(which, wide_send_sem)
    total = row_sum(wide_tiles(2))
    b_w, p_w, w_curve = [read_scalar(total, at) for at in range(3)]
    rz1 = alpha0 * (alpha0 * p_w - b_w)
    cross1 = curve0 - alpha0 * p_w
    curve1 = cross1 - alpha0 * (p_w - alpha0 * w_curve)
    beta = rz1 * inverse
    alpha1 = rz1 / (curve1 + beta * (2.0 * cross1 + beta * curve0))
    steps_ref[0:8, :] = alpha0 + alpha1 * (1.0 + beta)
    steps_ref[8:16, :] = alpha0 * alpha1
    store("steps", steps_ref)
    stores[-1].wait()


def finish_body(*refs):
    count = len(OUT_NAMES)
    sources, targets, bufs, load_sem, store_sem = refs[:count], refs[count : count + 3], refs[count + 3 : 2 * count + 3], refs[-2], refs[-1]
    loads = {}
    for at in (6, 0, 1, 2, 3, 4, 5):
        loads[OUT_NAMES[at]] = pltpu.make_async_copy(sources[at], bufs[at], load_sem.at[at])
        loads[OUT_NAMES[at]].start()
    z0, w, b, aw, p0, sol, steps = bufs
    for name in ("steps", "z0", "w"):
        loads[name].wait()
    first, second = steps[0:8, :], steps[8:16, :]
    for plane in range(LOCAL_X):
        at = slice(32 * plane, 32 * plane + 32)
        z0[at, :] = times_tile(z0[at, :], first) - times_tile(w[at, :], second)
    stores = [pltpu.make_async_copy(z0, targets[0], store_sem.at[0])]
    stores[0].start()
    for name in ("b", "aw", "p0"):
        loads[name].wait()
    for plane in range(LOCAL_X):
        at = slice(32 * plane, 32 * plane + 32)
        b[at, :] = b[at, :] - times_tile(p0[at, :], first) + times_tile(aw[at, :], second)
    stores.append(pltpu.make_async_copy(b, targets[1], store_sem.at[1]))
    stores[1].start()
    loads["sol"].wait()
    stores.append(pltpu.make_async_copy(sol, targets[2], store_sem.at[2]))
    stores[2].start()
    for copy in stores:
        copy.wait()


def finish(fields):
    far = pl.BlockSpec(memory_space=pltpu.HBM)
    return pl.pallas_call(
        finish_body,
        out_shape=[jax.ShapeDtypeStruct((ROWS, LOCAL_Z), F32)] * 3,
        in_specs=[far] * len(OUT_NAMES),
        out_specs=[far] * 3,
        scratch_shapes=[pltpu.VMEM(v.shape, F32) for v in fields]
        + [pltpu.SemaphoreType.DMA((len(OUT_NAMES),)), pltpu.SemaphoreType.DMA((3,))],
        compiler_params=pltpu.CompilerParams(vmem_limit_bytes=63 * 1024 * 1024),
    )(*fields)


def run_kernel(sizes, fields, flags, coarse_row, tables):
    constants = [jnp.asarray(tables[name]) for name in TABLE_NAMES]
    far = pl.BlockSpec(memory_space=pltpu.HBM)
    field = pltpu.VMEM((ROWS, LOCAL_Z), F32)

    def rows(count):
        return pltpu.VMEM((count, LOCAL_Z), F32)

    halo = [rows(message_offsets(layers, extra)[-1]) for _, layers, extra in ROUNDS]
    scratch = (
        [field] * 5
        + [rows(720), rows(720), rows(800), rows(800), rows(640)]
        + [field] * 6
        + [rows(8)]
        + halo
        + halo
        + [rows(72), rows(8 * 63)]
        + [pltpu.SemaphoreType.DMA((count,)) for count in (48, 48, 63, 63, 6 + len(constants), len(OUT_NAMES))]
        + [pltpu.VMEM(flags.shape, jnp.int32), pltpu.VMEM(coarse_row.shape, F32), rows(16)]
        + [rows(128), pltpu.SemaphoreType.DMA((2,)), pltpu.SemaphoreType.DMA((2,))]
        + [pltpu.VMEM(table.shape, table.dtype) for table in constants]
    )
    return pl.pallas_call(
        functools.partial(body, sizes),
        out_shape=[
            jax.ShapeDtypeStruct((16 if name == "steps" else ROWS, LOCAL_Z), F32) for name in OUT_NAMES
        ],
        in_specs=[far] * (6 + len(constants)),
        out_specs=[far] * len(OUT_NAMES),
        scratch_shapes=scratch,
        compiler_params=pltpu.CompilerParams(
            collective_id=0, has_side_effects=True, vmem_limit_bytes=63 * 1024 * 1024
        ),
    )(*fields, flags, coarse_row, *constants)


def solution(mesh):
    n_grp, n_dev = (mesh.shape["grp"], mesh.shape["dev"])
    n_low = 8 if n_dev % 8 == 0 else 2
    sizes = (n_grp, n_low, n_dev // n_low)
    tables = make_tables()

    def shards(right_side, coefficient, solute, diffusivity, interface_flags, coarse_inverse):
        fields = [v.reshape(ROWS, LOCAL_Z) for v in (right_side, coefficient, solute, diffusivity)]
        outs = run_kernel(sizes, fields, interface_flags, coarse_inverse, tables)
        return tuple(v.reshape(LOCAL_X, LOCAL_Y, LOCAL_Z) for v in finish(outs))

    placed = (
        P("grp", "dev", None),
        P("grp", "dev", None),
        P("grp", "dev", None),
        P("grp", "dev", None),
        P("grp", "dev", None),
        P(("grp", "dev"), None),
    )
    return jax.shard_map(
        shards,
        mesh=mesh,
        in_specs=placed,
        out_specs=(P("grp", "dev", None), P("grp", "dev", None), P("grp", "dev", None)),
        check_vma=False,
    )
```
